128 devices in a mesh: dp: 16 (over x, y_lo, core), row: 4 (over z), col: 2 (over y_hi).
Axes of the slice: x: 4, y: 4 (y_hi: 2, y_lo: 2; y = y_hi * 2 + y_lo), z: 4, core: 2. Of those that a mesh axis runs over, the one named last changes fastest.
Arguments:
- activations: bfloat16 [16384, 896], P('dp', 'row'), may hold values from -6 to 6
- starts: int32 [16384], P('dp'), may hold values from 0 to 16383, as said below
- first_gain: float32 [896], P('row'), may hold values from 0.5 to 1.5
- project_weight: bfloat16 [896, 1152], P('row', 'col'), may hold values from -0.1875 to 0.1875
- project_bias: float32 [1152], P('col'), may hold values from -3 to 3
- output_weight: bfloat16 [896, 896], P('col', 'row'), may hold values from -0.75 to 0.75
- second_gain: float32 [896], P('row'), may hold values from 0.5 to 1.5
- gate_weight: bfloat16 [896, 4864], P('row', 'col'), may hold values from -0.1875 to 0.1875
- up_weight: bfloat16 [896, 4864], P('row', 'col'), may hold values from -0.1875 to 0.1875
- down_weight: bfloat16 [4864, 896], P('col', 'row'), may hold values from -0.15625 to 0.15625
- cotangent: bfloat16 [16384, 896], P('dp', 'row'), may hold values from -6 to 6
Outputs:
- block_output: bfloat16 [16384, 896], P('dp', 'row')
- input_grad: float32 [16384, 896], P('dp', 'row')
- first_gain_grad: float32 [896], P('row')
- project_weight_grad: float32 [896, 1152], P('row', 'col')
- project_bias_grad: float32 [1152], P('col')
- output_weight_grad: float32 [896, 896], P('col', 'row')
- second_gain_grad: float32 [896], P('row')
- gate_weight_grad: float32 [896, 4864], P('row', 'col')
- up_weight_grad: float32 [896, 4864], P('row', 'col')
- down_weight_grad: float32 [4864, 896], P('col', 'row')
The draws below stay inside these ranges and needn't reach their ends.
Inputs may be any that keep to these rules, and one draw needn't show every extreme that they name: starts never falls, starts[t] <= t, and starts[t] is t or starts[t - 1]; a sequence holds at most 1024 tokens, and one holds exactly 1024.
All inputs are finite; a program needn't handle non-finite values.
Results may differ from the reference program's by a relative error of at most 0.012.
Values may be sent and summed in bfloat16 or wider, within the bound.
A program may use at most 192 MiB of HBM per device.

```python
import jax
import jax.numpy as jnp
from jax import lax

D = 896
HEADS = 14
GROUPS = 2
HEAD_DIM = 64
FF = 4864
SHARD_TOK = 1024
MAXLEN = 1024
TOKENS = 16384
QKV_WIDTH = 1152


def draw_starts(key, part):
    key = jax.random.fold_in(key, 11)
    first_key, second_key = jax.random.split(key)
    lengths = jax.random.randint(first_key, (TOKENS,), 1, MAXLEN + 1)
    forced = jax.random.randint(second_key, (), 0, 4)
    lengths = jnp.where(jnp.arange(TOKENS) == forced, MAXLEN, lengths)
    ends = jnp.cumsum(lengths)
    index = jnp.arange(TOKENS)
    which = jnp.searchsorted(ends, index, side='right')
    return (ends[which] - lengths[which]).astype(jnp.int32)


def levels(rng, extent, cuts, least, largest):
    level, own = 1.0, jax.random.fold_in(rng, 6)
    for axis_at, parts in cuts:
        steps = jnp.exp(jax.random.uniform(jax.random.fold_in(own, axis_at), (parts,), jnp.float32, least / len(cuts), largest / len(cuts)))
        level = level * jnp.repeat(steps, extent[axis_at] // parts).reshape([-1 if axis == axis_at else 1 for axis in range(len(extent))])
    return level


def noise(key, extent, spread, limit, cuts=(), kind=jnp.bfloat16):
    values = jax.random.normal(key, extent, jnp.float32) * spread
    if len(cuts) > 0:
        values = levels(key, extent, cuts, -0.22, 0.18) * values
    return jnp.clip(values, min=-limit, max=limit).astype(kind)


def setup_inputs(seed: int = 0) -> dict:
    key_of = jax.random.split(jax.random.key(seed), 12)
    activations = noise(key_of[0], (TOKENS, D), 1.0, 6.0, ((0, 16), (1, 4)))
    starts = draw_starts(jax.random.fold_in(key_of[11], 71), 0)
    first_gain = jnp.clip(1.0 + 0.1 * jax.random.normal(key_of[2], (D,), jnp.float32), 0.5, 1.5)
    project_weight = noise(key_of[3], (D, QKV_WIDTH), D ** -0.5, 0.1875, ((0, 4), (1, 2)))
    project_bias = noise(key_of[4], (QKV_WIDTH,), 0.5, 3.0, ((0, 2),), jnp.float32)
    output_weight = noise(key_of[5], (HEADS * HEAD_DIM, D), (max(HEAD_DIM, HEADS * HEAD_DIM // 64)) ** -0.5, 0.75, ((0, 2), (1, 4)))
    second_gain = jnp.clip(1.0 + 0.1 * jax.random.normal(key_of[6], (D,), jnp.float32), 0.5, 1.5)
    gate_weight = noise(key_of[7], (D, FF), D ** -0.5, 0.1875, ((0, 4), (1, 2)))
    up_weight = noise(key_of[8], (D, FF), D ** -0.5, 0.1875, ((0, 4), (1, 2)))
    down_weight = noise(key_of[9], (FF, D), (FF // 4) ** -0.5, 0.15625, ((0, 2), (1, 4)))
    cotangent = noise(key_of[10], (TOKENS, D), 1.0, 6.0, ((0, 16), (1, 4)))
    return dict(activations=activations, starts=starts, first_gain=first_gain, project_weight=project_weight, project_bias=project_bias, output_weight=output_weight, second_gain=second_gain, gate_weight=gate_weight, up_weight=up_weight, down_weight=down_weight, cotangent=cotangent)


@jax.custom_vjp
def low(v):
    return lax.optimization_barrier(v.astype(jnp.bfloat16)).astype(jnp.float32)

@jax.custom_vjp
def low_back(v):
    return v

def low_keep(v):
    return (low(v), None)

def low_pass(kept, grad):
    return (grad,)

def back_keep(v):
    return (v, None)

def back_low(kept, grad):
    return (low(grad),)
low.defvjp(low_keep, low_pass)
low_back.defvjp(back_keep, back_low)
EPS = 1e-06
HIGHEST = lax.Precision.HIGHEST

def matmul(left, right):
    return jnp.dot(left, right, precision=HIGHEST)

def rms_norm(values, gain):
    rate = lax.rsqrt(lax.optimization_barrier(jnp.mean(values * values, axis=-1, keepdims=True)) + EPS)
    return values * rate * gain

def rotate(values, positions):
    half = HEAD_DIM // 2
    freqs = 1000000.0 ** (-jnp.arange(half, dtype=jnp.float32) * 2.0 / HEAD_DIM)
    angle = positions.astype(jnp.float32)[:, None] * freqs[None, :]
    cosine = jnp.cos(angle)[:, None, :]
    sine = jnp.sin(angle)[:, None, :]
    first = values[..., :half]
    second = values[..., half:]
    return jnp.concatenate([first * cosine - second * sine, second * cosine + first * sine], axis=-1)

def attention(queries, keys, values, starts):
    group_heads = HEADS // GROUPS
    blocks = TOKENS // SHARD_TOK
    window = SHARD_TOK + MAXLEN
    keys_pad = jnp.concatenate([jnp.zeros((MAXLEN, GROUPS, HEAD_DIM), keys.dtype), keys], 0)
    values_pad = jnp.concatenate([jnp.zeros((MAXLEN, GROUPS, HEAD_DIM), values.dtype), values], 0)

    def one_block(index):
        base = index * SHARD_TOK
        query_block = lax.dynamic_slice_in_dim(queries, base, SHARD_TOK, 0).reshape(SHARD_TOK, GROUPS, group_heads, HEAD_DIM)
        key_block = lax.dynamic_slice_in_dim(keys_pad, base, window, 0)
        value_block = lax.dynamic_slice_in_dim(values_pad, base, window, 0)
        start_block = lax.dynamic_slice_in_dim(starts, base, SHARD_TOK, 0)
        key_index = base - MAXLEN + jnp.arange(window, dtype=jnp.int32)
        query_index = base + jnp.arange(SHARD_TOK, dtype=jnp.int32)
        allowed = (key_index[None, :] >= start_block[:, None]) & (key_index[None, :] <= query_index[:, None])
        scores = low_back(HEAD_DIM ** (-0.5) * jnp.einsum('qgmd,kgd->gmqk', query_block, key_block, precision=HIGHEST))
        scores = jnp.where(allowed[None, None], scores, -1e+30)
        peak = lax.optimization_barrier(jnp.max(scores, axis=-1, keepdims=True))
        powered = jnp.exp(scores - peak)
        probs = low(powered / lax.optimization_barrier(jnp.sum(powered, axis=-1, keepdims=True)))
        mixed = jnp.einsum('gmqk,kgd->qgmd', probs, value_block, precision=HIGHEST)
        return mixed.reshape(SHARD_TOK, HEADS * HEAD_DIM)
    blocks_out = lax.map(jax.checkpoint(one_block), jnp.arange(blocks, dtype=jnp.int32))
    return blocks_out.reshape(TOKENS, HEADS * HEAD_DIM)

def forward(inputs, first_gain, project_weight, project_bias, output_weight, second_gain, gate_weight, up_weight, down_weight, starts):
    group_heads = HEADS // GROUPS
    normed_first = low(rms_norm(inputs, first_gain))
    projected = low_back(matmul(normed_first, project_weight) + project_bias)
    projected = projected.reshape(TOKENS, GROUPS, group_heads + 2, HEAD_DIM)
    positions = jnp.arange(TOKENS, dtype=jnp.int32) - starts
    queries = low(rotate(projected[:, :, :group_heads].reshape(TOKENS, HEADS, HEAD_DIM), positions))
    keys = low(rotate(projected[:, :, group_heads], positions))
    values = low(projected[:, :, group_heads + 1])
    attended = low_back(low(attention(queries, keys, values, starts)))
    middle = inputs + low_back(matmul(attended, output_weight))
    normed_second = low(rms_norm(middle, second_gain))
    gate_values = low_back(matmul(normed_second, gate_weight))
    up_values = low_back(matmul(normed_second, up_weight))
    hidden = low(jax.nn.silu(gate_values) * up_values)
    return middle + low_back(matmul(hidden, down_weight))

def reference(activations, starts, first_gain, project_weight, project_bias, output_weight, second_gain, gate_weight, up_weight, down_weight, cotangent):
    floats = tuple((array.astype(jnp.float32) for array in (activations, first_gain, project_weight, project_bias, output_weight, second_gain, gate_weight, up_weight, down_weight)))

    def layer(*pieces):
        return forward(*pieces, starts)
    result, pull = jax.vjp(layer, *floats)
    grads = pull(cotangent.astype(jnp.float32))
    return (result.astype(jnp.bfloat16), grads[0], grads[1], grads[2], grads[3], grads[4], grads[5], grads[6], grads[7], grads[8])
```

```python
import functools

import jax
import jax.numpy as jnp
from jax import lax
from jax.experimental import pallas as pl
from jax.experimental.pallas import tpu as pltpu
from jax.sharding import PartitionSpec as P

D = 896
HEADS = 14
GROUPS = 2
HEAD_DIM = 64
MAXLEN = 1024
EPS = 1e-06
BF = jnp.bfloat16
F32 = jnp.float32
ROWS = 4
FEAT = 224
SHARE = 256
SHARD = 1024
HALF_FF = 2432
WIN = 640
LAST = HALF_FF - WIN
PADF = 256
VMEM_LIMIT = 60 * 1024 * 1024


def from_behind(block, axis, distance):
    devices = range(lax.axis_size(axis))
    route = [(i - distance, i) for i in devices if i - distance in devices]
    return lax.ppermute(block, axis, route)


def rotate(values, cosine, sine):
    half = HEAD_DIM // 2
    if values.ndim == 3:
        cosine = cosine[:, None, :]
        sine = sine[:, None, :]
    first = values[..., :half]
    second = values[..., half:]
    return jnp.concatenate(
        [first * cosine - second * sine, second * cosine + first * sine], axis=-1
    )


def dot(a, b):
    return jnp.dot(a, b, preferred_element_type=F32)


def dot_nt(a, b):
    return lax.dot_general(a, b, (((1,), (1,)), ((), ())), preferred_element_type=F32)


def dot_tn(a, b):
    return lax.dot_general(a, b, (((0,), (0,)), ((), ())), preferred_element_type=F32)


def rcopy(src, dst, send, recv, **device):
    return pltpu.make_async_remote_copy(
        src_ref=src,
        dst_ref=dst,
        send_sem=send,
        recv_sem=recv,
        device_id=device,
        device_id_type=pl.DeviceIdType.MESH,
    )


def greet(peers):
    barrier = pltpu.get_barrier_semaphore()
    for peer in peers:
        pl.semaphore_signal(
            barrier, inc=1, device_id=peer, device_id_type=pl.DeviceIdType.MESH
        )
    pl.semaphore_wait(barrier, len(peers))


def vmem_call(kernel, inputs, outs, scratch, collective, cost=None):
    return pl.pallas_call(
        kernel,
        out_shape=outs,
        in_specs=[pl.BlockSpec(memory_space=pltpu.VMEM)] * inputs,
        out_specs=jax.tree.map(lambda _: pl.BlockSpec(memory_space=pltpu.VMEM), outs),
        scratch_shapes=scratch,
        compiler_params=pltpu.CompilerParams(
            collective_id=collective,
            has_side_effects=True,
            vmem_limit_bytes=VMEM_LIMIT,
        ),
        cost_estimate=cost,
    )


def grads_kernel(
    count,
    joined,
    g_ref,
    out_ref,
    core_in,
    part,
    part_low,
    x_in,
    y_in,
    mine,
    z_in,
    sem_core,
    sem_x,
    sem_y,
    sem_z,
    sem_gy,
    sem_gx,
    sem_gc,
):
    d = lax.axis_index("dp")
    r = lax.axis_index("row")
    core = lax.rem(d, 2)
    y = lax.rem(d // 2, 2)
    x = d // 4
    other_core = d + 1 - 2 * core
    other_y = d + 2 - 4 * y

    def x_peer(k):
        return lax.rem(x + k, 4) * 4 + y * 2 + core

    greet(
        [{"dp": other_core}, {"dp": other_y}]
        + [{"dp": x_peer(k)} for k in (1, 2, 3)]
        + [{"row": lax.rem(r + k, 4)} for k in (1, 2, 3)]
    )
    rows = lambda start, size: pl.ds(pl.multiple_of(start, 16), size)
    pending = []

    def go(*args, **device):
        copy = rcopy(*args, **device)
        copy.start()
        pending.append(copy)
        return copy

    first = [
        go(
            g_ref.at[t, :, rows((1 - core) * 128, 128), :],
            core_in.at[t],
            sem_core.at[0, t],
            sem_core.at[1, t],
            dp=other_core,
        )
        for t in range(count)
    ]
    second = []
    for t in range(count):
        first[t].wait_recv()
        total = g_ref[t, :, rows(core * 128, 128), :].astype(F32) + core_in[t].astype(F32)
        part[t] = total
        part_low[t, :, 0:128, :] = total.astype(BF)
        second.append(
            [
                go(
                    part_low.at[t, :, rows(lax.rem(x + k, 4) * 32, 32), :],
                    x_in.at[t, k - 1],
                    sem_x.at[0, t, k - 1],
                    sem_x.at[1, t, k - 1],
                    dp=x_peer(k),
                )
                for k in (1, 2, 3)
            ]
        )
    third = []
    for t in range(count):
        total = part[t, :, rows(x * 32, 32), :]
        for k in (1, 2, 3):
            second[t][k - 1].wait_recv()
            total = total + x_in[t, k - 1].astype(F32)
        part[t, :, 0:32, :] = total
        part_low[t, :, 128:160, :] = total.astype(BF)
        third.append(
            go(
                part_low.at[t, :, rows(128 + (1 - y) * 16, 16), :],
                y_in.at[t],
                sem_y.at[0, t],
                sem_y.at[1, t],
                dp=other_y,
            )
        )
    fourth = []
    for t in range(count):
        third[t].wait_recv()
        total = part[t, :, rows(y * 16, 16), :] + y_in[t].astype(F32)
        mine[t] = total.astype(BF)
        fourth.append(
            [
                go(
                    mine.at[t, lax.rem(r + k, 4)],
                    z_in.at[t, r],
                    sem_z.at[0, t, k - 1],
                    sem_z.at[1, t, k - 1],
                    row=lax.rem(r + k, 4),
                )
                for k in (1, 2, 3)
            ]
        )
    own = core * 128 + x * 32 + y * 16
    gather = []
    for t in range(count):
        z_in[t, r] = mine[t, r]
        for k in (1, 2, 3):
            fourth[t][k - 1].wait_recv()
        if joined:
            for q in range(3):
                out_ref[t, rows(own, 16), q * WIN : (q + 1) * WIN] = z_in[t, q]
            out_ref[t, rows(own, 16), 3 * WIN : HALF_FF] = z_in[t, 3][:, 4 * WIN - HALF_FF :]
        else:
            total = z_in[t, 0].astype(F32)
            for q in range(1, 4):
                total = total + z_in[t, q].astype(F32)
            out_ref[t, rows(own, 16), :] = total.astype(BF)
        block = out_ref.at[t, rows(own, 16), :]
        gather.append(go(block, block, sem_gy.at[0, t], sem_gy.at[1, t], dp=other_y))
    wide = core * 128 + x * 32
    spread = []
    for t in range(count):
        gather[t].wait_recv()
        block = out_ref.at[t, rows(wide, 32), :]
        spread.append(
            [
                go(
                    block,
                    block,
                    sem_gx.at[0, t, k - 1],
                    sem_gx.at[1, t, k - 1],
                    dp=x_peer(k),
                )
                for k in (1, 2, 3)
            ]
        )
    last = []
    for t in range(count):
        for k in (1, 2, 3):
            spread[t][k - 1].wait_recv()
        block = out_ref.at[t, rows(core * 128, 128), :]
        last.append(go(block, block, sem_gc.at[0, t], sem_gc.at[1, t], dp=other_core))
    for t in range(count):
        last[t].wait_recv()
    for copy in pending:
        copy.wait_send()


def sum_grads(grads, joined, collective):
    count = grads.shape[0]
    width = grads.shape[3]
    out_width = HALF_FF if joined else width
    dma = pltpu.SemaphoreType.DMA
    return vmem_call(
        functools.partial(grads_kernel, count, joined),
        1,
        jax.ShapeDtypeStruct((count, PADF, out_width), BF),
        [
            pltpu.VMEM((count, 4, 128, width), BF),
            pltpu.VMEM((count, 4, 128, width), F32),
            pltpu.VMEM((count, 4, 160, width), BF),
            pltpu.VMEM((count, 3, 4, 32, width), BF),
            pltpu.VMEM((count, 4, 16, width), BF),
            pltpu.VMEM((count, 4, 16, width), BF),
            pltpu.VMEM((count, 4, 16, width), BF),
            dma((2, count)),
            dma((2, count, 3)),
            dma((2, count)),
            dma((2, count, 3)),
            dma((2, count)),
            dma((2, count, 3)),
            dma((2, count)),
        ],
        collective,
    )(grads)


def ffn_kernel(
    ns_ref,
    cot_ref,
    gate_ref,
    up_ref,
    down_ref,
    mid_ref,
    second_ref,
    block_ref,
    grads_ref,
    ns_all,
    hid,
    gg,
    gu,
    sp_send,
    sp_in,
    op_send,
    op_in,
    cs_send,
    cs_in,
    co_send,
    co_in,
    sem_ag,
    sem_sp,
    sem_op,
    sem_cs,
    sem_co,
):
    r = lax.axis_index("row")
    c = lax.axis_index("col")
    greet([{"row": lax.rem(r + k, 4)} for k in (1, 2, 3)] + [{"col": 1 - c}])
    pending = []

    def go(*args, **device):
        copy = rcopy(*args, **device)
        copy.start()
        pending.append(copy)
        return copy

    span = lambda q: pl.ds(pl.multiple_of(q * SHARE, SHARE), SHARE)
    incoming = [
        go(
            ns_ref,
            ns_all.at[:, span(r), :],
            sem_ag.at[0, k - 1],
            sem_ag.at[1, k - 1],
            row=lax.rem(r + k, 4),
        )
        for k in (1, 2, 3)
    ]
    ns_all[:, span(r), :] = ns_ref[...]
    back = []
    for k in range(4):
        q = lax.rem(r + 4 - k, 4)
        grad_hidden = dot_nt(cot_ref[0, span(q), :], down_ref[0])
        for j in range(1, 4):
            grad_hidden += dot_nt(cot_ref[j, span(q), :], down_ref[j])
        if k:
            incoming[k - 1].wait_recv()
        gate = dot(ns_all[0, span(q), :], gate_ref[0])
        up = dot(ns_all[0, span(q), :], up_ref[0])
        for j in range(1, 4):
            gate += dot(ns_all[j, span(q), :], gate_ref[j])
            up += dot(ns_all[j, span(q), :], up_ref[j])
        sigma = 1.0 / (1.0 + jnp.exp(-gate))
        silu = gate * sigma
        hid[span(q), :] = (silu * up).astype(BF)
        g_gate = (grad_hidden * up * (sigma + silu * (1.0 - sigma))).astype(BF)
        g_up = (grad_hidden * silu).astype(BF)
        gg[span(q), :] = g_gate
        gu[span(q), :] = g_up
        for j in range(4):
            sp_send[k, j] = (
                dot_nt(g_gate, gate_ref[j]) + dot_nt(g_up, up_ref[j])
            ).astype(BF)
        if k:
            back.append(
                go(
                    sp_send.at[k],
                    sp_in.at[k - 1],
                    sem_sp.at[0, k - 1],
                    sem_sp.at[1, k - 1],
                    row=q,
                )
            )
    outgoing = []
    for k in (1, 2, 3, 0):
        j = lax.rem(r + k, 4)
        for q in range(4):
            op_send[j, q * SHARE : (q + 1) * SHARE, :] = dot(
                hid[q * SHARE : (q + 1) * SHARE, :], down_ref[j]
            ).astype(BF)
        op_send[j, span(r), :] = (
            op_send[j, span(r), :].astype(F32) + 0.5 * mid_ref[j]
        ).astype(BF)
        if k:
            outgoing.append(
                go(
                    op_send.at[j],
                    op_in.at[k - 1],
                    sem_op.at[0, k - 1],
                    sem_op.at[1, k - 1],
                    row=j,
                )
            )
    total = sp_send[0].astype(F32)
    for k in (1, 2, 3):
        back[k - 1].wait_recv()
        total += sp_in[k - 1].astype(F32)
    cs_send[...] = total.astype(BF)
    cross = go(cs_send, cs_in, sem_cs.at[0], sem_cs.at[1], col=1 - c)
    grads_ref[:, :, FEAT:PADF, :] = jnp.zeros((3, 4, PADF - FEAT, WIN), BF)
    for j in range(4):
        grads_ref[0, j, 0:FEAT, :] = dot_tn(ns_all[j], gg[...]).astype(BF)
        grads_ref[1, j, 0:FEAT, :] = dot_tn(ns_all[j], gu[...]).astype(BF)
        grads_ref[2, j, 0:FEAT, :] = dot_tn(cot_ref[j], hid[...]).astype(BF)
    total = op_send[r].astype(F32)
    for k in (1, 2, 3):
        outgoing[k - 1].wait_recv()
        total += op_in[k - 1].astype(F32)
    co_send[...] = total.astype(BF)
    final = go(co_send, co_in, sem_co.at[0], sem_co.at[1], col=1 - c)
    cross.wait_recv()
    second_ref[...] = cs_send[...].astype(F32) + cs_in[...].astype(F32)
    final.wait_recv()
    block_ref[...] = (co_send[...].astype(F32) + co_in[...].astype(F32)).astype(BF)
    for copy in pending:
        copy.wait_send()


def feed_forward(ns, cot_all, gate_full, up_full, down_full, middle):
    dma = pltpu.SemaphoreType.DMA
    blocked = pltpu.VMEM((4, SHARE, FEAT), BF)
    return vmem_call(
        ffn_kernel,
        6,
        (
            jax.ShapeDtypeStruct((4, SHARE, FEAT), F32),
            jax.ShapeDtypeStruct((SHARD, FEAT), BF),
            jax.ShapeDtypeStruct((3, 4, PADF, WIN), BF),
        ),
        [
            pltpu.VMEM((4, SHARD, FEAT), BF),
            pltpu.VMEM((SHARD, WIN), BF),
            pltpu.VMEM((SHARD, WIN), BF),
            pltpu.VMEM((SHARD, WIN), BF),
            pltpu.VMEM((4, 4, SHARE, FEAT), BF),
            pltpu.VMEM((3, 4, SHARE, FEAT), BF),
            pltpu.VMEM((4, SHARD, FEAT), BF),
            pltpu.VMEM((3, SHARD, FEAT), BF),
            blocked,
            blocked,
            pltpu.VMEM((SHARD, FEAT), BF),
            pltpu.VMEM((SHARD, FEAT), BF),
            dma((2, 3)),
            dma((2, 3)),
            dma((2, 3)),
            dma((2,)),
            dma((2,)),
        ],
        1,
        pl.CostEstimate(flops=12 * 10**9, bytes_accessed=16 * 10**6, transcendentals=10**6),
    )(ns, cot_all, gate_full, up_full, down_full, middle)


def col_sum(values):
    own = values.astype(BF)
    other = lax.ppermute(own, "col", [(0, 1), (1, 0)])
    return own.astype(F32) + other.astype(F32)


def masked_scores(queries, key_part, allowed):
    scores = (
        jnp.einsum("qmd,kd->mqk", queries, key_part, preferred_element_type=F32)
        * HEAD_DIM ** (-0.5)
    )
    return jnp.where(allowed[None], scores, -1e30)


def attend_forward(queries, pairs, allowed):
    scores = masked_scores(queries, pairs[:, :HEAD_DIM], allowed)
    peak = jnp.max(scores, axis=-1, keepdims=True)
    powered = jnp.exp(scores - peak)
    denominator = jnp.sum(powered, axis=-1, keepdims=True)
    probs = (powered / denominator).astype(BF)
    mixed = jnp.einsum(
        "mqk,kd->qmd", probs, pairs[:, HEAD_DIM:], preferred_element_type=F32
    )
    return (mixed, peak + jnp.log(denominator))


def attend_backward(queries, pairs, allowed, log_total, grad_mixed):
    key_part = pairs[:, :HEAD_DIM]
    value_part = pairs[:, HEAD_DIM:]
    scores = masked_scores(queries, key_part, allowed)
    probs = jnp.exp(scores - log_total)
    probs_low = probs.astype(BF)
    grad_values = jnp.einsum(
        "mqk,qmd->kd", probs_low, grad_mixed, preferred_element_type=F32
    )
    grad_probs = jnp.einsum(
        "qmd,kd->mqk", grad_mixed, value_part, preferred_element_type=F32
    )
    inner_sum = jnp.sum(probs * grad_probs, axis=-1, keepdims=True)
    grad_scores = (probs * (grad_probs - inner_sum)).astype(BF)
    grad_queries = (
        jnp.einsum("mqk,kd->qmd", grad_scores, key_part, preferred_element_type=F32)
        * HEAD_DIM ** (-0.5)
    )
    grad_keys = (
        jnp.einsum("mqk,qmd->kd", grad_scores, queries, preferred_element_type=F32)
        * HEAD_DIM ** (-0.5)
    )
    return (grad_queries, jnp.concatenate([grad_keys, grad_values], axis=1))


def windows(weight, axis):
    return jnp.stack(
        [
            lax.slice_in_dim(weight, min(WIN * q, LAST), min(WIN * q, LAST) + WIN, axis=axis)
            for q in range(ROWS)
        ]
    )


def exchange(blocks):
    return lax.all_to_all(blocks, "row", 0, 0, tiled=True)


def body(
    activations,
    starts,
    first_gain,
    project_weight,
    project_bias,
    output_weight,
    second_gain,
    gate_weight,
    up_weight,
    down_weight,
    cotangent,
):
    window = MAXLEN + SHARE
    r = lax.axis_index("row")
    shard = lax.axis_index("dp")
    group_heads = HEADS // GROUPS
    query_width = group_heads * HEAD_DIM

    x_low = exchange(activations.reshape(ROWS, SHARE, FEAT))
    gains = lax.all_gather(jnp.stack([first_gain, second_gain]), "row")
    gain_one = gains[:, 0][:, None, :]
    gain_two = gains[:, 1][:, None, :]
    project_full = lax.all_gather(project_weight, "row")
    output_full = lax.all_gather(output_weight, "row")
    live = (jnp.arange(WIN) >= 4 * WIN - HALF_FF) | (r < 3)
    gate_full = jnp.where(live, exchange(windows(gate_weight, 1)), 0).astype(BF)
    up_full = jnp.where(live, exchange(windows(up_weight, 1)), 0).astype(BF)
    down_full = exchange(windows(down_weight, 0))
    cot_all = lax.all_gather(cotangent, "row")

    local_index = r * SHARE + jnp.arange(SHARE, dtype=jnp.int32)
    start_local = (
        lax.dynamic_slice_in_dim(starts, r * SHARE, SHARE, 0) - shard * SHARD
    )
    positions = (local_index - start_local).astype(F32)
    half = HEAD_DIM // 2
    freqs = 1000000.0 ** (-jnp.arange(half, dtype=F32) * 2.0 / HEAD_DIM)
    angle = positions[:, None] * freqs[None, :]
    cosine, sine = jnp.cos(angle), jnp.sin(angle)
    key_local = r * SHARE - MAXLEN + jnp.arange(window, dtype=jnp.int32)
    allowed = (key_local[None, :] >= start_local[:, None]) & (
        key_local[None, :] <= local_index[:, None]
    )

    x = x_low.astype(F32)
    first_rate = lax.rsqrt(jnp.mean(x * x, axis=(0, 2))[None, :, None] + EPS)
    normed_first = (x * first_rate * gain_one).astype(BF)
    projected = (
        jnp.einsum("jtf,jfn->tn", normed_first, project_full, preferred_element_type=F32)
        + project_bias
    )
    queries = rotate(
        projected[:, :query_width].reshape(SHARE, group_heads, HEAD_DIM), cosine, sine
    ).astype(BF)
    keys_new = rotate(projected[:, query_width : query_width + HEAD_DIM], cosine, sine)
    pair_share = jnp.concatenate(
        [keys_new, projected[:, query_width + HEAD_DIM :]], axis=1
    ).astype(BF)
    shard_pairs = lax.all_gather(pair_share, "row", axis=0, tiled=True)
    earlier = from_behind(shard_pairs, "dp", 1)
    pairs = lax.dynamic_slice_in_dim(
        jnp.concatenate([earlier, shard_pairs], axis=0), r * SHARE, window, 0
    )
    mixed, log_total = attend_forward(queries, pairs, allowed)
    attended = mixed.reshape(SHARE, query_width).astype(BF)
    middle = x + col_sum(
        jnp.einsum("th,jhf->jtf", attended, output_full, preferred_element_type=F32)
    )
    second_rate = lax.rsqrt(jnp.mean(middle * middle, axis=(0, 2))[None, :, None] + EPS)
    normed_second = (middle * second_rate * gain_two).astype(BF)

    grad_second, block_output, ff_grads = feed_forward(
        normed_second, cot_all, gate_full, up_full, down_full, middle
    )

    cot_own = lax.dynamic_slice_in_dim(cot_all, r * SHARE, SHARE, 1).astype(F32)
    weighted_second = grad_second * gain_two
    second_inner = jnp.sum(weighted_second * middle, axis=(0, 2))[None, :, None]
    second_gain_grad = jnp.sum(grad_second * middle * second_rate, axis=1)
    grad_middle = (
        cot_own
        + second_rate * weighted_second
        - middle * (second_rate**3 * second_inner / D)
    )
    grad_branch = grad_middle.astype(BF)
    grad_attended = (
        jnp.einsum("jtf,jhf->th", grad_branch, output_full, preferred_element_type=F32)
        .astype(BF)
        .reshape(SHARE, group_heads, HEAD_DIM)
    )
    grad_queries, grad_pairs = attend_backward(
        queries, pairs, allowed, log_total, grad_attended
    )
    grad_wide = lax.dynamic_update_slice(
        jnp.zeros((MAXLEN + SHARD, 2 * HEAD_DIM), F32), grad_pairs, (r * SHARE, 0)
    )
    returned = from_behind(grad_wide[:MAXLEN].astype(BF), "dp", -1)
    own_pairs = (grad_wide[MAXLEN:] + returned.astype(F32)).astype(BF)
    grad_pair = lax.psum_scatter(
        own_pairs, "row", scatter_dimension=0, tiled=True
    ).astype(F32)
    grad_keys = rotate(grad_pair[:, :HEAD_DIM], cosine, -sine)
    grad_query_plain = rotate(grad_queries, cosine, -sine).reshape(SHARE, query_width)
    grad_projected = jnp.concatenate(
        [grad_query_plain, grad_keys, grad_pair[:, HEAD_DIM:]], axis=1
    ).astype(BF)
    grad_first = col_sum(
        jnp.einsum("tn,jfn->jtf", grad_projected, project_full, preferred_element_type=F32)
    )
    weighted_first = grad_first * gain_one
    first_inner = jnp.sum(weighted_first * x, axis=(0, 2))[None, :, None]
    first_gain_grad = jnp.sum(grad_first * x * first_rate, axis=1)
    input_own = (
        grad_middle
        + first_rate * weighted_first
        - x * (first_rate**3 * first_inner / D)
    )
    input_grad = exchange(input_own.astype(BF)).reshape(SHARD, FEAT).astype(F32)

    ff_sum = sum_grads(ff_grads, True, 2)[:, :FEAT].astype(F32)
    width = project_weight.shape[1]
    at_grads = jnp.concatenate(
        [
            jnp.einsum("jtf,tn->jfn", normed_first, grad_projected, preferred_element_type=F32),
            jnp.einsum("jtf,th->jfh", grad_branch, attended, preferred_element_type=F32),
        ],
        axis=2,
    ).astype(BF)
    at_grads = jnp.pad(at_grads, ((0, 0), (0, PADF - FEAT), (0, 0)))
    at_sum = sum_grads(at_grads[None], False, 3)[0, :FEAT].astype(F32)
    bias_grad = jnp.sum(grad_projected.astype(F32), axis=0)
    small = lax.psum(
        jnp.concatenate([first_gain_grad.ravel(), second_gain_grad.ravel(), bias_grad]),
        ("dp", "row"),
    )
    first_gain_grad = lax.dynamic_slice_in_dim(small[:D], r * FEAT, FEAT, 0)
    second_gain_grad = lax.dynamic_slice_in_dim(small[D : 2 * D], r * FEAT, FEAT, 0)
    bias_grad = small[2 * D :]
    return (
        block_output,
        input_grad,
        first_gain_grad,
        at_sum[:, :width],
        bias_grad,
        at_sum[:, width:].T,
        second_gain_grad,
        ff_sum[0],
        ff_sum[1],
        ff_sum[2].T,
    )


def solution(mesh):
    return jax.shard_map(
        body,
        mesh=mesh,
        in_specs=(
            P("dp", "row"),
            P("dp"),
            P("row"),
            P("row", "col"),
            P("col"),
            P("col", "row"),
            P("row"),
            P("row", "col"),
            P("row", "col"),
            P("col", "row"),
            P("dp", "row"),
        ),
        out_specs=(
            P("dp", "row"),
            P("dp", "row"),
            P("row"),
            P("row", "col"),
            P("col"),
            P("col", "row"),
            P("row"),
            P("row", "col"),
            P("row", "col"),
            P("col", "row"),
        ),
        check_vma=False,
    )
```

```python
import functools

import jax
import jax.numpy as jnp
from jax import lax
from jax.experimental import pallas as pl
from jax.experimental.pallas import tpu as pltpu
from jax.sharding import PartitionSpec as P

D = 896
HEADS = 14
GROUPS = 2
HEAD_DIM = 64
MAXLEN = 1024
EPS = 1e-06
BF = jnp.bfloat16
F32 = jnp.float32
ROWS = 4
FEAT = 224
SHARE = 256
SHARD = 1024
HALF_FF = 2432
WIN = 640
LAST = HALF_FF - WIN
PADF = 256
VMEM_LIMIT = 60 * 1024 * 1024


def from_behind(block, axis, distance):
    devices = range(lax.axis_size(axis))
    route = [(i - distance, i) for i in devices if i - distance in devices]
    return lax.ppermute(block, axis, route)


def rotate(values, cosine, sine):
    half = HEAD_DIM // 2
    if values.ndim == 3:
        cosine = cosine[:, None, :]
        sine = sine[:, None, :]
    first = values[..., :half]
    second = values[..., half:]
    return jnp.concatenate(
        [first * cosine - second * sine, second * cosine + first * sine], axis=-1
    )


def dot(a, b):
    return jnp.dot(a, b, preferred_element_type=F32)


def dot_nt(a, b):
    return lax.dot_general(a, b, (((1,), (1,)), ((), ())), preferred_element_type=F32)


def dot_tn(a, b):
    return lax.dot_general(a, b, (((0,), (0,)), ((), ())), preferred_element_type=F32)


def rcopy(src, dst, send, recv, **device):
    return pltpu.make_async_remote_copy(
        src_ref=src,
        dst_ref=dst,
        send_sem=send,
        recv_sem=recv,
        device_id=device,
        device_id_type=pl.DeviceIdType.MESH,
    )


def greet(peers):
    barrier = pltpu.get_barrier_semaphore()
    for peer in peers:
        pl.semaphore_signal(
            barrier, inc=1, device_id=peer, device_id_type=pl.DeviceIdType.MESH
        )
    pl.semaphore_wait(barrier, len(peers))


def vmem_call(kernel, inputs, outs, scratch, collective, cost=None):
    return pl.pallas_call(
        kernel,
        out_shape=outs,
        in_specs=[pl.BlockSpec(memory_space=pltpu.VMEM)] * inputs,
        out_specs=jax.tree.map(lambda _: pl.BlockSpec(memory_space=pltpu.VMEM), outs),
        scratch_shapes=scratch,
        compiler_params=pltpu.CompilerParams(
            collective_id=collective,
            has_side_effects=True,
            vmem_limit_bytes=VMEM_LIMIT,
        ),
        cost_estimate=cost,
    )


def grads_kernel(
    count,
    joined,
    g_ref,
    out_ref,
    core_in,
    part,
    part_low,
    x_in,
    y_in,
    mine,
    z_in,
    sem_core,
    sem_x,
    sem_y,
    sem_z,
    sem_gy,
    sem_gx,
    sem_gc,
):
    d = lax.axis_index("dp")
    r = lax.axis_index("row")
    core = lax.rem(d, 2)
    y = lax.rem(d // 2, 2)
    x = d // 4
    other_core = d + 1 - 2 * core
    other_y = d + 2 - 4 * y

    def x_peer(k):
        return lax.rem(x + k, 4) * 4 + y * 2 + core

    greet(
        [{"dp": other_core}, {"dp": other_y}]
        + [{"dp": x_peer(k)} for k in (1, 2, 3)]
        + [{"row": lax.rem(r + k, 4)} for k in (1, 2, 3)]
    )
    rows = lambda start, size: pl.ds(pl.multiple_of(start, 16), size)
    pending = []

    def go(*args, **device):
        copy = rcopy(*args, **device)
        copy.start()
        pending.append(copy)
        return copy

    first = [
        go(
            g_ref.at[t, :, rows((1 - core) * 128, 128), :],
            core_in.at[t],
            sem_core.at[0, t],
            sem_core.at[1, t],
            dp=other_core,
        )
        for t in range(count)
    ]
    second = []
    for t in range(count):
        first[t].wait_recv()
        total = g_ref[t, :, rows(core * 128, 128), :].astype(F32) + core_in[t].astype(F32)
        part[t] = total
        part_low[t, :, 0:128, :] = total.astype(BF)
        second.append(
            [
                go(
                    part_low.at[t, :, rows(lax.rem(x + k, 4) * 32, 32), :],
                    x_in.at[t, k - 1],
                    sem_x.at[0, t, k - 1],
                    sem_x.at[1, t, k - 1],
                    dp=x_peer(k),
                )
                for k in (1, 2, 3)
            ]
        )
    third = []
    for t in range(count):
        total = part[t, :, rows(x * 32, 32), :]
        for k in (1, 2, 3):
            second[t][k - 1].wait_recv()
            total = total + x_in[t, k - 1].astype(F32)
        part[t, :, 0:32, :] = total
        part_low[t, :, 128:160, :] = total.astype(BF)
        third.append(
            go(
                part_low.at[t, :, rows(128 + (1 - y) * 16, 16), :],
                y_in.at[t],
                sem_y.at[0, t],
                sem_y.at[1, t],
                dp=other_y,
            )
        )
    fourth = []
    for t in range(count):
        third[t].wait_recv()
        total = part[t, :, rows(y * 16, 16), :] + y_in[t].astype(F32)
        mine[t] = total.astype(BF)
        fourth.append(
            [
                go(
                    mine.at[t, lax.rem(r + k, 4)],
                    z_in.at[t, r],
                    sem_z.at[0, t, k - 1],
                    sem_z.at[1, t, k - 1],
                    row=lax.rem(r + k, 4),
                )
                for k in (1, 2, 3)
            ]
        )
    own = core * 128 + x * 32 + y * 16
    gather = []
    for t in range(count):
        z_in[t, r] = mine[t, r]
        for k in (1, 2, 3):
            fourth[t][k - 1].wait_recv()
        if joined:
            for q in range(3):
                out_ref[t, rows(own, 16), q * WIN : (q + 1) * WIN] = z_in[t, q]
            out_ref[t, rows(own, 16), 3 * WIN : HALF_FF] = z_in[t, 3][:, 4 * WIN - HALF_FF :]
        else:
            total = z_in[t, 0].astype(F32)
            for q in range(1, 4):
                total = total + z_in[t, q].astype(F32)
            out_ref[t, rows(own, 16), :] = total.astype(BF)
        block = out_ref.at[t, rows(own, 16), :]
        gather.append(go(block, block, sem_gy.at[0, t], sem_gy.at[1, t], dp=other_y))
    wide = core * 128 + x * 32
    spread = []
    for t in range(count):
        gather[t].wait_recv()
        block = out_ref.at[t, rows(wide, 32), :]
        spread.append(
            [
                go(
                    block,
                    block,
                    sem_gx.at[0, t, k - 1],
                    sem_gx.at[1, t, k - 1],
                    dp=x_peer(k),
                )
                for k in (1, 2, 3)
            ]
        )
    last = []
    for t in range(count):
        for k in (1, 2, 3):
            spread[t][k - 1].wait_recv()
        block = out_ref.at[t, rows(core * 128, 128), :]
        last.append(go(block, block, sem_gc.at[0, t], sem_gc.at[1, t], dp=other_core))
    for t in range(count):
        last[t].wait_recv()
    for copy in pending:
        copy.wait_send()


def sum_grads(grads, joined, collective):
    count = grads.shape[0]
    width = grads.shape[3]
    out_width = HALF_FF if joined else width
    dma = pltpu.SemaphoreType.DMA
    return vmem_call(
        functools.partial(grads_kernel, count, joined),
        1,
        jax.ShapeDtypeStruct((count, PADF, out_width), BF),
        [
            pltpu.VMEM((count, 4, 128, width), BF),
            pltpu.VMEM((count, 4, 128, width), F32),
            pltpu.VMEM((count, 4, 160, width), BF),
            pltpu.VMEM((count, 3, 4, 32, width), BF),
            pltpu.VMEM((count, 4, 16, width), BF),
            pltpu.VMEM((count, 4, 16, width), BF),
            pltpu.VMEM((count, 4, 16, width), BF),
            dma((2, count)),
            dma((2, count, 3)),
            dma((2, count)),
            dma((2, count, 3)),
            dma((2, count)),
            dma((2, count, 3)),
            dma((2, count)),
        ],
        collective,
    )(grads)


def ffn_kernel(
    ns_ref,
    cot_ref,
    gate_ref,
    up_ref,
    down_ref,
    mid_ref,
    second_ref,
    block_ref,
    grads_ref,
    ns_all,
    hid,
    gg,
    gu,
    sp_send,
    sp_in,
    op_send,
    op_in,
    cs_send,
    cs_in,
    co_send,
    co_in,
    sem_ag,
    sem_sp,
    sem_op,
    sem_cs,
    sem_co,
):
    r = lax.axis_index("row")
    c = lax.axis_index("col")
    greet([{"row": lax.rem(r + k, 4)} for k in (1, 2, 3)] + [{"col": 1 - c}])
    pending = []

    def go(*args, **device):
        copy = rcopy(*args, **device)
        copy.start()
        pending.append(copy)
        return copy

    span = lambda q: pl.ds(pl.multiple_of(q * SHARE, SHARE), SHARE)
    incoming = [
        go(
            ns_ref,
            ns_all.at[:, span(r), :],
            sem_ag.at[0, k - 1],
            sem_ag.at[1, k - 1],
            row=lax.rem(r + k, 4),
        )
        for k in (1, 2, 3)
    ]
    ns_all[:, span(r), :] = ns_ref[...]
    back = []
    for k in range(4):
        q = lax.rem(r + 4 - k, 4)
        grad_hidden = dot_nt(cot_ref[0, span(q), :], down_ref[0])
        for j in range(1, 4):
            grad_hidden += dot_nt(cot_ref[j, span(q), :], down_ref[j])
        if k:
            incoming[k - 1].wait_recv()
        gate = dot(ns_all[0, span(q), :], gate_ref[0])
        up = dot(ns_all[0, span(q), :], up_ref[0])
        for j in range(1, 4):
            gate += dot(ns_all[j, span(q), :], gate_ref[j])
            up += dot(ns_all[j, span(q), :], up_ref[j])
        sigma = 1.0 / (1.0 + jnp.exp(-gate))
        silu = gate * sigma
        hid[span(q), :] = (silu * up).astype(BF)
        g_gate = (grad_hidden * up * (sigma + silu * (1.0 - sigma))).astype(BF)
        g_up = (grad_hidden * silu).astype(BF)
        gg[span(q), :] = g_gate
        gu[span(q), :] = g_up
        for j in range(4):
            sp_send[k, j] = (
                dot_nt(g_gate, gate_ref[j]) + dot_nt(g_up, up_ref[j])
            ).astype(BF)
        if k:
            back.append(
                go(
                    sp_send.at[k],
                    sp_in.at[k - 1],
                    sem_sp.at[0, k - 1],
                    sem_sp.at[1, k - 1],
                    row=q,
                )
            )
    outgoing = []
    for k in (1, 2, 3, 0):
        j = lax.rem(r + k, 4)
        for q in range(4):
            op_send[j, q * SHARE : (q + 1) * SHARE, :] = dot(
                hid[q * SHARE : (q + 1) * SHARE, :], down_ref[j]
            ).astype(BF)
        op_send[j, span(r), :] = (
            op_send[j, span(r), :].astype(F32) + 0.5 * mid_ref[j]
        ).astype(BF)
        if k:
            outgoing.append(
                go(
                    op_send.at[j],
                    op_in.at[k - 1],
                    sem_op.at[0, k - 1],
                    sem_op.at[1, k - 1],
                    row=j,
                )
            )
    total = sp_send[0].astype(F32)
    for k in (1, 2, 3):
        back[k - 1].wait_recv()
        total += sp_in[k - 1].astype(F32)
    cs_send[...] = total.astype(BF)
    cross = go(cs_send, cs_in, sem_cs.at[0], sem_cs.at[1], col=1 - c)
    grads_ref[:, :, FEAT:PADF, :] = jnp.zeros((3, 4, PADF - FEAT, WIN), BF)
    for j in range(4):
        grads_ref[0, j, 0:FEAT, :] = dot_tn(ns_all[j], gg[...]).astype(BF)
        grads_ref[1, j, 0:FEAT, :] = dot_tn(ns_all[j], gu[...]).astype(BF)
        grads_ref[2, j, 0:FEAT, :] = dot_tn(cot_ref[j], hid[...]).astype(BF)
    total = op_send[r].astype(F32)
    for k in (1, 2, 3):
        outgoing[k - 1].wait_recv()
        total += op_in[k - 1].astype(F32)
    co_send[...] = total.astype(BF)
    final = go(co_send, co_in, sem_co.at[0], sem_co.at[1], col=1 - c)
    cross.wait_recv()
    second_ref[...] = cs_send[...].astype(F32) + cs_in[...].astype(F32)
    final.wait_recv()
    block_ref[...] = (co_send[...].astype(F32) + co_in[...].astype(F32)).astype(BF)
    for copy in pending:
        copy.wait_send()


def feed_forward(ns, cot_all, gate_full, up_full, down_full, middle):
    dma = pltpu.SemaphoreType.DMA
    blocked = pltpu.VMEM((4, SHARE, FEAT), BF)
    return vmem_call(
        ffn_kernel,
        6,
        (
            jax.ShapeDtypeStruct((4, SHARE, FEAT), F32),
            jax.ShapeDtypeStruct((SHARD, FEAT), BF),
            jax.ShapeDtypeStruct((3, 4, PADF, WIN), BF),
        ),
        [
            pltpu.VMEM((4, SHARD, FEAT), BF),
            pltpu.VMEM((SHARD, WIN), BF),
            pltpu.VMEM((SHARD, WIN), BF),
            pltpu.VMEM((SHARD, WIN), BF),
            pltpu.VMEM((4, 4, SHARE, FEAT), BF),
            pltpu.VMEM((3, 4, SHARE, FEAT), BF),
            pltpu.VMEM((4, SHARD, FEAT), BF),
            pltpu.VMEM((3, SHARD, FEAT), BF),
            blocked,
            blocked,
            pltpu.VMEM((SHARD, FEAT), BF),
            pltpu.VMEM((SHARD, FEAT), BF),
            dma((2, 3)),
            dma((2, 3)),
            dma((2, 3)),
            dma((2,)),
            dma((2,)),
        ],
        1,
        pl.CostEstimate(flops=12 * 10**9, bytes_accessed=16 * 10**6, transcendentals=10**6),
    )(ns, cot_all, gate_full, up_full, down_full, middle)


def swapped(values):
    width = values.shape[1]
    lane = lax.broadcasted_iota(jnp.int32, values.shape, 1)
    return jnp.where(
        lax.rem(lane, 64) < 32,
        pltpu.roll(values, width - 32, 1),
        pltpu.roll(values, 32, 1),
    )


def front_kernel(
    act_ref,
    cot_ref,
    proj_ref,
    outw_ref,
    gate_ref,
    up_ref,
    down_ref,
    gains_ref,
    bias_ref,
    cos_ref,
    sin_ref,
    start_ref,
    x_out,
    nf_out,
    q_out,
    kv_out,
    lse_out,
    att_out,
    mid_out,
    ns_out,
    proj_full,
    outw_full,
    gate_full,
    up_full,
    down_full,
    cot_all,
    gains_full,
    mask,
    own_kv,
    c_send,
    c_in,
    sem_x,
    sem_g,
    sem_w,
    sem_wc,
    sem_cot,
    sem_kv,
    sem_c,
    sem_l,
):
    d = lax.axis_index("dp")
    r = lax.axis_index("row")
    c = lax.axis_index("col")
    core = lax.rem(d, 2)
    sibling = d + 1 - 2 * core
    block = 4 * d + r
    near = lambda i: {
        "dp": lax.rem((block + 64 + i) // 4, 16),
        "row": lax.rem(r + 4 + i, 4),
    }
    greet(
        [{"row": lax.rem(r + k, 4)} for k in (1, 2, 3)]
        + [{"col": 1 - c}, {"dp": sibling}]
        + [near(i) for i in (1, 2, 3, 4, -1, -2, -3, -4)]
    )
    pending = []

    def go(*args, **device):
        copy = rcopy(*args, **device)
        copy.start()
        pending.append(copy)
        return copy

    peers = [(k, lax.rem(r + k, 4)) for k in (1, 2, 3)]
    span = lambda q: pl.ds(pl.multiple_of(q * SHARE, SHARE), SHARE)
    offset = lambda q: pl.multiple_of(jnp.minimum(q * WIN, LAST), 128)
    half = lambda n: pl.ds(pl.multiple_of(core * n, 16), n)

    def down_rows(q):
        return pl.ds(pl.multiple_of(offset(q) + core * (WIN // 2), 16), WIN // 2)

    pieces = (
        (lambda q: proj_ref.at[half(112), :], proj_full, 112),
        (lambda q: outw_ref.at[half(224), :], outw_full, 224),
        (lambda q: gate_ref.at[half(112), pl.ds(offset(q), WIN)], gate_full, 112),
        (lambda q: up_ref.at[half(112), pl.ds(offset(q), WIN)], up_full, 112),
        (lambda q: down_ref.at[down_rows(q), :], down_full, WIN // 2),
    )

    def fetch(w):
        source, full, n = pieces[w]
        copies = [
            go(
                source(q),
                full.at[r, half(n), :],
                sem_w.at[0, w, k - 1],
                sem_w.at[1, w, k - 1],
                row=q,
            )
            for k, q in peers
        ]
        local = pltpu.make_async_copy(source(r), full.at[r, half(n), :], sem_l.at[w])
        local.start()
        return copies, local

    def share(w, fetched):
        _, full, n = pieces[w]
        copies, local = fetched
        local.wait()
        for copy in copies:
            copy.wait_recv()
        part = full.at[:, half(n), :]
        return go(part, part, sem_wc.at[0, w], sem_wc.at[1, w], dp=sibling)

    x_copies = [
        go(
            act_ref.at[span(q), :],
            x_out.at[r],
            sem_x.at[0, k - 1],
            sem_x.at[1, k - 1],
            row=q,
        )
        for k, q in peers
    ]
    g_copies = [
        go(gains_ref, gains_full.at[r], sem_g.at[0, k - 1], sem_g.at[1, k - 1], row=q)
        for k, q in peers
    ]
    fetched = {0: fetch(0)}
    x_out[r] = act_ref[span(r), :]
    gains_full[r] = gains_ref[...]
    query_at = lax.broadcasted_iota(jnp.int32, (SHARE, 1), 0) + MAXLEN
    key_at = lax.broadcasted_iota(jnp.int32, (SHARE, MAXLEN + SHARE), 1)
    mask[...] = jnp.where(
        (key_at >= start_ref[...]) & (key_at <= query_at), 0.0, -1e30
    )
    shared = {0: share(0, fetched[0])}
    for copy in x_copies + g_copies:
        copy.wait_recv()
    for w in (1, 2, 3, 4):
        fetched[w] = fetch(w)
    cot_copies = [
        go(cot_ref, cot_all.at[r], sem_cot.at[0, k - 1], sem_cot.at[1, k - 1], row=q)
        for k, q in peers
    ]
    cot_all[r] = cot_ref[...]
    square = jnp.zeros((SHARE, 1), F32)
    for j in range(4):
        value = x_out[j].astype(F32)
        square += jnp.sum(value * value, axis=1, keepdims=True)
    rate = lax.rsqrt(square / D + EPS)
    for j in range(4):
        nf_out[j] = (x_out[j].astype(F32) * rate * gains_full[j, 0:1, :]).astype(BF)
    shared[0].wait_recv()
    projected = dot(nf_out[0], proj_full[0, :, 0:512])
    values = dot(nf_out[0], proj_full[0, :, 512:576])
    for j in range(1, 4):
        projected += dot(nf_out[j], proj_full[j, :, 0:512])
        values += dot(nf_out[j], proj_full[j, :, 512:576])
    projected += bias_ref[:, 0:512]
    values = (values + bias_ref[:, 512:576]).astype(BF)
    cosine = jnp.concatenate([cos_ref[...]] * 4, axis=1)
    sine = jnp.concatenate([sin_ref[...]] * 4, axis=1)
    turned = projected * cosine + swapped(projected) * sine
    q_out[...] = (turned * HEAD_DIM ** (-0.5)).astype(BF)
    tile = turned[:, 384:512]
    lane = lax.broadcasted_iota(jnp.int32, (SHARE, 128), 1)
    low = lane < 64
    own_kv[0] = jnp.where(low, pltpu.roll(tile, 64, 1), tile).astype(BF)
    double = (
        lax.rem(lax.broadcasted_iota(jnp.int32, (64, 128), 1), 64)
        == lax.broadcasted_iota(jnp.int32, (64, 128), 0)
    ).astype(F32).astype(BF)
    own_kv[1] = dot(values, double).astype(BF)
    kv_copies = [
        go(
            own_kv,
            kv_out.at[:, (4 - i) * SHARE : (5 - i) * SHARE, :],
            sem_kv.at[0, i - 1],
            sem_kv.at[1, i - 1],
            **near(i),
        )
        for i in (1, 2, 3, 4)
    ]
    kv_out[:, MAXLEN : MAXLEN + SHARE, :] = own_kv[...]
    for copy in kv_copies:
        copy.wait_recv()
    for m in range(HEADS // GROUPS):
        at = 128 * (m // 2)
        mine = low if m % 2 == 0 else jnp.logical_not(low)
        query = jnp.where(mine, q_out[:, at : at + 128].astype(F32), 0.0).astype(BF)
        scores = dot_nt(query, kv_out[0]) + mask[...]
        peak = jnp.max(scores, axis=1, keepdims=True)
        powered = jnp.exp(scores - peak)
        total = jnp.sum(powered, axis=1, keepdims=True)
        probs = (powered * (1.0 / total)).astype(BF)
        lse_out[m] = peak + jnp.log(total)
        mixed = dot(probs, kv_out[1])
        if m == 6:
            att_out[:, 384:448] = mixed[:, 0:64].astype(BF)
        elif m % 2 == 0:
            even = mixed
        else:
            att_out[:, at : at + 128] = jnp.where(low, even, mixed).astype(BF)
    shared[1] = share(1, fetched[1])
    shared[1].wait_recv()
    for j in range(4):
        c_send[j] = dot(att_out[...], outw_full[j]).astype(BF)
    cross = go(c_send, c_in, sem_c.at[0], sem_c.at[1], col=1 - c)
    for w in (2, 3, 4):
        shared[w] = share(w, fetched[w])
    cross.wait_recv()
    square = jnp.zeros((SHARE, 1), F32)
    for j in range(4):
        value = x_out[j].astype(F32) + (
            c_send[j].astype(F32) + c_in[j].astype(F32)
        )
        mid_out[j] = value
        square += jnp.sum(value * value, axis=1, keepdims=True)
    rate = lax.rsqrt(square / D + EPS)
    for j in range(4):
        ns_out[j] = (mid_out[j] * rate * gains_full[j, 1:2, :]).astype(BF)
    for copy in cot_copies:
        copy.wait_recv()
    for w in (2, 3, 4):
        shared[w].wait_recv()
    for copy in pending:
        copy.wait_send()
    live = jnp.where(r < 3, 1.0, 0.0)
    for j in range(4):
        extra = 4 * WIN - HALF_FF
        gate_full[j, :, 0:extra] = (gate_full[j, :, 0:extra].astype(F32) * live).astype(BF)
        up_full[j, :, 0:extra] = (up_full[j, :, 0:extra].astype(F32) * live).astype(BF)


def front(*operands):
    dma = pltpu.SemaphoreType.DMA
    shape = jax.ShapeDtypeStruct
    width = MAXLEN + SHARE
    blocked = pltpu.VMEM((4, SHARE, FEAT), BF)
    return vmem_call(
        front_kernel,
        12,
        (
            shape((4, SHARE, FEAT), BF),
            shape((4, SHARE, FEAT), BF),
            shape((SHARE, 512), BF),
            shape((2, width, 128), BF),
            shape((HEADS // GROUPS, SHARE, 1), F32),
            shape((SHARE, 448), BF),
            shape((4, SHARE, FEAT), F32),
            shape((4, SHARE, FEAT), BF),
            shape((4, FEAT, 576), BF),
            shape((4, 448, FEAT), BF),
            shape((4, FEAT, WIN), BF),
            shape((4, FEAT, WIN), BF),
            shape((4, WIN, FEAT), BF),
            shape((4, SHARD, FEAT), BF),
            shape((4, 8, FEAT), F32),
        ),
        [
            pltpu.VMEM((SHARE, width), F32),
            pltpu.VMEM((2, SHARE, 128), BF),
            blocked,
            blocked,
            dma((2, 3)),
            dma((2, 3)),
            dma((2, 5, 3)),
            dma((2, 5)),
            dma((2, 3)),
            dma((2, 4)),
            dma((2,)),
            dma((5,)),
        ],
        0,
    )(*operands)


def col_sum(values):
    own = values.astype(BF)
    other = lax.ppermute(own, "col", [(0, 1), (1, 0)])
    return own.astype(F32) + other.astype(F32)


def masked_scores(queries, key_part, allowed):
    scores = (
        jnp.einsum("qmd,kd->mqk", queries, key_part, preferred_element_type=F32)
        * HEAD_DIM ** (-0.5)
    )
    return jnp.where(allowed[None], scores, -1e30)


def attend_backward(queries, pairs, allowed, log_total, grad_mixed):
    key_part = pairs[:, :HEAD_DIM]
    value_part = pairs[:, HEAD_DIM:]
    scores = masked_scores(queries, key_part, allowed)
    probs = jnp.exp(scores - log_total)
    probs_low = probs.astype(BF)
    grad_values = jnp.einsum(
        "mqk,qmd->kd", probs_low, grad_mixed, preferred_element_type=F32
    )
    grad_probs = jnp.einsum(
        "qmd,kd->mqk", grad_mixed, value_part, preferred_element_type=F32
    )
    inner_sum = jnp.sum(probs * grad_probs, axis=-1, keepdims=True)
    grad_scores = (probs * (grad_probs - inner_sum)).astype(BF)
    grad_queries = (
        jnp.einsum("mqk,kd->qmd", grad_scores, key_part, preferred_element_type=F32)
        * HEAD_DIM ** (-0.5)
    )
    grad_keys = (
        jnp.einsum("mqk,qmd->kd", grad_scores, queries, preferred_element_type=F32)
        * HEAD_DIM ** (-0.5)
    )
    return (grad_queries, jnp.concatenate([grad_keys, grad_values], axis=1))


def exchange(blocks):
    return lax.all_to_all(blocks, "row", 0, 0, tiled=True)


def body(
    activations,
    starts,
    first_gain,
    project_weight,
    project_bias,
    output_weight,
    second_gain,
    gate_weight,
    up_weight,
    down_weight,
    cotangent,
):
    window = MAXLEN + SHARE
    r = lax.axis_index("row")
    shard = lax.axis_index("dp")
    group_heads = HEADS // GROUPS
    query_width = group_heads * HEAD_DIM

    base = shard * SHARD + r * SHARE
    start_window = (
        lax.dynamic_slice_in_dim(starts, r * SHARE, SHARE, 0) - base + MAXLEN
    )[:, None]
    positions = (MAXLEN + jnp.arange(SHARE, dtype=jnp.int32))[:, None] - start_window
    half = HEAD_DIM // 2
    freqs = 1000000.0 ** (-jnp.arange(half, dtype=F32) * 2.0 / HEAD_DIM)
    angle = positions.astype(F32) * jnp.tile(freqs, 4)[None, :]
    cosine = jnp.cos(angle)
    sine = jnp.sin(angle) * jnp.tile(jnp.repeat(jnp.array([-1.0, 1.0], F32), half), 2)[None, :]
    gains = jnp.pad(jnp.stack([first_gain, second_gain]), ((0, 6), (0, 0)))
    (
        x_low,
        normed_first,
        queries,
        kv,
        lse,
        attended,
        middle,
        normed_second,
        project_full,
        output_full,
        gate_full,
        up_full,
        down_full,
        cot_all,
        gains_full,
    ) = front(
        activations,
        cotangent,
        project_weight,
        output_weight,
        gate_weight,
        up_weight,
        down_weight,
        gains,
        project_bias[None, :],
        cosine,
        sine,
        start_window,
    )
    gain_one = gains_full[:, 0:1]
    gain_two = gains_full[:, 1:2]
    x = x_low.astype(F32)
    first_rate = lax.rsqrt(jnp.mean(x * x, axis=(0, 2))[None, :, None] + EPS)
    second_rate = lax.rsqrt(jnp.mean(middle * middle, axis=(0, 2))[None, :, None] + EPS)
    key_at = jnp.arange(window, dtype=jnp.int32)[None, :]
    allowed = (key_at >= start_window) & (
        key_at <= MAXLEN + jnp.arange(SHARE, dtype=jnp.int32)[:, None]
    )
    pairs = jnp.concatenate([kv[0, :, :64], kv[1, :, :64]], axis=1)
    log_total = lse
    queries = (
        (queries[:, :query_width].astype(F32) * 8.0)
        .astype(BF)
        .reshape(SHARE, group_heads, HEAD_DIM)
    )
    cosine = cosine[:, :half]
    sine = -sine[:, :half]

    grad_second, block_output, ff_grads = feed_forward(
        normed_second, cot_all, gate_full, up_full, down_full, middle
    )

    cot_own = lax.dynamic_slice_in_dim(cot_all, r * SHARE, SHARE, 1).astype(F32)
    weighted_second = grad_second * gain_two
    second_inner = jnp.sum(weighted_second * middle, axis=(0, 2))[None, :, None]
    second_gain_grad = jnp.sum(grad_second * middle * second_rate, axis=1)
    grad_middle = (
        cot_own
        + second_rate * weighted_second
        - middle * (second_rate**3 * second_inner / D)
    )
    grad_branch = grad_middle.astype(BF)
    grad_attended = (
        jnp.einsum("jtf,jhf->th", grad_branch, output_full, preferred_element_type=F32)
        .astype(BF)
        .reshape(SHARE, group_heads, HEAD_DIM)
    )
    grad_queries, grad_pairs = attend_backward(
        queries, pairs, allowed, log_total, grad_attended
    )
    grad_wide = lax.dynamic_update_slice(
        jnp.zeros((MAXLEN + SHARD, 2 * HEAD_DIM), F32), grad_pairs, (r * SHARE, 0)
    )
    returned = from_behind(grad_wide[:MAXLEN].astype(BF), "dp", -1)
    own_pairs = (grad_wide[MAXLEN:] + returned.astype(F32)).astype(BF)
    grad_pair = lax.psum_scatter(
        own_pairs, "row", scatter_dimension=0, tiled=True
    ).astype(F32)
    grad_keys = rotate(grad_pair[:, :HEAD_DIM], cosine, -sine)
    grad_query_plain = rotate(grad_queries, cosine, -sine).reshape(SHARE, query_width)
    grad_projected = jnp.concatenate(
        [grad_query_plain, grad_keys, grad_pair[:, HEAD_DIM:]], axis=1
    ).astype(BF)
    grad_first = col_sum(
        jnp.einsum("tn,jfn->jtf", grad_projected, project_full, preferred_element_type=F32)
    )
    weighted_first = grad_first * gain_one
    first_inner = jnp.sum(weighted_first * x, axis=(0, 2))[None, :, None]
    first_gain_grad = jnp.sum(grad_first * x * first_rate, axis=1)
    input_own = (
        grad_middle
        + first_rate * weighted_first
        - x * (first_rate**3 * first_inner / D)
    )
    input_grad = exchange(input_own.astype(BF)).reshape(SHARD, FEAT).astype(F32)

    ff_sum = sum_grads(ff_grads, True, 2)[:, :FEAT].astype(F32)
    width = project_weight.shape[1]
    at_grads = jnp.concatenate(
        [
            jnp.einsum("jtf,tn->jfn", normed_first, grad_projected, preferred_element_type=F32),
            jnp.einsum("jtf,th->jfh", grad_branch, attended, preferred_element_type=F32),
        ],
        axis=2,
    ).astype(BF)
    bias_grad = jnp.sum(grad_projected.astype(F32), axis=0)
    extra = jnp.stack(
        [
            jnp.broadcast_to(jnp.pad(bias_grad, (0, 1024 - width)), (4, 1024)),
            jnp.pad(first_gain_grad, ((0, 0), (0, 1024 - FEAT))),
            jnp.pad(second_gain_grad, ((0, 0), (0, 1024 - FEAT))),
        ],
        axis=1,
    ).astype(BF)
    extra = jnp.pad(extra, ((0, 0), (0, PADF - FEAT - 3), (0, 0)))
    at_grads = jnp.concatenate([at_grads, extra], axis=1)
    at_sum = sum_grads(at_grads[None], False, 3)[0].astype(F32)
    bias_grad = at_sum[FEAT, :width]
    first_gain_grad = at_sum[FEAT + 1, :FEAT]
    second_gain_grad = at_sum[FEAT + 2, :FEAT]
    at_sum = at_sum[:FEAT]
    return (
        block_output,
        input_grad,
        first_gain_grad,
        at_sum[:, :width],
        bias_grad,
        at_sum[:, width:].T,
        second_gain_grad,
        ff_sum[0],
        ff_sum[1],
        ff_sum[2].T,
    )


def solution(mesh):
    return jax.shard_map(
        body,
        mesh=mesh,
        in_specs=(
            P("dp", "row"),
            P("dp"),
            P("row"),
            P("row", "col"),
            P("col"),
            P("col", "row"),
            P("row"),
            P("row", "col"),
            P("row", "col"),
            P("col", "row"),
            P("dp", "row"),
        ),
        out_specs=(
            P("dp", "row"),
            P("dp", "row"),
            P("row"),
            P("row", "col"),
            P("col"),
            P("col", "row"),
            P("row"),
            P("row", "col"),
            P("row", "col"),
            P("col", "row"),
        ),
        check_vma=False,
    )
```

```python
import functools

import jax
import jax.numpy as jnp
from jax import lax
from jax.experimental import pallas as pl
from jax.experimental.pallas import tpu as pltpu
from jax.sharding import PartitionSpec as P

D = 896
HEADS = 14
GROUPS = 2
HEAD_DIM = 64
MAXLEN = 1024
EPS = 1e-06
BF = jnp.bfloat16
F32 = jnp.float32
ROWS = 4
FEAT = 224
SHARE = 256
SHARD = 1024
HALF_FF = 2432
WIN = 640
LAST = HALF_FF - WIN
PADF = 256
VMEM_LIMIT = 60 * 1024 * 1024


def dot(a, b):
    return jnp.dot(a, b, preferred_element_type=F32)


def dot_nt(a, b):
    return lax.dot_general(a, b, (((1,), (1,)), ((), ())), preferred_element_type=F32)


def dot_tn(a, b):
    return lax.dot_general(a, b, (((0,), (0,)), ((), ())), preferred_element_type=F32)


def rcopy(src, dst, send, recv, **device):
    return pltpu.make_async_remote_copy(
        src_ref=src,
        dst_ref=dst,
        send_sem=send,
        recv_sem=recv,
        device_id=device,
        device_id_type=pl.DeviceIdType.MESH,
    )


def greet(peers):
    barrier = pltpu.get_barrier_semaphore()
    for peer in peers:
        pl.semaphore_signal(
            barrier, inc=1, device_id=peer, device_id_type=pl.DeviceIdType.MESH
        )
    pl.semaphore_wait(barrier, len(peers))


def vmem_call(kernel, inputs, outs, scratch, collective, cost=None):
    return pl.pallas_call(
        kernel,
        out_shape=outs,
        in_specs=[pl.BlockSpec(memory_space=pltpu.VMEM)] * inputs,
        out_specs=jax.tree.map(lambda _: pl.BlockSpec(memory_space=pltpu.VMEM), outs),
        scratch_shapes=scratch,
        compiler_params=pltpu.CompilerParams(
            collective_id=collective,
            has_side_effects=True,
            vmem_limit_bytes=VMEM_LIMIT,
        ),
        cost_estimate=cost,
    )


def ffn_kernel(
    ns_ref,
    cot_ref,
    gate_ref,
    up_ref,
    down_ref,
    mid_ref,
    second_ref,
    block_ref,
    grads_ref,
    ns_all,
    hid,
    gg,
    gu,
    sp_send,
    sp_in,
    op_send,
    op_in,
    cs_send,
    cs_in,
    co_send,
    co_in,
    sem_ag,
    sem_sp,
    sem_op,
    sem_cs,
    sem_co,
):
    r = lax.axis_index("row")
    c = lax.axis_index("col")
    greet([{"row": lax.rem(r + k, 4)} for k in (1, 2, 3)] + [{"col": 1 - c}])
    pending = []

    def go(*args, **device):
        copy = rcopy(*args, **device)
        copy.start()
        pending.append(copy)
        return copy

    span = lambda q: pl.ds(pl.multiple_of(q * SHARE, SHARE), SHARE)
    incoming = [
        go(
            ns_ref,
            ns_all.at[:, span(r), :],
            sem_ag.at[0, k - 1],
            sem_ag.at[1, k - 1],
            row=lax.rem(r + k, 4),
        )
        for k in (1, 2, 3)
    ]
    ns_all[:, span(r), :] = ns_ref[...]
    back = []
    for k in range(4):
        q = lax.rem(r + 4 - k, 4)
        grad_hidden = dot_nt(cot_ref[0, span(q), :], down_ref[0])
        for j in range(1, 4):
            grad_hidden += dot_nt(cot_ref[j, span(q), :], down_ref[j])
        if k:
            incoming[k - 1].wait_recv()
        gate = dot(ns_all[0, span(q), :], gate_ref[0])
        up = dot(ns_all[0, span(q), :], up_ref[0])
        for j in range(1, 4):
            gate += dot(ns_all[j, span(q), :], gate_ref[j])
            up += dot(ns_all[j, span(q), :], up_ref[j])
        sigma = 1.0 / (1.0 + jnp.exp(-gate))
        silu = gate * sigma
        hid[span(q), :] = (silu * up).astype(BF)
        g_gate = (grad_hidden * up * (sigma + silu * (1.0 - sigma))).astype(BF)
        g_up = (grad_hidden * silu).astype(BF)
        gg[span(q), :] = g_gate
        gu[span(q), :] = g_up
        for j in range(4):
            sp_send[k, j] = (
                dot_nt(g_gate, gate_ref[j]) + dot_nt(g_up, up_ref[j])
            ).astype(BF)
        if k:
            back.append(
                go(
                    sp_send.at[k],
                    sp_in.at[k - 1],
                    sem_sp.at[0, k - 1],
                    sem_sp.at[1, k - 1],
                    row=q,
                )
            )
    outgoing = []
    for k in (1, 2, 3, 0):
        j = lax.rem(r + k, 4)
        for q in range(4):
            op_send[j, q * SHARE : (q + 1) * SHARE, :] = dot(
                hid[q * SHARE : (q + 1) * SHARE, :], down_ref[j]
            ).astype(BF)
        op_send[j, span(r), :] = (
            op_send[j, span(r), :].astype(F32) + 0.5 * mid_ref[j]
        ).astype(BF)
        if k:
            outgoing.append(
                go(
                    op_send.at[j],
                    op_in.at[k - 1],
                    sem_op.at[0, k - 1],
                    sem_op.at[1, k - 1],
                    row=j,
                )
            )
    total = sp_send[0].astype(F32)
    for k in (1, 2, 3):
        back[k - 1].wait_recv()
        total += sp_in[k - 1].astype(F32)
    cs_send[...] = total.astype(BF)
    cross = go(cs_send, cs_in, sem_cs.at[0], sem_cs.at[1], col=1 - c)
    grads_ref[:, :, FEAT:PADF, :] = jnp.zeros((3, 4, PADF - FEAT, WIN), BF)
    for j in range(4):
        grads_ref[0, j, 0:FEAT, :] = dot_tn(ns_all[j], gg[...]).astype(BF)
        grads_ref[1, j, 0:FEAT, :] = dot_tn(ns_all[j], gu[...]).astype(BF)
        grads_ref[2, j, 0:FEAT, :] = dot_tn(cot_ref[j], hid[...]).astype(BF)
    total = op_send[r].astype(F32)
    for k in (1, 2, 3):
        outgoing[k - 1].wait_recv()
        total += op_in[k - 1].astype(F32)
    co_send[...] = total.astype(BF)
    final = go(co_send, co_in, sem_co.at[0], sem_co.at[1], col=1 - c)
    cross.wait_recv()
    second_ref[...] = cs_send[...].astype(F32) + cs_in[...].astype(F32)
    final.wait_recv()
    block_ref[...] = (co_send[...].astype(F32) + co_in[...].astype(F32)).astype(BF)
    for copy in pending:
        copy.wait_send()


def feed_forward(ns, cot_all, gate_full, up_full, down_full, middle):
    dma = pltpu.SemaphoreType.DMA
    blocked = pltpu.VMEM((4, SHARE, FEAT), BF)
    return vmem_call(
        ffn_kernel,
        6,
        (
            jax.ShapeDtypeStruct((4, SHARE, FEAT), F32),
            jax.ShapeDtypeStruct((SHARD, FEAT), BF),
            jax.ShapeDtypeStruct((3, 4, PADF, WIN), BF),
        ),
        [
            pltpu.VMEM((4, SHARD, FEAT), BF),
            pltpu.VMEM((SHARD, WIN), BF),
            pltpu.VMEM((SHARD, WIN), BF),
            pltpu.VMEM((SHARD, WIN), BF),
            pltpu.VMEM((4, 4, SHARE, FEAT), BF),
            pltpu.VMEM((3, 4, SHARE, FEAT), BF),
            pltpu.VMEM((4, SHARD, FEAT), BF),
            pltpu.VMEM((3, SHARD, FEAT), BF),
            blocked,
            blocked,
            pltpu.VMEM((SHARD, FEAT), BF),
            pltpu.VMEM((SHARD, FEAT), BF),
            dma((2, 3)),
            dma((2, 3)),
            dma((2, 3)),
            dma((2,)),
            dma((2,)),
        ],
        1,
        pl.CostEstimate(flops=12 * 10**9, bytes_accessed=16 * 10**6, transcendentals=10**6),
    )(ns, cot_all, gate_full, up_full, down_full, middle)


def swapped(values):
    width = values.shape[1]
    lane = lax.broadcasted_iota(jnp.int32, values.shape, 1)
    return jnp.where(
        lax.rem(lane, 64) < 32,
        pltpu.roll(values, width - 32, 1),
        pltpu.roll(values, 32, 1),
    )


def front_kernel(
    act_ref,
    cot_ref,
    proj_ref,
    outw_ref,
    gate_ref,
    up_ref,
    down_ref,
    gains_ref,
    bias_ref,
    cos_ref,
    sin_ref,
    start_ref,
    x_out,
    nf_out,
    q_out,
    kv_out,
    lse_out,
    att_out,
    mid_out,
    ns_out,
    proj_full,
    outw_full,
    gate_full,
    up_full,
    down_full,
    cot_all,
    gains_full,
    mask,
    own_kv,
    c_send,
    c_in,
    sem_x,
    sem_g,
    sem_w,
    sem_wc,
    sem_cot,
    sem_kv,
    sem_c,
    sem_l,
):
    d = lax.axis_index("dp")
    r = lax.axis_index("row")
    c = lax.axis_index("col")
    core = lax.rem(d, 2)
    sibling = d + 1 - 2 * core
    block = 4 * d + r
    near = lambda i: {
        "dp": lax.rem((block + 64 + i) // 4, 16),
        "row": lax.rem(r + 4 + i, 4),
    }
    greet(
        [{"row": lax.rem(r + k, 4)} for k in (1, 2, 3)]
        + [{"col": 1 - c}, {"dp": sibling}]
        + [near(i) for i in (1, 2, 3, 4, -1, -2, -3, -4)]
    )
    pending = []

    def go(*args, **device):
        copy = rcopy(*args, **device)
        copy.start()
        pending.append(copy)
        return copy

    peers = [(k, lax.rem(r + k, 4)) for k in (1, 2, 3)]
    span = lambda q: pl.ds(pl.multiple_of(q * SHARE, SHARE), SHARE)
    offset = lambda q: pl.multiple_of(jnp.minimum(q * WIN, LAST), 128)
    half = lambda n: pl.ds(pl.multiple_of(core * n, 16), n)

    def down_rows(q):
        return pl.ds(pl.multiple_of(offset(q) + core * (WIN // 2), 16), WIN // 2)

    pieces = (
        (lambda q: proj_ref.at[half(112), :], proj_full, 112),
        (lambda q: outw_ref.at[half(224), :], outw_full, 224),
        (lambda q: gate_ref.at[half(112), pl.ds(offset(q), WIN)], gate_full, 112),
        (lambda q: up_ref.at[half(112), pl.ds(offset(q), WIN)], up_full, 112),
        (lambda q: down_ref.at[down_rows(q), :], down_full, WIN // 2),
    )

    def fetch(w):
        source, full, n = pieces[w]
        copies = [
            go(
                source(q),
                full.at[r, half(n), :],
                sem_w.at[0, w, k - 1],
                sem_w.at[1, w, k - 1],
                row=q,
            )
            for k, q in peers
        ]
        local = pltpu.make_async_copy(source(r), full.at[r, half(n), :], sem_l.at[w])
        local.start()
        return copies, local

    def share(w, fetched):
        _, full, n = pieces[w]
        copies, local = fetched
        local.wait()
        for copy in copies:
            copy.wait_recv()
        part = full.at[:, half(n), :]
        return go(part, part, sem_wc.at[0, w], sem_wc.at[1, w], dp=sibling)

    x_copies = [
        go(
            act_ref.at[span(q), :],
            x_out.at[r],
            sem_x.at[0, k - 1],
            sem_x.at[1, k - 1],
            row=q,
        )
        for k, q in peers
    ]
    g_copies = [
        go(gains_ref, gains_full.at[r], sem_g.at[0, k - 1], sem_g.at[1, k - 1], row=q)
        for k, q in peers
    ]
    fetched = {0: fetch(0)}
    x_out[r] = act_ref[span(r), :]
    gains_full[r] = gains_ref[...]
    query_at = lax.broadcasted_iota(jnp.int32, (SHARE, 1), 0) + MAXLEN
    key_at = lax.broadcasted_iota(jnp.int32, (SHARE, MAXLEN + SHARE), 1)
    mask[...] = jnp.where(
        (key_at >= start_ref[...]) & (key_at <= query_at), 0.0, -1e30
    )
    shared = {0: share(0, fetched[0])}
    for copy in x_copies + g_copies:
        copy.wait_recv()
    for w in (1, 2, 3, 4):
        fetched[w] = fetch(w)
    cot_copies = [
        go(cot_ref, cot_all.at[r], sem_cot.at[0, k - 1], sem_cot.at[1, k - 1], row=q)
        for k, q in peers
    ]
    cot_all[r] = cot_ref[...]
    square = jnp.zeros((SHARE, 1), F32)
    for j in range(4):
        value = x_out[j].astype(F32)
        square += jnp.sum(value * value, axis=1, keepdims=True)
    rate = lax.rsqrt(square / D + EPS)
    for j in range(4):
        nf_out[j] = (x_out[j].astype(F32) * rate * gains_full[j, 0:1, :]).astype(BF)
    shared[0].wait_recv()
    projected = dot(nf_out[0], proj_full[0, :, 0:512])
    values = dot(nf_out[0], proj_full[0, :, 512:576])
    for j in range(1, 4):
        projected += dot(nf_out[j], proj_full[j, :, 0:512])
        values += dot(nf_out[j], proj_full[j, :, 512:576])
    projected += bias_ref[:, 0:512]
    values = (values + bias_ref[:, 512:576]).astype(BF)
    cosine = jnp.concatenate([cos_ref[...]] * 4, axis=1)
    sine = jnp.concatenate([sin_ref[...]] * 4, axis=1)
    turned = projected * cosine + swapped(projected) * sine
    q_out[...] = (turned * HEAD_DIM ** (-0.5)).astype(BF)
    tile = turned[:, 384:512]
    lane = lax.broadcasted_iota(jnp.int32, (SHARE, 128), 1)
    low = lane < 64
    own_kv[0] = jnp.where(low, pltpu.roll(tile, 64, 1), tile).astype(BF)
    double = (
        lax.rem(lax.broadcasted_iota(jnp.int32, (64, 128), 1), 64)
        == lax.broadcasted_iota(jnp.int32, (64, 128), 0)
    ).astype(F32).astype(BF)
    own_kv[1] = dot(values, double).astype(BF)
    kv_copies = [
        go(
            own_kv,
            kv_out.at[:, (4 - i) * SHARE : (5 - i) * SHARE, :],
            sem_kv.at[0, i - 1],
            sem_kv.at[1, i - 1],
            **near(i),
        )
        for i in (1, 2, 3, 4)
    ]
    kv_out[:, MAXLEN : MAXLEN + SHARE, :] = own_kv[...]
    for copy in kv_copies:
        copy.wait_recv()
    for m in range(HEADS // GROUPS):
        at = 128 * (m // 2)
        mine = low if m % 2 == 0 else jnp.logical_not(low)
        query = jnp.where(mine, q_out[:, at : at + 128].astype(F32), 0.0).astype(BF)
        scores = dot_nt(query, kv_out[0]) + mask[...]
        peak = jnp.max(scores, axis=1, keepdims=True)
        powered = jnp.exp(scores - peak)
        total = jnp.sum(powered, axis=1, keepdims=True)
        probs = (powered * (1.0 / total)).astype(BF)
        lse_out[m] = peak + jnp.log(total)
        mixed = dot(probs, kv_out[1])
        if m == 6:
            att_out[:, 384:448] = mixed[:, 0:64].astype(BF)
        elif m % 2 == 0:
            even = mixed
        else:
            att_out[:, at : at + 128] = jnp.where(low, even, mixed).astype(BF)
    shared[1] = share(1, fetched[1])
    shared[1].wait_recv()
    for j in range(4):
        c_send[j] = dot(att_out[...], outw_full[j]).astype(BF)
    cross = go(c_send, c_in, sem_c.at[0], sem_c.at[1], col=1 - c)
    for w in (2, 3, 4):
        shared[w] = share(w, fetched[w])
    cross.wait_recv()
    square = jnp.zeros((SHARE, 1), F32)
    for j in range(4):
        value = x_out[j].astype(F32) + (
            c_send[j].astype(F32) + c_in[j].astype(F32)
        )
        mid_out[j] = value
        square += jnp.sum(value * value, axis=1, keepdims=True)
    rate = lax.rsqrt(square / D + EPS)
    for j in range(4):
        ns_out[j] = (mid_out[j] * rate * gains_full[j, 1:2, :]).astype(BF)
    for copy in cot_copies:
        copy.wait_recv()
    for w in (2, 3, 4):
        shared[w].wait_recv()
    for copy in pending:
        copy.wait_send()
    live = jnp.where(r < 3, 1.0, 0.0)
    for j in range(4):
        extra = 4 * WIN - HALF_FF
        gate_full[j, :, 0:extra] = (gate_full[j, :, 0:extra].astype(F32) * live).astype(BF)
        up_full[j, :, 0:extra] = (up_full[j, :, 0:extra].astype(F32) * live).astype(BF)


def front(*operands):
    dma = pltpu.SemaphoreType.DMA
    shape = jax.ShapeDtypeStruct
    width = MAXLEN + SHARE
    blocked = pltpu.VMEM((4, SHARE, FEAT), BF)
    return vmem_call(
        front_kernel,
        12,
        (
            shape((4, SHARE, FEAT), BF),
            shape((4, SHARE, FEAT), BF),
            shape((SHARE, 512), BF),
            shape((2, width, 128), BF),
            shape((HEADS // GROUPS, SHARE, 1), F32),
            shape((SHARE, 448), BF),
            shape((4, SHARE, FEAT), F32),
            shape((4, SHARE, FEAT), BF),
            shape((4, FEAT, 576), BF),
            shape((4, 448, FEAT), BF),
            shape((4, FEAT, WIN), BF),
            shape((4, FEAT, WIN), BF),
            shape((4, WIN, FEAT), BF),
            shape((4, SHARD, FEAT), BF),
            shape((4, 8, FEAT), F32),
        ),
        [
            pltpu.VMEM((SHARE, width), F32),
            pltpu.VMEM((2, SHARE, 128), BF),
            blocked,
            blocked,
            dma((2, 3)),
            dma((2, 3)),
            dma((2, 5, 3)),
            dma((2, 5)),
            dma((2, 3)),
            dma((2, 4)),
            dma((2,)),
            dma((5,)),
        ],
        0,
    )(*operands)


class GradSum:
    def __init__(self, t, source, out, joined, wide_first, place, buffers, sems, go):
        self.t, self.source, self.out, self.joined, self.go = t, source, out, joined, go
        self.r, d = place
        self.core = lax.rem(d, 2)
        y = lax.rem(d // 2, 2)
        x = d // 4
        self.sibling = d + 1 - 2 * self.core
        along_x = [
            (k, lax.rem(x + k, 4), lax.rem(x + k, 4) * 4 + lax.rem(d, 4)) for k in (1, 2, 3)
        ]
        along_y = [(1, 1 - y, d + 2 - 4 * y)]
        if wide_first:
            self.first, self.second = (along_x, x, 32), (along_y, y, 16)
        else:
            self.first, self.second = (along_y, y, 64), (along_x, x, 16)
        self.at_first = self.core * 128 + self.first[1] * self.first[2]
        self.at = self.at_first + self.second[1] * 16
        self.core_in, self.part, self.low, self.in1, self.low2, self.in2, self.mine, self.z_in = [
            buffer.at[t] for buffer in buffers
        ]
        self.sem = lambda stage, k: (sems.at[0, t, stage, k - 1], sems.at[1, t, stage, k - 1])
        self.waiting = []
        self.done = 0

    def rows(self, start, size):
        return pl.ds(pl.multiple_of(start, 16), size)

    def settle(self):
        for copy in self.waiting:
            copy.wait_recv()
        self.waiting = []

    def send(self, source, target, stage, k, **device):
        self.waiting.append(self.go(source, target, *self.sem(stage, k), **device))

    def step(self):
        self.settle()
        getattr(self, "step%d" % self.done)()
        self.done += 1

    def step0(self):
        self.send(
            self.source.at[:, self.rows((1 - self.core) * 128, 128), :],
            self.core_in,
            0,
            1,
            dp=self.sibling,
        )

    def step1(self):
        peers, own, unit = self.first
        total = self.source[:, self.rows(self.core * 128, 128), :].astype(F32)
        total = total + self.core_in[...].astype(F32)
        self.part[...] = total
        self.low[...] = total.astype(BF)
        for k, index, device in peers:
            self.send(
                self.low.at[:, self.rows(index * unit, unit), :],
                self.in1.at[:, (k - 1) * unit : k * unit, :],
                1,
                k,
                dp=device,
            )

    def step2(self):
        peers, own, unit = self.first
        total = self.part[:, self.rows(own * unit, unit), :]
        for k, _, _ in peers:
            total = total + self.in1[:, (k - 1) * unit : k * unit, :].astype(F32)
        self.part[:, 0:unit, :] = total
        self.low2[:, 0:unit, :] = total.astype(BF)
        peers, own, unit = self.second
        for k, index, device in peers:
            self.send(
                self.low2.at[:, self.rows(index * unit, unit), :],
                self.in2.at[:, (k - 1) * unit : k * unit, :],
                2,
                k,
                dp=device,
            )

    def step3(self):
        peers, own, unit = self.second
        total = self.part[:, self.rows(own * unit, unit), :]
        for k, _, _ in peers:
            total = total + self.in2[:, (k - 1) * unit : k * unit, :].astype(F32)
        self.mine[...] = total.astype(BF)
        for k in (1, 2, 3):
            q = lax.rem(self.r + k, 4)
            self.send(self.mine.at[q], self.z_in.at[self.r], 3, k, row=q)
        self.z_in[self.r] = self.mine[self.r]

    def step4(self):
        here = self.rows(self.at, 16)
        if self.joined:
            for q in range(3):
                self.out[here, q * WIN : (q + 1) * WIN] = self.z_in[q]
            self.out[here, 3 * WIN : HALF_FF] = self.z_in[3][:, 4 * WIN - HALF_FF :]
        else:
            total = self.z_in[0].astype(F32)
            for q in range(1, 4):
                total = total + self.z_in[q].astype(F32)
            self.out[here, :] = total.astype(BF)
        self.spread(self.second[0], self.at, 16, 4)

    def spread(self, peers, start, size, stage):
        block = self.out.at[self.rows(start, size), :]
        for k, _, device in peers:
            self.send(block, block, stage, k, dp=device)

    def step5(self):
        self.spread(self.first[0], self.at_first, self.first[2], 5)

    def step6(self):
        self.spread([(1, 0, self.sibling)], self.core * 128, 128, 6)

    def step7(self):
        pass


def back_kernel(
    second_ref,
    mid_ref,
    cot_ref,
    x_ref,
    nf_ref,
    q_ref,
    kv_ref,
    lse_ref,
    att_ref,
    proj_full,
    outw_full,
    gains_full,
    cos_ref,
    sin_ref,
    start_ref,
    ff_ref,
    input_out,
    ff_out,
    outw_out,
    proj_out,
    small_out,
    mask,
    g_mid,
    g_branch,
    g_att,
    dq,
    dk,
    dv,
    dkv,
    dkv_in,
    gp,
    gv,
    c_send,
    c_in,
    own_input,
    outw_grad,
    proj_grad,
    small,
    small_in,
    small_x,
    small_z,
    core_in,
    part,
    low_buf,
    in1,
    low2,
    in2,
    mine,
    z_in,
    sem_flow,
    sem_kv,
    sem_c,
    sem_in,
    sem_s,
):
    d = lax.axis_index("dp")
    r = lax.axis_index("row")
    c = lax.axis_index("col")
    core = lax.rem(d, 2)
    y = lax.rem(d // 2, 2)
    x = d // 4
    sibling = d + 1 - 2 * core
    other_y = d + 2 - 4 * y
    x_peers = [(k, lax.rem(x + k, 4) * 4 + lax.rem(d, 4)) for k in (1, 2, 3)]
    row_peers = [(k, lax.rem(r + k, 4)) for k in (1, 2, 3)]
    block = 4 * d + r
    near = lambda i: {
        "dp": lax.rem((block + 64 + i) // 4, 16),
        "row": lax.rem(r + 4 + i, 4),
    }
    greet(
        [{"row": q} for _, q in row_peers]
        + [{"dp": p} for _, p in x_peers]
        + [{"col": 1 - c}, {"dp": sibling}, {"dp": other_y}]
        + [near(i) for i in (1, 2, 3, 4, -1, -2, -3, -4)]
    )
    pending = []

    def go(*args, **device):
        copy = rcopy(*args, **device)
        copy.start()
        pending.append(copy)
        return copy

    span = lambda q: pl.ds(pl.multiple_of(q * SHARE, SHARE), SHARE)
    buffers = (core_in, part, low_buf, in1, low2, in2, mine, z_in)
    flows = [
        GradSum(t, source, out, joined, wide_first, (r, d), buffers, sem_flow, go)
        for t, source, out, joined, wide_first in (
            (0, ff_ref.at[0], ff_out.at[0], True, True),
            (1, ff_ref.at[1], ff_out.at[1], True, False),
            (2, ff_ref.at[2], ff_out.at[2], True, True),
            (3, outw_grad, outw_out, False, False),
            (4, proj_grad, proj_out, False, True),
        )
    ]
    early, tail = flows[:4], flows[4]
    for flow in early[:3]:
        flow.step()

    small[...] = jnp.zeros_like(small)
    square = jnp.zeros((SHARE, 1), F32)
    inner = jnp.zeros((SHARE, 1), F32)
    for j in range(4):
        value = mid_ref[j]
        square += jnp.sum(value * value, axis=1, keepdims=True)
        inner += jnp.sum(second_ref[j] * gains_full[j, 1:2, :] * value, axis=1, keepdims=True)
    rate = lax.rsqrt(square / D + EPS)
    scale = rate * rate * rate * inner / D
    for j in range(4):
        value = mid_ref[j]
        grad = second_ref[j]
        small[j, 1:2, 0:FEAT] = jnp.sum(grad * value * rate, axis=0, keepdims=True)
        total = (
            cot_ref[j, span(r), :].astype(F32)
            + rate * (grad * gains_full[j, 1:2, :])
            - value * scale
        )
        g_mid[j] = total
        g_branch[j] = total.astype(BF)
    grad_att = dot_nt(g_branch[0], outw_full[0])
    for j in range(1, 4):
        grad_att += dot_nt(g_branch[j], outw_full[j])
    g_att[:, 448:512] = jnp.zeros((SHARE, 64), BF)
    g_att[:, 0:448] = grad_att.astype(BF)
    for flow in early[:3]:
        flow.step()
    outw_grad[...] = jnp.zeros_like(outw_grad)
    for j in range(4):
        outw_grad[j, 0:FEAT, 0:448] = dot_tn(g_branch[j], att_ref[...]).astype(BF)
    early[3].step()
    query_at = lax.broadcasted_iota(jnp.int32, (SHARE, 1), 0) + MAXLEN
    key_at = lax.broadcasted_iota(jnp.int32, (SHARE, MAXLEN + SHARE), 1)
    mask[...] = jnp.where(
        (key_at >= start_ref[...]) & (key_at <= query_at), 0.0, -1e30
    )

    lane = lax.broadcasted_iota(jnp.int32, (SHARE, 128), 1)
    low = lane < 64
    for m in range(HEADS // GROUPS):
        at = 128 * (m // 2)
        mine_lanes = low if m % 2 == 0 else jnp.logical_not(low)
        pick = lambda ref: jnp.where(
            mine_lanes, ref[:, at : at + 128].astype(F32), 0.0
        ).astype(BF)
        query, grad = pick(q_ref), pick(g_att)
        probs = jnp.exp(dot_nt(query, kv_ref[0]) + mask[...] - lse_ref[m])
        grad_probs = dot_nt(grad, kv_ref[1])
        inner = jnp.sum(probs * grad_probs, axis=1, keepdims=True)
        grad_scores = (probs * (grad_probs - inner)).astype(BF)
        grad_v = dot_tn(probs.astype(BF), grad)
        grad_k = dot_tn(grad_scores, query)
        if m == 0:
            dv[...] = grad_v
            dk[...] = grad_k
        else:
            dv[...] += grad_v
            dk[...] += grad_k
        grad_q = dot(grad_scores, kv_ref[0]) * HEAD_DIM ** (-0.5)
        if m % 2 == 0:
            dq[:, at : at + 128] = grad_q
        else:
            dq[:, at : at + 128] = jnp.where(low, dq[:, at : at + 128], grad_q)
        if m == 1:
            early[3].step()
    wide_low = lax.broadcasted_iota(jnp.int32, (MAXLEN + SHARE, 128), 1) < 64
    dkv[...] = jnp.where(
        wide_low,
        dk[...] + pltpu.roll(dk[...], 64, 1),
        dv[...] + pltpu.roll(dv[...], 64, 1),
    ).astype(BF)
    kv_copies = [
        go(
            dkv.at[(4 - i) * SHARE : (5 - i) * SHARE, :],
            dkv_in.at[i - 1],
            sem_kv.at[0, i - 1],
            sem_kv.at[1, i - 1],
            **near(-i),
        )
        for i in (1, 2, 3, 4)
    ]
    for flow in early:
        flow.step()
    total = dkv[MAXLEN : MAXLEN + SHARE, :].astype(F32)
    for i in (1, 2, 3, 4):
        kv_copies[i - 1].wait_recv()
        total += dkv_in[i - 1].astype(F32)
    turned = pltpu.roll(total, 64, 1)
    dq[:, 384:512] = jnp.where(low, dq[:, 384:512], turned)
    gv[...] = turned[:, 0:64].astype(BF)
    cosine = jnp.concatenate([cos_ref[...]] * 4, axis=1)
    sine = jnp.concatenate([sin_ref[...]] * 4, axis=1)
    gp[...] = (dq[...] * cosine - swapped(dq[...]) * sine).astype(BF)
    for j in range(4):
        c_send[j] = (
            dot_nt(gp[...], proj_full[j, :, 0:512])
            + dot_nt(gv[...], proj_full[j, :, 512:576])
        ).astype(BF)
    cross = go(c_send, c_in, sem_c.at[0], sem_c.at[1], col=1 - c)
    proj_grad[...] = jnp.zeros_like(proj_grad)
    for j in range(4):
        proj_grad[j, 0:FEAT, 0:512] = dot_tn(nf_ref[j], gp[...]).astype(BF)
        proj_grad[j, 0:FEAT, 512:576] = dot_tn(nf_ref[j], gv[...]).astype(BF)
    tail.step()
    bias_a = jnp.sum(gp[...].astype(F32), axis=0, keepdims=True)
    bias_b = jnp.sum(gv[...].astype(F32), axis=0, keepdims=True)
    for j in range(4):
        small[j, 2:3, 0:512] = bias_a
        small[j, 2:3, 512:576] = bias_b
    for flow in early:
        flow.step()
    tail.step()

    square = jnp.zeros((SHARE, 1), F32)
    for j in range(4):
        value = x_ref[j].astype(F32)
        square += jnp.sum(value * value, axis=1, keepdims=True)
    rate = lax.rsqrt(square / D + EPS)
    cross.wait_recv()
    inner = jnp.zeros((SHARE, 1), F32)
    for j in range(4):
        grad = c_send[j].astype(F32) + c_in[j].astype(F32)
        inner += jnp.sum(
            grad * gains_full[j, 0:1, :] * x_ref[j].astype(F32), axis=1, keepdims=True
        )
    scale = rate * rate * rate * inner / D
    for j in range(4):
        value = x_ref[j].astype(F32)
        grad = c_send[j].astype(F32) + c_in[j].astype(F32)
        small[j, 0:1, 0:FEAT] = jnp.sum(grad * value * rate, axis=0, keepdims=True)
        own_input[j] = (
            g_mid[j] + rate * (grad * gains_full[j, 0:1, :]) - value * scale
        ).astype(BF)
    in_copies = [
        go(
            own_input.at[q],
            input_out.at[r],
            sem_in.at[0, k - 1],
            sem_in.at[1, k - 1],
            row=q,
        )
        for k, q in row_peers
    ]
    input_out[r] = own_input[r]

    def swap(stage, source, target, k, **device):
        return go(source, target, sem_s.at[0, stage, k - 1], sem_s.at[1, stage, k - 1], **device)

    copy = swap(0, small, small_in.at[0], 1, dp=sibling)
    for flow in early:
        flow.step()
    tail.step()
    copy.wait_recv()
    small_x[0] = small[...] + small_in[0]
    copies = [swap(1, small_x.at[0], small_in.at[k], k, dp=p) for k, p in x_peers]
    for flow in early:
        flow.step()
    tail.step()
    for copy in copies:
        copy.wait_recv()
    small_x[1] = small_x[0] + small_in[1] + small_in[2] + small_in[3]
    copy = swap(2, small_x.at[1], small_in.at[4], 1, dp=other_y)
    tail.step()
    copy.wait_recv()
    small_x[2] = small_x[1] + small_in[4]
    copies = [swap(3, small_x.at[2, q], small_z.at[r], k, row=q) for k, q in row_peers]
    small_z[r] = small_x[2, r]
    tail.step()
    for flow in early:
        flow.step()
    for copy in copies:
        copy.wait_recv()
    small_out[...] = small_z[0] + small_z[1] + small_z[2] + small_z[3]
    tail.step()
    for flow in early:
        flow.step()
    tail.step()
    for copy in in_copies:
        copy.wait_recv()
    for copy in pending:
        copy.wait_send()


def back(*operands):
    dma = pltpu.SemaphoreType.DMA
    shape = jax.ShapeDtypeStruct
    width = MAXLEN + SHARE
    blocked = pltpu.VMEM((4, SHARE, FEAT), BF)
    count = 5
    return vmem_call(
        back_kernel,
        16,
        (
            shape((4, SHARE, FEAT), BF),
            shape((3, PADF, HALF_FF), BF),
            shape((PADF, WIN), BF),
            shape((PADF, WIN), BF),
            shape((8, WIN), F32),
        ),
        [
            pltpu.VMEM((SHARE, width), F32),
            pltpu.VMEM((4, SHARE, FEAT), F32),
            blocked,
            pltpu.VMEM((SHARE, 512), BF),
            pltpu.VMEM((SHARE, 512), F32),
            pltpu.VMEM((width, 128), F32),
            pltpu.VMEM((width, 128), F32),
            pltpu.VMEM((width, 128), BF),
            pltpu.VMEM((4, SHARE, 128), BF),
            pltpu.VMEM((SHARE, 512), BF),
            pltpu.VMEM((SHARE, 64), BF),
            blocked,
            blocked,
            blocked,
            pltpu.VMEM((4, PADF, WIN), BF),
            pltpu.VMEM((4, PADF, WIN), BF),
            pltpu.VMEM((4, 8, WIN), F32),
            pltpu.VMEM((5, 4, 8, WIN), F32),
            pltpu.VMEM((3, 4, 8, WIN), F32),
            pltpu.VMEM((4, 8, WIN), F32),
            pltpu.VMEM((count, 4, 128, WIN), BF),
            pltpu.VMEM((count, 4, 128, WIN), F32),
            pltpu.VMEM((count, 4, 128, WIN), BF),
            pltpu.VMEM((count, 4, 96, WIN), BF),
            pltpu.VMEM((count, 4, 64, WIN), BF),
            pltpu.VMEM((count, 4, 48, WIN), BF),
            pltpu.VMEM((count, 4, 16, WIN), BF),
            pltpu.VMEM((count, 4, 16, WIN), BF),
            dma((2, count, 7, 3)),
            dma((2, 4)),
            dma((2,)),
            dma((2, 3)),
            dma((2, 4, 3)),
        ],
        2,
    )(*operands)


def body(
    activations,
    starts,
    first_gain,
    project_weight,
    project_bias,
    output_weight,
    second_gain,
    gate_weight,
    up_weight,
    down_weight,
    cotangent,
):
    r = lax.axis_index("row")
    shard = lax.axis_index("dp")
    query_width = HEADS // GROUPS * HEAD_DIM

    base = shard * SHARD + r * SHARE
    start_window = (
        lax.dynamic_slice_in_dim(starts, r * SHARE, SHARE, 0) - base + MAXLEN
    )[:, None]
    positions = (MAXLEN + jnp.arange(SHARE, dtype=jnp.int32))[:, None] - start_window
    half = HEAD_DIM // 2
    freqs = 1000000.0 ** (-jnp.arange(half, dtype=F32) * 2.0 / HEAD_DIM)
    angle = positions.astype(F32) * jnp.tile(freqs, 4)[None, :]
    cosine = jnp.cos(angle)
    sine = jnp.sin(angle) * jnp.tile(jnp.repeat(jnp.array([-1.0, 1.0], F32), half), 2)[None, :]
    gains = jnp.pad(jnp.stack([first_gain, second_gain]), ((0, 6), (0, 0)))
    (
        x_low,
        normed_first,
        queries,
        kv,
        lse,
        attended,
        middle,
        normed_second,
        project_full,
        output_full,
        gate_full,
        up_full,
        down_full,
        cot_all,
        gains_full,
    ) = front(
        activations,
        cotangent,
        project_weight,
        output_weight,
        gate_weight,
        up_weight,
        down_weight,
        gains,
        project_bias[None, :],
        cosine,
        sine,
        start_window,
    )
    grad_second, block_output, ff_grads = feed_forward(
        normed_second, cot_all, gate_full, up_full, down_full, middle
    )

    input_grad, ff_sum, outw_sum, project_sum, small = back(
        grad_second,
        middle,
        cot_all,
        x_low,
        normed_first,
        queries,
        kv,
        lse,
        attended,
        project_full,
        output_full,
        gains_full,
        cosine,
        sine,
        start_window,
        ff_grads,
    )
    width = project_weight.shape[1]
    ff_sum = ff_sum[:, :FEAT].astype(F32)
    return (
        block_output,
        input_grad.reshape(SHARD, FEAT).astype(F32),
        small[0, :FEAT],
        project_sum[:FEAT, :width].astype(F32),
        small[2, :width],
        outw_sum[:FEAT, :query_width].astype(F32).T,
        small[1, :FEAT],
        ff_sum[0],
        ff_sum[1],
        ff_sum[2].T,
    )


def solution(mesh):
    return jax.shard_map(
        body,
        mesh=mesh,
        in_specs=(
            P("dp", "row"),
            P("dp"),
            P("row"),
            P("row", "col"),
            P("col"),
            P("col", "row"),
            P("row"),
            P("row", "col"),
            P("row", "col"),
            P("col", "row"),
            P("dp", "row"),
        ),
        out_specs=(
            P("dp", "row"),
            P("dp", "row"),
            P("row"),
            P("row", "col"),
            P("col"),
            P("col", "row"),
            P("row"),
            P("row", "col"),
            P("row", "col"),
            P("col", "row"),
        ),
        check_vma=False,
    )
```

```python
import functools

import jax
import jax.numpy as jnp
from jax import lax
from jax.experimental import pallas as pl
from jax.experimental.pallas import tpu as pltpu
from jax.sharding import PartitionSpec as P

D = 896
HEADS = 14
GROUPS = 2
HEAD_DIM = 64
MAXLEN = 1024
EPS = 1e-06
BF = jnp.bfloat16
F32 = jnp.float32
ROWS = 4
FEAT = 224
SHARE = 256
SHARD = 1024
HALF_FF = 2432
WIN = 640
LAST = HALF_FF - WIN
PADF = 256
VMEM_LIMIT = 60 * 1024 * 1024


def dot(a, b):
    return jnp.dot(a, b, preferred_element_type=F32)


def dot_nt(a, b):
    return lax.dot_general(a, b, (((1,), (1,)), ((), ())), preferred_element_type=F32)


def dot_tn(a, b):
    return lax.dot_general(a, b, (((0,), (0,)), ((), ())), preferred_element_type=F32)


def rcopy(src, dst, send, recv, **device):
    return pltpu.make_async_remote_copy(
        src_ref=src,
        dst_ref=dst,
        send_sem=send,
        recv_sem=recv,
        device_id=device,
        device_id_type=pl.DeviceIdType.MESH,
    )


def greet(peers):
    barrier = pltpu.get_barrier_semaphore()
    for peer in peers:
        pl.semaphore_signal(
            barrier, inc=1, device_id=peer, device_id_type=pl.DeviceIdType.MESH
        )
    pl.semaphore_wait(barrier, len(peers))


def vmem_call(kernel, inputs, outs, scratch, collective, cost=None):
    return pl.pallas_call(
        kernel,
        out_shape=outs,
        in_specs=[pl.BlockSpec(memory_space=pltpu.VMEM)] * inputs,
        out_specs=jax.tree.map(lambda _: pl.BlockSpec(memory_space=pltpu.VMEM), outs),
        scratch_shapes=scratch,
        compiler_params=pltpu.CompilerParams(
            collective_id=collective,
            has_side_effects=True,
            vmem_limit_bytes=VMEM_LIMIT,
        ),
        cost_estimate=cost,
    )


def swapped(values):
    width = values.shape[1]
    lane = lax.broadcasted_iota(jnp.int32, values.shape, 1)
    return jnp.where(
        lax.rem(lane, 64) < 32,
        pltpu.roll(values, width - 32, 1),
        pltpu.roll(values, 32, 1),
    )


def forward_kernel(
    act_ref,
    cot_ref,
    proj_ref,
    outw_ref,
    gate_ref,
    up_ref,
    down_ref,
    gains_ref,
    bias_ref,
    cos_ref,
    sin_ref,
    start_ref,
    x_out,
    nf_out,
    q_out,
    kv_out,
    lse_out,
    att_out,
    mid_out,
    proj_full,
    outw_full,
    gains_full,
    cot_out,
    second_out,
    op_out,
    grads_out,
    gate_full,
    up_full,
    down_full,
    cot_all,
    mask,
    own_kv,
    c_send,
    c_in,
    second_in,
    ns_all,
    hid,
    gg,
    gu,
    sp_send,
    sp_in,
    sem_x,
    sem_g,
    sem_w,
    sem_wx,
    sem_wc,
    sem_cot,
    sem_kv,
    sem_c,
    sem_ag,
    sem_sp,
    sem_cs,
    sem_l,
):
    d = lax.axis_index("dp")
    r = lax.axis_index("row")
    c = lax.axis_index("col")
    core = lax.rem(d, 2)
    x_at = d // 4
    sibling = d + 1 - 2 * core
    x_peers = [(k, lax.rem(x_at + k, 4) * 4 + lax.rem(d, 4)) for k in (1, 2, 3)]
    block = 4 * d + r
    near = lambda i: {
        "dp": lax.rem((block + 64 + i) // 4, 16),
        "row": lax.rem(r + 4 + i, 4),
    }
    greet(
        [{"row": lax.rem(r + k, 4)} for k in (1, 2, 3)]
        + [{"dp": p} for _, p in x_peers]
        + [{"col": 1 - c}, {"dp": sibling}]
        + [near(i) for i in (1, 2, 3, 4, -1, -2, -3, -4)]
    )
    pending = []

    def go(*args, **device):
        copy = rcopy(*args, **device)
        copy.start()
        pending.append(copy)
        return copy

    peers = [(k, lax.rem(r + k, 4)) for k in (1, 2, 3)]
    span = lambda q: pl.ds(pl.multiple_of(q * SHARE, SHARE), SHARE)
    offset = lambda q: pl.multiple_of(jnp.minimum(q * WIN, LAST), 128)
    half = lambda n: pl.ds(pl.multiple_of(core * n, 16), n)

    def down_rows(q):
        return pl.ds(pl.multiple_of(offset(q) + core * (WIN // 2), 16), WIN // 2)

    pieces = (
        (lambda q: proj_ref.at[half(112), :], proj_full, 112),
        (lambda q: outw_ref.at[half(224), :], outw_full, 224),
        (lambda q: gate_ref.at[half(112), pl.ds(offset(q), WIN)], gate_full, 112),
        (lambda q: up_ref.at[half(112), pl.ds(offset(q), WIN)], up_full, 112),
        (lambda q: down_ref.at[down_rows(q), :], down_full, WIN // 2),
    )

    def crossing(w):
        source, full, n = pieces[w]
        return [
            rcopy(
                source(q),
                full.at[r, half(n), :],
                sem_w.at[0, w, k - 1],
                sem_w.at[1, w, k - 1],
                row=q,
            )
            for k, q in peers
        ]

    def passing(w):
        _, full, n = pieces[w]
        copies = []
        for k, q in peers:
            part = full.at[q, half(n), :]
            for e, device in x_peers:
                copies.append(
                    rcopy(
                        part,
                        part,
                        sem_wx.at[0, w - 2, k - 1, e - 1],
                        sem_wx.at[1, w - 2, k - 1, 0],
                        dp=device,
                    )
                )
        return copies

    def fetch(w):
        source, full, n = pieces[w]
        local = pltpu.make_async_copy(source(r), full.at[r, half(n), :], sem_l.at[w])
        local.start()
        copies = crossing(w)
        if w < 2:
            for copy in copies:
                copy.start()
                pending.append(copy)
        else:

            @pl.when(x_at == w - 2)
            def _():
                for copy in copies:
                    copy.start()

        return copies, local

    def pass_on(w, fetched):
        @pl.when(x_at == w - 2)
        def _():
            for copy in fetched[0]:
                copy.wait_recv()
            for copy in passing(w):
                copy.start()

    def share(w, fetched):
        _, full, n = pieces[w]
        copies, local = fetched
        local.wait()
        if w < 2:
            for copy in copies:
                copy.wait_recv()
        else:

            @pl.when(x_at != w - 2)
            def _():
                for copy in passing(w)[::3]:
                    copy.wait_recv()

        part = full.at[:, half(n), :]
        copy = rcopy(part, part, sem_wc.at[0, w], sem_wc.at[1, w], dp=sibling)
        copy.start()
        if w < 2:
            pending.append(copy)
        return copy

    def finish(w, fetched):
        @pl.when(x_at == w - 2)
        def _():
            for copy in fetched[0] + passing(w):
                copy.wait_send()

    x_copies = [
        go(
            act_ref.at[span(q), :],
            x_out.at[r],
            sem_x.at[0, k - 1],
            sem_x.at[1, k - 1],
            row=q,
        )
        for k, q in peers
    ]
    g_copies = [
        go(gains_ref, gains_full.at[r], sem_g.at[0, k - 1], sem_g.at[1, k - 1], row=q)
        for k, q in peers
    ]
    fetched = {0: fetch(0)}
    x_out[r] = act_ref[span(r), :]
    gains_full[r] = gains_ref[...]
    query_at = lax.broadcasted_iota(jnp.int32, (SHARE, 1), 0) + MAXLEN
    key_at = lax.broadcasted_iota(jnp.int32, (SHARE, MAXLEN + SHARE), 1)
    mask[...] = jnp.where(
        (key_at >= start_ref[...]) & (key_at <= query_at), 0.0, -1e30
    )
    shared = {0: share(0, fetched[0])}
    for copy in x_copies + g_copies:
        copy.wait_recv()
    for w in (1, 2, 3, 4):
        fetched[w] = fetch(w)
    cot_all[r] = cot_ref[...]
    square = jnp.zeros((SHARE, 1), F32)
    for j in range(4):
        value = x_out[j].astype(F32)
        square += jnp.sum(value * value, axis=1, keepdims=True)
    rate = lax.rsqrt(square / D + EPS)
    for j in range(4):
        nf_out[j] = (x_out[j].astype(F32) * rate * gains_full[j, 0:1, :]).astype(BF)
    shared[0].wait_recv()
    projected = dot(nf_out[0], proj_full[0, :, 0:512])
    values = dot(nf_out[0], proj_full[0, :, 512:576])
    for j in range(1, 4):
        projected += dot(nf_out[j], proj_full[j, :, 0:512])
        values += dot(nf_out[j], proj_full[j, :, 512:576])
    projected += bias_ref[:, 0:512]
    values = (values + bias_ref[:, 512:576]).astype(BF)
    cosine = jnp.concatenate([cos_ref[...]] * 4, axis=1)
    sine = jnp.concatenate([sin_ref[...]] * 4, axis=1)
    turned = projected * cosine + swapped(projected) * sine
    q_out[...] = (turned * HEAD_DIM ** (-0.5)).astype(BF)
    tile = turned[:, 384:512]
    lane = lax.broadcasted_iota(jnp.int32, (SHARE, 128), 1)
    low = lane < 64
    own_kv[0] = jnp.where(low, pltpu.roll(tile, 64, 1), tile).astype(BF)
    double = (
        lax.rem(lax.broadcasted_iota(jnp.int32, (64, 128), 1), 64)
        == lax.broadcasted_iota(jnp.int32, (64, 128), 0)
    ).astype(F32).astype(BF)
    own_kv[1] = dot(values, double).astype(BF)
    kv_copies = [
        go(
            own_kv,
            kv_out.at[:, (4 - i) * SHARE : (5 - i) * SHARE, :],
            sem_kv.at[0, i - 1],
            sem_kv.at[1, i - 1],
            **near(i),
        )
        for i in (1, 2, 3, 4)
    ]
    kv_out[:, MAXLEN : MAXLEN + SHARE, :] = own_kv[...]
    for w in (2, 3, 4):
        pass_on(w, fetched[w])
    for copy in kv_copies:
        copy.wait_recv()
    cot_copies = [
        go(cot_ref, cot_all.at[r], sem_cot.at[0, k - 1], sem_cot.at[1, k - 1], row=q)
        for k, q in (peers[0], peers[2], peers[1])
    ]
    for m in range(HEADS // GROUPS):
        at = 128 * (m // 2)
        mine = low if m % 2 == 0 else jnp.logical_not(low)
        query = jnp.where(mine, q_out[:, at : at + 128].astype(F32), 0.0).astype(BF)
        scores = dot_nt(query, kv_out[0]) + mask[...]
        peak = jnp.max(scores, axis=1, keepdims=True)
        powered = jnp.exp(scores - peak)
        total = jnp.sum(powered, axis=1, keepdims=True)
        probs = (powered * (1.0 / total)).astype(BF)
        lse_out[m] = peak + jnp.log(total)
        mixed = dot(probs, kv_out[1])
        if m == 6:
            att_out[:, 384:448] = mixed[:, 0:64].astype(BF)
        elif m % 2 == 0:
            even = mixed
        else:
            att_out[:, at : at + 128] = jnp.where(low, even, mixed).astype(BF)
    shared[1] = share(1, fetched[1])
    shared[1].wait_recv()
    for j in range(4):
        c_send[j] = dot(att_out[...], outw_full[j]).astype(BF)
    cross = rcopy(c_send, c_in, sem_c.at[0], sem_c.at[1], col=1 - c)
    cross.start()
    for w in (2, 3, 4):
        shared[w] = share(w, fetched[w])
    cross.wait_recv()
    square = jnp.zeros((SHARE, 1), F32)
    for j in range(4):
        value = x_out[j].astype(F32) + (
            c_send[j].astype(F32) + c_in[j].astype(F32)
        )
        mid_out[j] = value
        square += jnp.sum(value * value, axis=1, keepdims=True)
    rate = lax.rsqrt(square / D + EPS)
    for j in range(4):
        ns_all[j, span(r), :] = (mid_out[j] * rate * gains_full[j, 1:2, :]).astype(BF)

    right, across, left = [q for _, q in peers]

    def spread(blocks, source, index, q):
        part = ns_all.at[blocks, span(source), :]
        return go(part, part, sem_ag.at[0, index], sem_ag.at[1, index], row=q)

    every, front_half, back_half = pl.ds(0, 4), pl.ds(0, 2), pl.ds(2, 2)
    from_left = spread(every, r, 0, right)
    from_right = spread(every, r, 1, left)
    for copy in cot_copies:
        copy.wait_recv()
    for w in (2, 3, 4):
        shared[w].wait_recv()
        shared[w].wait_send()
        finish(w, fetched[w])
    live = jnp.where(r < 3, 1.0, 0.0)
    extra = 4 * WIN - HALF_FF
    for j in range(4):
        gate_full[j, :, 0:extra] = (gate_full[j, :, 0:extra].astype(F32) * live).astype(BF)
        up_full[j, :, 0:extra] = (up_full[j, :, 0:extra].astype(F32) * live).astype(BF)
        cot_out[j] = cot_all[j, span(r), :]

    def feed(k, q, arrived):
        grad_hidden = dot_nt(cot_all[0, span(q), :], down_full[0])
        for j in range(1, 4):
            grad_hidden += dot_nt(cot_all[j, span(q), :], down_full[j])
        arrived()
        gate = dot(ns_all[0, span(q), :], gate_full[0])
        up = dot(ns_all[0, span(q), :], up_full[0])
        for j in range(1, 4):
            gate += dot(ns_all[j, span(q), :], gate_full[j])
            up += dot(ns_all[j, span(q), :], up_full[j])
        sigma = 1.0 / (1.0 + jnp.exp(-gate))
        silu = gate * sigma
        hid[span(q), :] = (silu * up).astype(BF)
        g_gate = (grad_hidden * up * (sigma + silu * (1.0 - sigma))).astype(BF)
        g_up = (grad_hidden * silu).astype(BF)
        gg[span(q), :] = g_gate
        gu[span(q), :] = g_up
        for j in range(4):
            sp_send[k, j] = (
                dot_nt(g_gate, gate_full[j]) + dot_nt(g_up, up_full[j])
            ).astype(BF)
        if k:
            return go(
                sp_send.at[k],
                sp_in.at[k - 1],
                sem_sp.at[0, k - 1],
                sem_sp.at[1, k - 1],
                row=q,
            )

    forwarded = []

    def neighbours_here():
        from_left.wait_recv()
        forwarded.append(spread(front_half, left, 2, right))
        from_right.wait_recv()
        forwarded.append(spread(back_half, right, 3, left))

    def opposite_here():
        for copy in forwarded:
            copy.wait_recv()

    feed(0, r, lambda: None)
    back = {}
    back[1] = feed(1, right, neighbours_here)
    back[3] = feed(3, left, lambda: None)
    back[2] = feed(2, across, opposite_here)

    grads_out[:, :, FEAT:PADF, :] = jnp.zeros((3, 4, PADF - FEAT, WIN), BF)
    for j in range(4):
        grads_out[0, j, 0:FEAT, :] = dot_tn(ns_all[j], gg[...]).astype(BF)
        grads_out[1, j, 0:FEAT, :] = dot_tn(ns_all[j], gu[...]).astype(BF)
    total = sp_send[0].astype(F32)
    for k in (1, 3, 2):
        back[k].wait_recv()
        total += sp_in[k - 1].astype(F32)
    cross.wait_send()
    c_send[...] = total.astype(BF)
    cross_two = go(c_send, second_in, sem_cs.at[0], sem_cs.at[1], col=1 - c)
    for j in range(4):
        grads_out[2, j, 0:FEAT, :] = dot_tn(cot_all[j], hid[...]).astype(BF)
        for q in range(4):
            op_out[j, q * SHARE : (q + 1) * SHARE, :] = dot(
                hid[q * SHARE : (q + 1) * SHARE, :], down_full[j]
            ).astype(BF)
        op_out[j, span(r), :] = (
            op_out[j, span(r), :].astype(F32) + 0.5 * mid_out[j]
        ).astype(BF)
    cross_two.wait_recv()
    second_out[...] = c_send[...].astype(F32) + second_in[...].astype(F32)
    for copy in pending:
        copy.wait_send()


def forward(*operands):
    dma = pltpu.SemaphoreType.DMA
    shape = jax.ShapeDtypeStruct
    width = MAXLEN + SHARE
    blocked = pltpu.VMEM((4, SHARE, FEAT), BF)
    return vmem_call(
        forward_kernel,
        12,
        (
            shape((4, SHARE, FEAT), BF),
            shape((4, SHARE, FEAT), BF),
            shape((SHARE, 512), BF),
            shape((2, width, 128), BF),
            shape((HEADS // GROUPS, SHARE, 1), F32),
            shape((SHARE, 448), BF),
            shape((4, SHARE, FEAT), F32),
            shape((4, FEAT, 576), BF),
            shape((4, 448, FEAT), BF),
            shape((4, 8, FEAT), F32),
            shape((4, SHARE, FEAT), BF),
            shape((4, SHARE, FEAT), F32),
            shape((4, SHARD, FEAT), BF),
            shape((3, 4, PADF, WIN), BF),
        ),
        [
            pltpu.VMEM((4, FEAT, WIN), BF),
            pltpu.VMEM((4, FEAT, WIN), BF),
            pltpu.VMEM((4, WIN, FEAT), BF),
            pltpu.VMEM((4, SHARD, FEAT), BF),
            pltpu.VMEM((SHARE, width), F32),
            pltpu.VMEM((2, SHARE, 128), BF),
            blocked,
            blocked,
            blocked,
            pltpu.VMEM((4, SHARD, FEAT), BF),
            pltpu.VMEM((SHARD, WIN), BF),
            pltpu.VMEM((SHARD, WIN), BF),
            pltpu.VMEM((SHARD, WIN), BF),
            pltpu.VMEM((4, 4, SHARE, FEAT), BF),
            pltpu.VMEM((3, 4, SHARE, FEAT), BF),
            dma((2, 3)),
            dma((2, 3)),
            dma((2, 5, 3)),
            dma((2, 3, 3, 3)),
            dma((2, 5)),
            dma((2, 3)),
            dma((2, 4)),
            dma((2,)),
            dma((2, 4)),
            dma((2, 3)),
            dma((2,)),
            dma((5,)),
        ],
        0,
    )(*operands)


class GradSum:
    def __init__(self, t, source, out, joined, wide_first, place, buffers, sems, go):
        self.t, self.source, self.out, self.joined, self.go = t, source, out, joined, go
        self.r, d = place
        self.core = lax.rem(d, 2)
        y = lax.rem(d // 2, 2)
        x = d // 4
        self.sibling = d + 1 - 2 * self.core
        along_x = [
            (k, lax.rem(x + k, 4), lax.rem(x + k, 4) * 4 + lax.rem(d, 4)) for k in (1, 2, 3)
        ]
        along_y = [(1, 1 - y, d + 2 - 4 * y)]
        if wide_first:
            self.first, self.second = (along_x, x, 32), (along_y, y, 16)
        else:
            self.first, self.second = (along_y, y, 64), (along_x, x, 16)
        self.at_first = self.core * 128 + self.first[1] * self.first[2]
        self.at = self.at_first + self.second[1] * 16
        self.core_in, self.part, self.low, self.in1, self.low2, self.in2, self.mine, self.z_in = [
            buffer.at[t] for buffer in buffers
        ]
        self.sem = lambda stage, k: (sems.at[0, t, stage, k - 1], sems.at[1, t, stage, k - 1])
        self.waiting = []
        self.done = 0

    def rows(self, start, size):
        return pl.ds(pl.multiple_of(start, 16), size)

    def settle(self):
        for copy in self.waiting:
            copy.wait_recv()
        self.waiting = []

    def send(self, source, target, stage, k, **device):
        self.waiting.append(self.go(source, target, *self.sem(stage, k), **device))

    def step(self):
        self.settle()
        getattr(self, "step%d" % self.done)()
        self.done += 1

    def step0(self):
        self.send(
            self.source.at[:, self.rows((1 - self.core) * 128, 128), :],
            self.core_in,
            0,
            1,
            dp=self.sibling,
        )

    def step1(self):
        peers, own, unit = self.first
        total = self.source[:, self.rows(self.core * 128, 128), :].astype(F32)
        total = total + self.core_in[...].astype(F32)
        self.part[...] = total
        self.low[...] = total.astype(BF)
        for k, index, device in peers:
            self.send(
                self.low.at[:, self.rows(index * unit, unit), :],
                self.in1.at[:, (k - 1) * unit : k * unit, :],
                1,
                k,
                dp=device,
            )

    def step2(self):
        peers, own, unit = self.first
        total = self.part[:, self.rows(own * unit, unit), :]
        for k, _, _ in peers:
            total = total + self.in1[:, (k - 1) * unit : k * unit, :].astype(F32)
        self.part[:, 0:unit, :] = total
        self.low2[:, 0:unit, :] = total.astype(BF)
        peers, own, unit = self.second
        for k, index, device in peers:
            self.send(
                self.low2.at[:, self.rows(index * unit, unit), :],
                self.in2.at[:, (k - 1) * unit : k * unit, :],
                2,
                k,
                dp=device,
            )

    def step3(self):
        peers, own, unit = self.second
        total = self.part[:, self.rows(own * unit, unit), :]
        for k, _, _ in peers:
            total = total + self.in2[:, (k - 1) * unit : k * unit, :].astype(F32)
        self.mine[...] = total.astype(BF)
        for k in (1, 2, 3):
            q = lax.rem(self.r + k, 4)
            self.send(self.mine.at[q], self.z_in.at[self.r], 3, k, row=q)
        self.z_in[self.r] = self.mine[self.r]

    def step4(self):
        here = self.rows(self.at, 16)
        if self.joined:
            for q in range(3):
                self.out[here, q * WIN : (q + 1) * WIN] = self.z_in[q]
            self.out[here, 3 * WIN : HALF_FF] = self.z_in[3][:, 4 * WIN - HALF_FF :]
        else:
            total = self.z_in[0].astype(F32)
            for q in range(1, 4):
                total = total + self.z_in[q].astype(F32)
            self.out[here, :] = total.astype(BF)
        self.spread(self.second[0], self.at, 16, 4)

    def spread(self, peers, start, size, stage):
        block = self.out.at[self.rows(start, size), :]
        for k, _, device in peers:
            self.send(block, block, stage, k, dp=device)

    def step5(self):
        self.spread(self.first[0], self.at_first, self.first[2], 5)

    def step6(self):
        self.spread([(1, 0, self.sibling)], self.core * 128, 128, 6)

    def step7(self):
        pass


def back_kernel(
    second_ref,
    mid_ref,
    cot_ref,
    x_ref,
    nf_ref,
    q_ref,
    kv_ref,
    lse_ref,
    att_ref,
    proj_full,
    outw_full,
    gains_full,
    cos_ref,
    sin_ref,
    start_ref,
    ff_ref,
    op_ref,
    block_out,
    input_out,
    ff_out,
    outw_out,
    proj_out,
    small_out,
    mask,
    g_mid,
    g_branch,
    g_att,
    dq,
    dk,
    dv,
    dkv,
    dkv_in,
    gp,
    gv,
    c_send,
    c_in,
    op_in,
    co_send,
    co_in,
    own_input,
    outw_grad,
    proj_grad,
    small,
    small_in,
    small_x,
    small_z,
    core_in,
    part,
    low_buf,
    in1,
    low2,
    in2,
    mine,
    z_in,
    sem_flow,
    sem_kv,
    sem_c,
    sem_in,
    sem_s,
    sem_op,
    sem_co,
):
    d = lax.axis_index("dp")
    r = lax.axis_index("row")
    c = lax.axis_index("col")
    core = lax.rem(d, 2)
    y = lax.rem(d // 2, 2)
    x = d // 4
    sibling = d + 1 - 2 * core
    other_y = d + 2 - 4 * y
    x_peers = [(k, lax.rem(x + k, 4) * 4 + lax.rem(d, 4)) for k in (1, 2, 3)]
    row_peers = [(k, lax.rem(r + k, 4)) for k in (1, 2, 3)]
    block = 4 * d + r
    near = lambda i: {
        "dp": lax.rem((block + 64 + i) // 4, 16),
        "row": lax.rem(r + 4 + i, 4),
    }
    greet(
        [{"row": q} for _, q in row_peers]
        + [{"dp": p} for _, p in x_peers]
        + [{"col": 1 - c}, {"dp": sibling}, {"dp": other_y}]
        + [near(i) for i in (1, 2, 3, 4, -1, -2, -3, -4)]
    )
    pending = []

    def go(*args, **device):
        copy = rcopy(*args, **device)
        copy.start()
        pending.append(copy)
        return copy

    span = lambda q: pl.ds(pl.multiple_of(q * SHARE, SHARE), SHARE)
    buffers = (core_in, part, low_buf, in1, low2, in2, mine, z_in)
    flows = [
        GradSum(t, source, out, joined, wide_first, (r, d), buffers, sem_flow, go)
        for t, source, out, joined, wide_first in (
            (0, ff_ref.at[0], ff_out.at[0], True, True),
            (1, ff_ref.at[1], ff_out.at[1], True, False),
            (2, ff_ref.at[2], ff_out.at[2], True, True),
            (3, outw_grad, outw_out, False, False),
            (4, proj_grad, proj_out, False, True),
        )
    ]
    early, tail = flows[:4], flows[4]
    for flow in early[:3]:
        flow.step()

    def scatter(k, q):
        return go(
            op_ref.at[q], op_in.at[k - 1], sem_op.at[0, k - 1], sem_op.at[1, k - 1], row=q
        )

    op_copies = [scatter(*row_peers[0]), scatter(*row_peers[2])]

    small[...] = jnp.zeros_like(small)
    square = jnp.zeros((SHARE, 1), F32)
    inner = jnp.zeros((SHARE, 1), F32)
    for j in range(4):
        value = mid_ref[j]
        square += jnp.sum(value * value, axis=1, keepdims=True)
        inner += jnp.sum(second_ref[j] * gains_full[j, 1:2, :] * value, axis=1, keepdims=True)
    rate = lax.rsqrt(square / D + EPS)
    scale = rate * rate * rate * inner / D
    for j in range(4):
        value = mid_ref[j]
        grad = second_ref[j]
        small[j, 1:2, 0:FEAT] = jnp.sum(grad * value * rate, axis=0, keepdims=True)
        total = (
            cot_ref[j].astype(F32)
            + rate * (grad * gains_full[j, 1:2, :])
            - value * scale
        )
        g_mid[j] = total
        g_branch[j] = total.astype(BF)
    grad_att = dot_nt(g_branch[0], outw_full[0])
    for j in range(1, 4):
        grad_att += dot_nt(g_branch[j], outw_full[j])
    g_att[:, 448:512] = jnp.zeros((SHARE, 64), BF)
    g_att[:, 0:448] = grad_att.astype(BF)
    for flow in early[:3]:
        flow.step()
    outw_grad[...] = jnp.zeros_like(outw_grad)
    for j in range(4):
        outw_grad[j, 0:FEAT, 0:448] = dot_tn(g_branch[j], att_ref[...]).astype(BF)
    early[3].step()
    query_at = lax.broadcasted_iota(jnp.int32, (SHARE, 1), 0) + MAXLEN
    key_at = lax.broadcasted_iota(jnp.int32, (SHARE, MAXLEN + SHARE), 1)
    mask[...] = jnp.where(
        (key_at >= start_ref[...]) & (key_at <= query_at), 0.0, -1e30
    )

    lane = lax.broadcasted_iota(jnp.int32, (SHARE, 128), 1)
    low = lane < 64
    for m in range(HEADS // GROUPS):
        at = 128 * (m // 2)
        mine_lanes = low if m % 2 == 0 else jnp.logical_not(low)
        pick = lambda ref: jnp.where(
            mine_lanes, ref[:, at : at + 128].astype(F32), 0.0
        ).astype(BF)
        query, grad = pick(q_ref), pick(g_att)
        probs = jnp.exp(dot_nt(query, kv_ref[0]) + mask[...] - lse_ref[m])
        grad_probs = dot_nt(grad, kv_ref[1])
        inner = jnp.sum(probs * grad_probs, axis=1, keepdims=True)
        grad_scores = (probs * (grad_probs - inner)).astype(BF)
        grad_v = dot_tn(probs.astype(BF), grad)
        grad_k = dot_tn(grad_scores, query)
        if m == 0:
            dv[...] = grad_v
            dk[...] = grad_k
        else:
            dv[...] += grad_v
            dk[...] += grad_k
        grad_q = dot(grad_scores, kv_ref[0]) * HEAD_DIM ** (-0.5)
        if m % 2 == 0:
            dq[:, at : at + 128] = grad_q
        else:
            dq[:, at : at + 128] = jnp.where(low, dq[:, at : at + 128], grad_q)
        if m == 1:
            early[3].step()
    wide_low = lax.broadcasted_iota(jnp.int32, (MAXLEN + SHARE, 128), 1) < 64
    dkv[...] = jnp.where(
        wide_low,
        dk[...] + pltpu.roll(dk[...], 64, 1),
        dv[...] + pltpu.roll(dv[...], 64, 1),
    ).astype(BF)
    kv_copies = [
        go(
            dkv.at[(4 - i) * SHARE : (5 - i) * SHARE, :],
            dkv_in.at[i - 1],
            sem_kv.at[0, i - 1],
            sem_kv.at[1, i - 1],
            **near(-i),
        )
        for i in (1, 2, 3, 4)
    ]
    for flow in early:
        flow.step()
    total = dkv[MAXLEN : MAXLEN + SHARE, :].astype(F32)
    for i in (1, 2, 3, 4):
        kv_copies[i - 1].wait_recv()
        total += dkv_in[i - 1].astype(F32)
    op_copies.append(scatter(*row_peers[1]))
    turned = pltpu.roll(total, 64, 1)
    dq[:, 384:512] = jnp.where(low, dq[:, 384:512], turned)
    gv[...] = turned[:, 0:64].astype(BF)
    cosine = jnp.concatenate([cos_ref[...]] * 4, axis=1)
    sine = jnp.concatenate([sin_ref[...]] * 4, axis=1)
    gp[...] = (dq[...] * cosine - swapped(dq[...]) * sine).astype(BF)
    for j in range(4):
        c_send[j] = (
            dot_nt(gp[...], proj_full[j, :, 0:512])
            + dot_nt(gv[...], proj_full[j, :, 512:576])
        ).astype(BF)
    cross = go(c_send, c_in, sem_c.at[0], sem_c.at[1], col=1 - c)
    proj_grad[...] = jnp.zeros_like(proj_grad)
    for j in range(4):
        proj_grad[j, 0:FEAT, 0:512] = dot_tn(nf_ref[j], gp[...]).astype(BF)
        proj_grad[j, 0:FEAT, 512:576] = dot_tn(nf_ref[j], gv[...]).astype(BF)
    tail.step()
    bias_a = jnp.sum(gp[...].astype(F32), axis=0, keepdims=True)
    bias_b = jnp.sum(gv[...].astype(F32), axis=0, keepdims=True)
    for j in range(4):
        small[j, 2:3, 0:512] = bias_a
        small[j, 2:3, 512:576] = bias_b
    for flow in early:
        flow.step()
    tail.step()

    square = jnp.zeros((SHARE, 1), F32)
    for j in range(4):
        value = x_ref[j].astype(F32)
        square += jnp.sum(value * value, axis=1, keepdims=True)
    rate = lax.rsqrt(square / D + EPS)
    cross.wait_recv()
    inner = jnp.zeros((SHARE, 1), F32)
    for j in range(4):
        grad = c_send[j].astype(F32) + c_in[j].astype(F32)
        inner += jnp.sum(
            grad * gains_full[j, 0:1, :] * x_ref[j].astype(F32), axis=1, keepdims=True
        )
    scale = rate * rate * rate * inner / D
    for j in range(4):
        value = x_ref[j].astype(F32)
        grad = c_send[j].astype(F32) + c_in[j].astype(F32)
        small[j, 0:1, 0:FEAT] = jnp.sum(grad * value * rate, axis=0, keepdims=True)
        own_input[j] = (
            g_mid[j] + rate * (grad * gains_full[j, 0:1, :]) - value * scale
        ).astype(BF)
    in_copies = [
        go(
            own_input.at[q],
            input_out.at[r],
            sem_in.at[0, k - 1],
            sem_in.at[1, k - 1],
            row=q,
        )
        for k, q in row_peers
    ]
    input_out[r] = own_input[r]

    total = op_ref[r].astype(F32)
    for copy in op_copies:
        copy.wait_recv()
    for k in range(3):
        total += op_in[k].astype(F32)
    co_send[...] = total.astype(BF)
    final = go(co_send, co_in, sem_co.at[0], sem_co.at[1], col=1 - c)

    def swap(stage, source, target, k, **device):
        return go(source, target, sem_s.at[0, stage, k - 1], sem_s.at[1, stage, k - 1], **device)

    copy = swap(0, small, small_in.at[0], 1, dp=sibling)
    for flow in early:
        flow.step()
    tail.step()
    copy.wait_recv()
    small_x[0] = small[...] + small_in[0]
    copies = [swap(1, small_x.at[0], small_in.at[k], k, dp=p) for k, p in x_peers]
    for flow in early:
        flow.step()
    tail.step()
    for copy in copies:
        copy.wait_recv()
    small_x[1] = small_x[0] + small_in[1] + small_in[2] + small_in[3]
    copy = swap(2, small_x.at[1], small_in.at[4], 1, dp=other_y)
    tail.step()
    copy.wait_recv()
    small_x[2] = small_x[1] + small_in[4]
    copies = [swap(3, small_x.at[2, q], small_z.at[r], k, row=q) for k, q in row_peers]
    small_z[r] = small_x[2, r]
    tail.step()
    for flow in early:
        flow.step()
    for copy in copies:
        copy.wait_recv()
    small_out[...] = small_z[0] + small_z[1] + small_z[2] + small_z[3]
    tail.step()
    for flow in early:
        flow.step()
    tail.step()
    for copy in in_copies:
        copy.wait_recv()
    final.wait_recv()
    block_out[...] = (co_send[...].astype(F32) + co_in[...].astype(F32)).astype(BF)
    for copy in pending:
        copy.wait_send()


def back(*operands):
    dma = pltpu.SemaphoreType.DMA
    shape = jax.ShapeDtypeStruct
    width = MAXLEN + SHARE
    blocked = pltpu.VMEM((4, SHARE, FEAT), BF)
    count = 5
    return vmem_call(
        back_kernel,
        17,
        (
            shape((SHARD, FEAT), BF),
            shape((4, SHARE, FEAT), BF),
            shape((3, PADF, HALF_FF), BF),
            shape((PADF, WIN), BF),
            shape((PADF, WIN), BF),
            shape((8, WIN), F32),
        ),
        [
            pltpu.VMEM((SHARE, width), F32),
            pltpu.VMEM((4, SHARE, FEAT), F32),
            blocked,
            pltpu.VMEM((SHARE, 512), BF),
            pltpu.VMEM((SHARE, 512), F32),
            pltpu.VMEM((width, 128), F32),
            pltpu.VMEM((width, 128), F32),
            pltpu.VMEM((width, 128), BF),
            pltpu.VMEM((4, SHARE, 128), BF),
            pltpu.VMEM((SHARE, 512), BF),
            pltpu.VMEM((SHARE, 64), BF),
            blocked,
            blocked,
            pltpu.VMEM((3, SHARD, FEAT), BF),
            pltpu.VMEM((SHARD, FEAT), BF),
            pltpu.VMEM((SHARD, FEAT), BF),
            blocked,
            pltpu.VMEM((4, PADF, WIN), BF),
            pltpu.VMEM((4, PADF, WIN), BF),
            pltpu.VMEM((4, 8, WIN), F32),
            pltpu.VMEM((5, 4, 8, WIN), F32),
            pltpu.VMEM((3, 4, 8, WIN), F32),
            pltpu.VMEM((4, 8, WIN), F32),
            pltpu.VMEM((count, 4, 128, WIN), BF),
            pltpu.VMEM((count, 4, 128, WIN), F32),
            pltpu.VMEM((count, 4, 128, WIN), BF),
            pltpu.VMEM((count, 4, 96, WIN), BF),
            pltpu.VMEM((count, 4, 64, WIN), BF),
            pltpu.VMEM((count, 4, 48, WIN), BF),
            pltpu.VMEM((count, 4, 16, WIN), BF),
            pltpu.VMEM((count, 4, 16, WIN), BF),
            dma((2, count, 7, 3)),
            dma((2, 4)),
            dma((2,)),
            dma((2, 3)),
            dma((2, 4, 3)),
            dma((2, 3)),
            dma((2,)),
        ],
        1,
    )(*operands)


def body(
    activations,
    starts,
    first_gain,
    project_weight,
    project_bias,
    output_weight,
    second_gain,
    gate_weight,
    up_weight,
    down_weight,
    cotangent,
):
    r = lax.axis_index("row")
    shard = lax.axis_index("dp")
    query_width = HEADS // GROUPS * HEAD_DIM

    base = shard * SHARD + r * SHARE
    start_window = (
        lax.dynamic_slice_in_dim(starts, r * SHARE, SHARE, 0) - base + MAXLEN
    )[:, None]
    positions = (MAXLEN + jnp.arange(SHARE, dtype=jnp.int32))[:, None] - start_window
    half = HEAD_DIM // 2
    freqs = 1000000.0 ** (-jnp.arange(half, dtype=F32) * 2.0 / HEAD_DIM)
    angle = positions.astype(F32) * jnp.tile(freqs, 4)[None, :]
    cosine = jnp.cos(angle)
    sine = jnp.sin(angle) * jnp.tile(jnp.repeat(jnp.array([-1.0, 1.0], F32), half), 2)[None, :]
    gains = jnp.pad(jnp.stack([first_gain, second_gain]), ((0, 6), (0, 0)))
    (
        x_low,
        normed_first,
        queries,
        kv,
        lse,
        attended,
        middle,
        project_full,
        output_full,
        gains_full,
        cot_own,
        grad_second,
        out_partial,
        ff_grads,
    ) = forward(
        activations,
        cotangent,
        project_weight,
        output_weight,
        gate_weight,
        up_weight,
        down_weight,
        gains,
        project_bias[None, :],
        cosine,
        sine,
        start_window,
    )
    block_output, input_grad, ff_sum, outw_sum, project_sum, small = back(
        grad_second,
        middle,
        cot_own,
        x_low,
        normed_first,
        queries,
        kv,
        lse,
        attended,
        project_full,
        output_full,
        gains_full,
        cosine,
        sine,
        start_window,
        ff_grads,
        out_partial,
    )
    width = project_weight.shape[1]
    ff_sum = ff_sum[:, :FEAT].astype(F32)
    return (
        block_output,
        input_grad.reshape(SHARD, FEAT).astype(F32),
        small[0, :FEAT],
        project_sum[:FEAT, :width].astype(F32),
        small[2, :width],
        outw_sum[:FEAT, :query_width].astype(F32).T,
        small[1, :FEAT],
        ff_sum[0],
        ff_sum[1],
        ff_sum[2].T,
    )


def solution(mesh):
    return jax.shard_map(
        body,
        mesh=mesh,
        in_specs=(
            P("dp", "row"),
            P("dp"),
            P("row"),
            P("row", "col"),
            P("col"),
            P("col", "row"),
            P("row"),
            P("row", "col"),
            P("row", "col"),
            P("col", "row"),
            P("dp", "row"),
        ),
        out_specs=(
            P("dp", "row"),
            P("dp", "row"),
            P("row"),
            P("row", "col"),
            P("col"),
            P("col", "row"),
            P("row"),
            P("row", "col"),
            P("row", "col"),
            P("col", "row"),
        ),
        check_vma=False,
    )
```

```python
import functools

import jax
import jax.numpy as jnp
from jax import lax
from jax.experimental import pallas as pl
from jax.experimental.pallas import tpu as pltpu
from jax.sharding import PartitionSpec as P

D = 896
HEADS = 14
GROUPS = 2
HEAD_DIM = 64
MAXLEN = 1024
EPS = 1e-06
BF = jnp.bfloat16
F32 = jnp.float32
ROWS = 4
FEAT = 224
SHARE = 256
SHARD = 1024
HALF_FF = 2432
WIN = 640
LAST = HALF_FF - WIN
PADF = 256
VMEM_LIMIT = 60 * 1024 * 1024


def dot(a, b):
    return jnp.dot(a, b, preferred_element_type=F32)


def dot_nt(a, b):
    return lax.dot_general(a, b, (((1,), (1,)), ((), ())), preferred_element_type=F32)


def dot_tn(a, b):
    return lax.dot_general(a, b, (((0,), (0,)), ((), ())), preferred_element_type=F32)


def rcopy(src, dst, send, recv, **device):
    return pltpu.make_async_remote_copy(
        src_ref=src,
        dst_ref=dst,
        send_sem=send,
        recv_sem=recv,
        device_id=device,
        device_id_type=pl.DeviceIdType.MESH,
    )


def greet(peers):
    barrier = pltpu.get_barrier_semaphore()
    for peer in peers:
        pl.semaphore_signal(
            barrier, inc=1, device_id=peer, device_id_type=pl.DeviceIdType.MESH
        )
    pl.semaphore_wait(barrier, len(peers))


def vmem_call(kernel, inputs, outs, scratch, collective, cost=None):
    return pl.pallas_call(
        kernel,
        out_shape=outs,
        in_specs=[pl.BlockSpec(memory_space=pltpu.VMEM)] * inputs,
        out_specs=jax.tree.map(lambda _: pl.BlockSpec(memory_space=pltpu.VMEM), outs),
        scratch_shapes=scratch,
        compiler_params=pltpu.CompilerParams(
            collective_id=collective,
            has_side_effects=True,
            vmem_limit_bytes=VMEM_LIMIT,
        ),
        cost_estimate=cost,
    )


class GradSum:
    def __init__(self, t, source, out, joined, wide_first, place, buffers, sems, go):
        self.t, self.source, self.out, self.joined, self.go = t, source, out, joined, go
        self.r, d = place
        self.core = lax.rem(d, 2)
        y = lax.rem(d // 2, 2)
        x = d // 4
        self.sibling = d + 1 - 2 * self.core
        along_x = [
            (k, lax.rem(x + k, 4), lax.rem(x + k, 4) * 4 + lax.rem(d, 4)) for k in (1, 2, 3)
        ]
        along_y = [(1, 1 - y, d + 2 - 4 * y)]
        if wide_first:
            self.first, self.second = (along_x, x, 32), (along_y, y, 16)
        else:
            self.first, self.second = (along_y, y, 64), (along_x, x, 16)
        self.at_first = self.core * 128 + self.first[1] * self.first[2]
        self.at = self.at_first + self.second[1] * 16
        self.core_in, self.part, self.low, self.in1, self.low2, self.in2, self.mine, self.z_in = [
            buffer.at[t] if buffer is not None else None for buffer in buffers
        ]
        self.sem = lambda stage, k: (sems.at[0, t, stage, k - 1], sems.at[1, t, stage, k - 1])
        self.waiting = []
        self.done = 0

    def rows(self, start, size):
        return pl.ds(pl.multiple_of(start, 16), size)

    def settle(self):
        for copy in self.waiting:
            copy.wait_recv()
        self.waiting = []

    def send(self, source, target, stage, k, **device):
        self.waiting.append(self.go(source, target, *self.sem(stage, k), **device))

    def step(self):
        self.settle()
        getattr(self, "step%d" % self.done)()
        self.done += 1

    def step0(self):
        self.send(
            self.source.at[:, self.rows((1 - self.core) * 128, 128), :],
            self.core_in,
            0,
            1,
            dp=self.sibling,
        )

    def step1(self):
        peers, own, unit = self.first
        total = self.source[:, self.rows(self.core * 128, 128), :].astype(F32)
        total = total + self.core_in[...].astype(F32)
        self.part[...] = total
        self.low[...] = total.astype(BF)
        for k, index, device in peers:
            self.send(
                self.low.at[:, self.rows(index * unit, unit), :],
                self.in1.at[:, (k - 1) * unit : k * unit, :],
                1,
                k,
                dp=device,
            )

    def step2(self):
        peers, own, unit = self.first
        total = self.part[:, self.rows(own * unit, unit), :]
        for k, _, _ in peers:
            total = total + self.in1[:, (k - 1) * unit : k * unit, :].astype(F32)
        self.part[:, 0:unit, :] = total
        self.low2[:, 0:unit, :] = total.astype(BF)
        peers, own, unit = self.second
        for k, index, device in peers:
            self.send(
                self.low2.at[:, self.rows(index * unit, unit), :],
                self.in2.at[:, (k - 1) * unit : k * unit, :],
                2,
                k,
                dp=device,
            )

    def step3(self):
        self.reduce()
        self.cross_rows()

    def reduce(self):
        self.settle()
        peers, own, unit = self.second
        total = self.part[:, self.rows(own * unit, unit), :]
        for k, _, _ in peers:
            total = total + self.in2[:, (k - 1) * unit : k * unit, :].astype(F32)
        self.mine[...] = total.astype(BF)

    def cross_rows(self):
        for k in (1, 2, 3):
            q = lax.rem(self.r + k, 4)
            self.send(self.mine.at[q], self.z_in.at[self.r], 3, k, row=q)
        self.z_in[self.r] = self.mine[self.r]

    def step4(self):
        here = self.rows(self.at, 16)
        if self.joined:
            for q in range(3):
                self.out[here, q * WIN : (q + 1) * WIN] = self.z_in[q]
            self.out[here, 3 * WIN : HALF_FF] = self.z_in[3][:, 4 * WIN - HALF_FF :]
        else:
            total = self.z_in[0].astype(F32)
            for q in range(1, 4):
                total = total + self.z_in[q].astype(F32)
            self.out[here, :] = total.astype(BF)
        self.spread(self.second[0], self.at, 16, 4)

    def spread(self, peers, start, size, stage):
        block = self.out.at[self.rows(start, size), :]
        for k, _, device in peers:
            self.send(block, block, stage, k, dp=device)

    def step5(self):
        self.spread(self.first[0], self.at_first, self.first[2], 5)

    def step6(self):
        self.spread([(1, 0, self.sibling)], self.core * 128, 128, 6)

    def step7(self):
        pass


def swapped(values):
    width = values.shape[1]
    lane = lax.broadcasted_iota(jnp.int32, values.shape, 1)
    return jnp.where(
        lax.rem(lane, 64) < 32,
        pltpu.roll(values, width - 32, 1),
        pltpu.roll(values, 32, 1),
    )


def forward_kernel(
    act_ref,
    cot_ref,
    proj_ref,
    outw_ref,
    gate_ref,
    up_ref,
    down_ref,
    gains_ref,
    bias_ref,
    cos_ref,
    sin_ref,
    start_ref,
    x_out,
    nf_out,
    q_out,
    kv_out,
    lse_out,
    att_out,
    mid_out,
    proj_full,
    outw_full,
    gains_full,
    cot_out,
    second_out,
    op_out,
    mine_out,
    gate_full,
    up_full,
    down_full,
    cot_all,
    mask,
    own_kv,
    c_send,
    c_in,
    second_in,
    ns_all,
    hid,
    gg,
    gu,
    sp_send,
    sp_in,
    grads,
    core_in,
    part,
    low_buf,
    in1,
    low2,
    in2,
    sem_x,
    sem_g,
    sem_w,
    sem_wx,
    sem_wc,
    sem_cot,
    sem_kv,
    sem_c,
    sem_ag,
    sem_sp,
    sem_cs,
    sem_flow,
    sem_l,
):
    d = lax.axis_index("dp")
    r = lax.axis_index("row")
    c = lax.axis_index("col")
    core = lax.rem(d, 2)
    x_at = d // 4
    sibling = d + 1 - 2 * core
    other_y = d + 2 - 4 * lax.rem(d // 2, 2)
    x_peers = [(k, lax.rem(x_at + k, 4) * 4 + lax.rem(d, 4)) for k in (1, 2, 3)]
    block = 4 * d + r
    near = lambda i: {
        "dp": lax.rem((block + 64 + i) // 4, 16),
        "row": lax.rem(r + 4 + i, 4),
    }
    greet(
        [{"row": lax.rem(r + k, 4)} for k in (1, 2, 3)]
        + [{"dp": p} for _, p in x_peers]
        + [{"col": 1 - c}, {"dp": sibling}, {"dp": other_y}]
        + [near(i) for i in (1, 2, 3, 4, -1, -2, -3, -4)]
    )
    pending = []

    def go(*args, **device):
        copy = rcopy(*args, **device)
        copy.start()
        pending.append(copy)
        return copy

    peers = [(k, lax.rem(r + k, 4)) for k in (1, 2, 3)]
    span = lambda q: pl.ds(pl.multiple_of(q * SHARE, SHARE), SHARE)
    offset = lambda q: pl.multiple_of(jnp.minimum(q * WIN, LAST), 128)
    half = lambda n: pl.ds(pl.multiple_of(core * n, 16), n)

    def down_rows(q):
        return pl.ds(pl.multiple_of(offset(q) + core * (WIN // 2), 16), WIN // 2)

    pieces = (
        (lambda q: proj_ref.at[half(112), :], proj_full, 112),
        (lambda q: outw_ref.at[half(224), :], outw_full, 224),
        (lambda q: gate_ref.at[half(112), pl.ds(offset(q), WIN)], gate_full, 112),
        (lambda q: up_ref.at[half(112), pl.ds(offset(q), WIN)], up_full, 112),
        (lambda q: down_ref.at[down_rows(q), :], down_full, WIN // 2),
    )

    def crossing(w):
        source, full, n = pieces[w]
        return [
            rcopy(
                source(q),
                full.at[r, half(n), :],
                sem_w.at[0, w, k - 1],
                sem_w.at[1, w, k - 1],
                row=q,
            )
            for k, q in peers
        ]

    def passing(w):
        _, full, n = pieces[w]
        copies = []
        for k, q in peers:
            part = full.at[q, half(n), :]
            for e, device in x_peers:
                copies.append(
                    rcopy(
                        part,
                        part,
                        sem_wx.at[0, w - 2, k - 1, e - 1],
                        sem_wx.at[1, w - 2, k - 1, 0],
                        dp=device,
                    )
                )
        return copies

    def fetch(w):
        source, full, n = pieces[w]
        local = pltpu.make_async_copy(source(r), full.at[r, half(n), :], sem_l.at[w])
        local.start()
        copies = crossing(w)
        if w < 2:
            for copy in copies:
                copy.start()
                pending.append(copy)
        else:

            @pl.when(x_at == w - 2)
            def _():
                for copy in copies:
                    copy.start()

        return copies, local

    def pass_on(w, fetched):
        @pl.when(x_at == w - 2)
        def _():
            for copy in fetched[0]:
                copy.wait_recv()
            for copy in passing(w):
                copy.start()

    def share(w, fetched):
        _, full, n = pieces[w]
        copies, local = fetched
        local.wait()
        if w < 2:
            for copy in copies:
                copy.wait_recv()
        else:

            @pl.when(x_at != w - 2)
            def _():
                for copy in passing(w)[::3]:
                    copy.wait_recv()

        part = full.at[:, half(n), :]
        copy = rcopy(part, part, sem_wc.at[0, w], sem_wc.at[1, w], dp=sibling)
        copy.start()
        if w < 2:
            pending.append(copy)
        return copy

    def finish(w, fetched):
        @pl.when(x_at == w - 2)
        def _():
            for copy in fetched[0] + passing(w):
                copy.wait_send()

    x_copies = [
        go(
            act_ref.at[span(q), :],
            x_out.at[r],
            sem_x.at[0, k - 1],
            sem_x.at[1, k - 1],
            row=q,
        )
        for k, q in peers
    ]
    g_copies = [
        go(gains_ref, gains_full.at[r], sem_g.at[0, k - 1], sem_g.at[1, k - 1], row=q)
        for k, q in peers
    ]
    fetched = {0: fetch(0)}
    x_out[r] = act_ref[span(r), :]
    gains_full[r] = gains_ref[...]
    query_at = lax.broadcasted_iota(jnp.int32, (SHARE, 1), 0) + MAXLEN
    key_at = lax.broadcasted_iota(jnp.int32, (SHARE, MAXLEN + SHARE), 1)
    mask[...] = jnp.where(
        (key_at >= start_ref[...]) & (key_at <= query_at), 0.0, -1e30
    )
    shared = {0: share(0, fetched[0])}
    for copy in x_copies + g_copies:
        copy.wait_recv()
    for w in (1, 2, 3, 4):
        fetched[w] = fetch(w)
    cot_all[r] = cot_ref[...]
    square = jnp.zeros((SHARE, 1), F32)
    for j in range(4):
        value = x_out[j].astype(F32)
        square += jnp.sum(value * value, axis=1, keepdims=True)
    rate = lax.rsqrt(square / D + EPS)
    for j in range(4):
        nf_out[j] = (x_out[j].astype(F32) * rate * gains_full[j, 0:1, :]).astype(BF)
    shared[0].wait_recv()
    projected = dot(nf_out[0], proj_full[0, :, 0:512])
    values = dot(nf_out[0], proj_full[0, :, 512:576])
    for j in range(1, 4):
        projected += dot(nf_out[j], proj_full[j, :, 0:512])
        values += dot(nf_out[j], proj_full[j, :, 512:576])
    projected += bias_ref[:, 0:512]
    values = (values + bias_ref[:, 512:576]).astype(BF)
    cosine = jnp.concatenate([cos_ref[...]] * 4, axis=1)
    sine = jnp.concatenate([sin_ref[...]] * 4, axis=1)
    turned = projected * cosine + swapped(projected) * sine
    q_out[...] = (turned * HEAD_DIM ** (-0.5)).astype(BF)
    tile = turned[:, 384:512]
    lane = lax.broadcasted_iota(jnp.int32, (SHARE, 128), 1)
    low = lane < 64
    own_kv[0] = jnp.where(low, pltpu.roll(tile, 64, 1), tile).astype(BF)
    double = (
        lax.rem(lax.broadcasted_iota(jnp.int32, (64, 128), 1), 64)
        == lax.broadcasted_iota(jnp.int32, (64, 128), 0)
    ).astype(F32).astype(BF)
    own_kv[1] = dot(values, double).astype(BF)
    kv_copies = [
        go(
            own_kv,
            kv_out.at[:, (4 - i) * SHARE : (5 - i) * SHARE, :],
            sem_kv.at[0, i - 1],
            sem_kv.at[1, i - 1],
            **near(i),
        )
        for i in (1, 2, 3, 4)
    ]
    kv_out[:, MAXLEN : MAXLEN + SHARE, :] = own_kv[...]
    for w in (2, 3, 4):
        pass_on(w, fetched[w])
    for copy in kv_copies:
        copy.wait_recv()
    cot_copies = [
        go(cot_ref, cot_all.at[r], sem_cot.at[0, k - 1], sem_cot.at[1, k - 1], row=q)
        for k, q in (peers[0], peers[2], peers[1])
    ]
    for m in range(HEADS // GROUPS):
        at = 128 * (m // 2)
        mine = low if m % 2 == 0 else jnp.logical_not(low)
        query = jnp.where(mine, q_out[:, at : at + 128].astype(F32), 0.0).astype(BF)
        scores = dot_nt(query, kv_out[0]) + mask[...]
        peak = jnp.max(scores, axis=1, keepdims=True)
        powered = jnp.exp(scores - peak)
        total = jnp.sum(powered, axis=1, keepdims=True)
        probs = (powered * (1.0 / total)).astype(BF)
        lse_out[m] = peak + jnp.log(total)
        mixed = dot(probs, kv_out[1])
        if m == 6:
            att_out[:, 384:448] = mixed[:, 0:64].astype(BF)
        elif m % 2 == 0:
            even = mixed
        else:
            att_out[:, at : at + 128] = jnp.where(low, even, mixed).astype(BF)
    shared[1] = share(1, fetched[1])
    shared[1].wait_recv()
    for j in range(4):
        c_send[j] = dot(att_out[...], outw_full[j]).astype(BF)
    cross = rcopy(c_send, c_in, sem_c.at[0], sem_c.at[1], col=1 - c)
    cross.start()
    for w in (2, 3, 4):
        shared[w] = share(w, fetched[w])
    cross.wait_recv()
    square = jnp.zeros((SHARE, 1), F32)
    for j in range(4):
        value = x_out[j].astype(F32) + (
            c_send[j].astype(F32) + c_in[j].astype(F32)
        )
        mid_out[j] = value
        square += jnp.sum(value * value, axis=1, keepdims=True)
    rate = lax.rsqrt(square / D + EPS)
    for j in range(4):
        ns_all[j, span(r), :] = (mid_out[j] * rate * gains_full[j, 1:2, :]).astype(BF)

    right, across, left = [q for _, q in peers]

    def spread(blocks, source, index, q):
        part = ns_all.at[blocks, span(source), :]
        return go(part, part, sem_ag.at[0, index], sem_ag.at[1, index], row=q)

    every, front_half, back_half = pl.ds(0, 4), pl.ds(0, 2), pl.ds(2, 2)
    from_left = spread(every, r, 0, right)
    from_right = spread(every, r, 1, left)
    for copy in cot_copies:
        copy.wait_recv()
    for w in (2, 3, 4):
        shared[w].wait_recv()
        shared[w].wait_send()
        finish(w, fetched[w])
    live = jnp.where(r < 3, 1.0, 0.0)
    extra = 4 * WIN - HALF_FF
    for j in range(4):
        gate_full[j, :, 0:extra] = (gate_full[j, :, 0:extra].astype(F32) * live).astype(BF)
        up_full[j, :, 0:extra] = (up_full[j, :, 0:extra].astype(F32) * live).astype(BF)
        cot_out[j] = cot_all[j, span(r), :]

    def feed(k, q, arrived):
        grad_hidden = dot_nt(cot_all[0, span(q), :], down_full[0])
        for j in range(1, 4):
            grad_hidden += dot_nt(cot_all[j, span(q), :], down_full[j])
        arrived()
        gate = dot(ns_all[0, span(q), :], gate_full[0])
        up = dot(ns_all[0, span(q), :], up_full[0])
        for j in range(1, 4):
            gate += dot(ns_all[j, span(q), :], gate_full[j])
            up += dot(ns_all[j, span(q), :], up_full[j])
        sigma = 1.0 / (1.0 + jnp.exp(-gate))
        silu = gate * sigma
        hid[span(q), :] = (silu * up).astype(BF)
        g_gate = (grad_hidden * up * (sigma + silu * (1.0 - sigma))).astype(BF)
        g_up = (grad_hidden * silu).astype(BF)
        gg[span(q), :] = g_gate
        gu[span(q), :] = g_up
        copies = []
        for j in range(4):
            sp_send[k, j] = (
                dot_nt(g_gate, gate_full[j]) + dot_nt(g_up, up_full[j])
            ).astype(BF)
            if k and j % 2:
                copies.append(
                    go(
                        sp_send.at[k, j - 1 : j + 1],
                        sp_in.at[k - 1, j - 1 : j + 1],
                        sem_sp.at[0, k - 1, j // 2],
                        sem_sp.at[1, k - 1, j // 2],
                        row=q,
                    )
                )
        return copies

    forwarded = []

    def neighbours_here():
        from_left.wait_recv()
        forwarded.append(spread(front_half, left, 2, right))
        from_right.wait_recv()
        forwarded.append(spread(back_half, right, 3, left))

    def opposite_here():
        for copy in forwarded:
            copy.wait_recv()

    feed(0, r, lambda: None)
    back = {}
    back[1] = feed(1, right, neighbours_here)
    back[3] = feed(3, left, lambda: None)
    back[2] = feed(2, across, opposite_here)

    buffers = (core_in, part, low_buf, in1, low2, in2, mine_out, None)
    flows = [
        GradSum(t, grads.at[t], None, True, True, (r, d), buffers, sem_flow, go)
        for t in range(3)
    ]
    grads[:, :, FEAT:PADF, :] = jnp.zeros((3, 4, PADF - FEAT, WIN), BF)
    for t, left_side, right_side in ((0, ns_all, gg), (1, ns_all, gu), (2, cot_all, hid)):
        for j in range(4):
            grads[t, j, 0:FEAT, :] = dot_tn(left_side[j], right_side[...]).astype(BF)
        flows[t].step()
        if t:
            flows[t - 1].step()
    flows[2].step()
    cross.wait_send()
    crosses = []
    for h in (0, 2):
        total = sp_send[0, h : h + 2].astype(F32)
        for k in (1, 3, 2):
            back[k][h // 2].wait_recv()
            total += sp_in[k - 1, h : h + 2].astype(F32)
        c_send[h : h + 2] = total.astype(BF)
        crosses.append(
            go(
                c_send.at[h : h + 2],
                second_in.at[h : h + 2],
                sem_cs.at[0, h // 2],
                sem_cs.at[1, h // 2],
                col=1 - c,
            )
        )
    for j in range(4):
        for q in range(4):
            op_out[j, q * SHARE : (q + 1) * SHARE, :] = dot(
                hid[q * SHARE : (q + 1) * SHARE, :], down_full[j]
            ).astype(BF)
        op_out[j, span(r), :] = (
            op_out[j, span(r), :].astype(F32) + 0.5 * mid_out[j]
        ).astype(BF)
    for flow in flows:
        flow.step()
    for copy in crosses:
        copy.wait_recv()
    second_out[...] = c_send[...].astype(F32) + second_in[...].astype(F32)
    for flow in flows:
        flow.reduce()
    for copy in pending:
        copy.wait_send()


def forward(*operands):
    dma = pltpu.SemaphoreType.DMA
    shape = jax.ShapeDtypeStruct
    width = MAXLEN + SHARE
    blocked = pltpu.VMEM((4, SHARE, FEAT), BF)
    return vmem_call(
        forward_kernel,
        12,
        (
            shape((4, SHARE, FEAT), BF),
            shape((4, SHARE, FEAT), BF),
            shape((SHARE, 512), BF),
            shape((2, width, 128), BF),
            shape((HEADS // GROUPS, SHARE, 1), F32),
            shape((SHARE, 448), BF),
            shape((4, SHARE, FEAT), F32),
            shape((4, FEAT, 576), BF),
            shape((4, 448, FEAT), BF),
            shape((4, 8, FEAT), F32),
            shape((4, SHARE, FEAT), BF),
            shape((4, SHARE, FEAT), F32),
            shape((4, SHARD, FEAT), BF),
            shape((3, 4, 16, WIN), BF),
        ),
        [
            pltpu.VMEM((4, FEAT, WIN), BF),
            pltpu.VMEM((4, FEAT, WIN), BF),
            pltpu.VMEM((4, WIN, FEAT), BF),
            pltpu.VMEM((4, SHARD, FEAT), BF),
            pltpu.VMEM((SHARE, width), F32),
            pltpu.VMEM((2, SHARE, 128), BF),
            blocked,
            blocked,
            blocked,
            pltpu.VMEM((4, SHARD, FEAT), BF),
            pltpu.VMEM((SHARD, WIN), BF),
            pltpu.VMEM((SHARD, WIN), BF),
            pltpu.VMEM((SHARD, WIN), BF),
            pltpu.VMEM((4, 4, SHARE, FEAT), BF),
            pltpu.VMEM((3, 4, SHARE, FEAT), BF),
            pltpu.VMEM((3, 4, PADF, WIN), BF),
            pltpu.VMEM((3, 4, 128, WIN), BF),
            pltpu.VMEM((3, 4, 128, WIN), F32),
            pltpu.VMEM((3, 4, 128, WIN), BF),
            pltpu.VMEM((3, 4, 96, WIN), BF),
            pltpu.VMEM((3, 4, 64, WIN), BF),
            pltpu.VMEM((3, 4, 48, WIN), BF),
            dma((2, 3)),
            dma((2, 3)),
            dma((2, 5, 3)),
            dma((2, 3, 3, 3)),
            dma((2, 5)),
            dma((2, 3)),
            dma((2, 4)),
            dma((2,)),
            dma((2, 4)),
            dma((2, 3, 2)),
            dma((2, 2)),
            dma((2, 3, 3, 3)),
            dma((5,)),
        ],
        0,
    )(*operands)


def back_kernel(
    second_ref,
    mid_ref,
    cot_ref,
    x_ref,
    nf_ref,
    q_ref,
    kv_ref,
    lse_ref,
    att_ref,
    proj_full,
    outw_full,
    gains_full,
    cos_ref,
    sin_ref,
    start_ref,
    ff_ref,
    op_ref,
    block_out,
    input_out,
    ff_out,
    outw_out,
    proj_out,
    small_out,
    mask,
    g_mid,
    g_branch,
    g_att,
    dq,
    dk,
    dv,
    dkv,
    dkv_in,
    gp,
    gv,
    c_send,
    c_in,
    op_in,
    co_send,
    co_in,
    own_input,
    outw_grad,
    proj_grad,
    small,
    small_in,
    small_x,
    small_z,
    core_in,
    part,
    low_buf,
    in1,
    low2,
    in2,
    mine,
    z_in,
    ff_z,
    sem_flow,
    sem_ff,
    sem_kv,
    sem_c,
    sem_in,
    sem_s,
    sem_op,
    sem_co,
):
    d = lax.axis_index("dp")
    r = lax.axis_index("row")
    c = lax.axis_index("col")
    core = lax.rem(d, 2)
    y = lax.rem(d // 2, 2)
    x = d // 4
    sibling = d + 1 - 2 * core
    other_y = d + 2 - 4 * y
    x_peers = [(k, lax.rem(x + k, 4) * 4 + lax.rem(d, 4)) for k in (1, 2, 3)]
    row_peers = [(k, lax.rem(r + k, 4)) for k in (1, 2, 3)]
    block = 4 * d + r
    near = lambda i: {
        "dp": lax.rem((block + 64 + i) // 4, 16),
        "row": lax.rem(r + 4 + i, 4),
    }
    greet(
        [{"row": q} for _, q in row_peers]
        + [{"dp": p} for _, p in x_peers]
        + [{"col": 1 - c}, {"dp": sibling}, {"dp": other_y}]
        + [near(i) for i in (1, 2, 3, 4, -1, -2, -3, -4)]
    )
    pending = []

    def go(*args, **device):
        copy = rcopy(*args, **device)
        copy.start()
        pending.append(copy)
        return copy

    span = lambda q: pl.ds(pl.multiple_of(q * SHARE, SHARE), SHARE)
    buffers = (core_in, part, low_buf, in1, low2, in2, mine, z_in)
    flows = [
        GradSum(t, source, out, joined, wide_first, (r, d), buffers, sem_flow, go)
        for t, source, out, joined, wide_first in (
            (0, outw_grad, outw_out, False, True),
            (1, proj_grad, proj_out, False, True),
        )
    ]
    out, tail = flows
    spare = (None,) * 6 + (ff_ref, ff_z)
    ff = [
        GradSum(t, None, ff_out.at[t], True, True, (r, d), spare, sem_ff, go)
        for t in range(3)
    ]
    for flow in ff:
        flow.cross_rows()
        flow.done = 4

    def scatter(k, q):
        return go(
            op_ref.at[q], op_in.at[k - 1], sem_op.at[0, k - 1], sem_op.at[1, k - 1], row=q
        )

    op_copies = [scatter(*row_peers[0]), scatter(*row_peers[2])]

    small[...] = jnp.zeros_like(small)
    square = jnp.zeros((SHARE, 1), F32)
    inner = jnp.zeros((SHARE, 1), F32)
    for j in range(4):
        value = mid_ref[j]
        square += jnp.sum(value * value, axis=1, keepdims=True)
        inner += jnp.sum(second_ref[j] * gains_full[j, 1:2, :] * value, axis=1, keepdims=True)
    rate = lax.rsqrt(square / D + EPS)
    scale = rate * rate * rate * inner / D
    for j in range(4):
        value = mid_ref[j]
        grad = second_ref[j]
        small[j, 1:2, 0:FEAT] = jnp.sum(grad * value * rate, axis=0, keepdims=True)
        total = (
            cot_ref[j].astype(F32)
            + rate * (grad * gains_full[j, 1:2, :])
            - value * scale
        )
        g_mid[j] = total
        g_branch[j] = total.astype(BF)
    grad_att = dot_nt(g_branch[0], outw_full[0])
    for j in range(1, 4):
        grad_att += dot_nt(g_branch[j], outw_full[j])
    g_att[:, 448:512] = jnp.zeros((SHARE, 64), BF)
    g_att[:, 0:448] = grad_att.astype(BF)
    for flow in ff:
        flow.step()
    outw_grad[...] = jnp.zeros_like(outw_grad)
    for j in range(4):
        outw_grad[j, 0:FEAT, 0:448] = dot_tn(g_branch[j], att_ref[...]).astype(BF)
    out.step()
    query_at = lax.broadcasted_iota(jnp.int32, (SHARE, 1), 0) + MAXLEN
    key_at = lax.broadcasted_iota(jnp.int32, (SHARE, MAXLEN + SHARE), 1)
    mask[...] = jnp.where(
        (key_at >= start_ref[...]) & (key_at <= query_at), 0.0, -1e30
    )

    lane = lax.broadcasted_iota(jnp.int32, (SHARE, 128), 1)
    low = lane < 64
    for m in range(HEADS // GROUPS):
        at = 128 * (m // 2)
        mine_lanes = low if m % 2 == 0 else jnp.logical_not(low)
        pick = lambda ref: jnp.where(
            mine_lanes, ref[:, at : at + 128].astype(F32), 0.0
        ).astype(BF)
        query, grad = pick(q_ref), pick(g_att)
        probs = jnp.exp(dot_nt(query, kv_ref[0]) + mask[...] - lse_ref[m])
        grad_probs = dot_nt(grad, kv_ref[1])
        inner = jnp.sum(probs * grad_probs, axis=1, keepdims=True)
        grad_scores = (probs * (grad_probs - inner)).astype(BF)
        grad_v = dot_tn(probs.astype(BF), grad)
        grad_k = dot_tn(grad_scores, query)
        if m == 0:
            dv[...] = grad_v
            dk[...] = grad_k
        else:
            dv[...] += grad_v
            dk[...] += grad_k
        grad_q = dot(grad_scores, kv_ref[0]) * HEAD_DIM ** (-0.5)
        if m % 2 == 0:
            dq[:, at : at + 128] = grad_q
        else:
            dq[:, at : at + 128] = jnp.where(low, dq[:, at : at + 128], grad_q)
        if m == 1:
            out.step()
            for flow in ff:
                flow.step()
    wide_low = lax.broadcasted_iota(jnp.int32, (MAXLEN + SHARE, 128), 1) < 64
    dkv[...] = jnp.where(
        wide_low,
        dk[...] + pltpu.roll(dk[...], 64, 1),
        dv[...] + pltpu.roll(dv[...], 64, 1),
    ).astype(BF)
    kv_copies = [
        go(
            dkv.at[(4 - i) * SHARE : (5 - i) * SHARE, :],
            dkv_in.at[i - 1],
            sem_kv.at[0, i - 1],
            sem_kv.at[1, i - 1],
            **near(-i),
        )
        for i in (1, 2, 3, 4)
    ]
    out.step()
    total = dkv[MAXLEN : MAXLEN + SHARE, :].astype(F32)
    for i in (1, 2, 3, 4):
        kv_copies[i - 1].wait_recv()
        total += dkv_in[i - 1].astype(F32)
    op_copies.append(scatter(*row_peers[1]))
    turned = pltpu.roll(total, 64, 1)
    dq[:, 384:512] = jnp.where(low, dq[:, 384:512], turned)
    gv[...] = turned[:, 0:64].astype(BF)
    cosine = jnp.concatenate([cos_ref[...]] * 4, axis=1)
    sine = jnp.concatenate([sin_ref[...]] * 4, axis=1)
    gp[...] = (dq[...] * cosine - swapped(dq[...]) * sine).astype(BF)
    for j in range(4):
        c_send[j] = (
            dot_nt(gp[...], proj_full[j, :, 0:512])
            + dot_nt(gv[...], proj_full[j, :, 512:576])
        ).astype(BF)
    cross = go(c_send, c_in, sem_c.at[0], sem_c.at[1], col=1 - c)
    proj_grad[...] = jnp.zeros_like(proj_grad)
    for j in range(4):
        proj_grad[j, 0:FEAT, 0:512] = dot_tn(nf_ref[j], gp[...]).astype(BF)
        proj_grad[j, 0:FEAT, 512:576] = dot_tn(nf_ref[j], gv[...]).astype(BF)
    tail.step()
    bias_a = jnp.sum(gp[...].astype(F32), axis=0, keepdims=True)
    bias_b = jnp.sum(gv[...].astype(F32), axis=0, keepdims=True)
    for j in range(4):
        small[j, 2:3, 0:512] = bias_a
        small[j, 2:3, 512:576] = bias_b
    out.step()
    tail.step()
    for flow in ff:
        flow.step()
    tail.step()
    out.step()
    tail.step()

    square = jnp.zeros((SHARE, 1), F32)
    for j in range(4):
        value = x_ref[j].astype(F32)
        square += jnp.sum(value * value, axis=1, keepdims=True)
    rate = lax.rsqrt(square / D + EPS)
    cross.wait_recv()
    inner = jnp.zeros((SHARE, 1), F32)
    for j in range(4):
        grad = c_send[j].astype(F32) + c_in[j].astype(F32)
        inner += jnp.sum(
            grad * gains_full[j, 0:1, :] * x_ref[j].astype(F32), axis=1, keepdims=True
        )
    scale = rate * rate * rate * inner / D
    for j in range(4):
        value = x_ref[j].astype(F32)
        grad = c_send[j].astype(F32) + c_in[j].astype(F32)
        small[j, 0:1, 0:FEAT] = jnp.sum(grad * value * rate, axis=0, keepdims=True)
        own_input[j] = (
            g_mid[j] + rate * (grad * gains_full[j, 0:1, :]) - value * scale
        ).astype(BF)
    in_copies = [
        go(
            own_input.at[q],
            input_out.at[r],
            sem_in.at[0, k - 1],
            sem_in.at[1, k - 1],
            row=q,
        )
        for k, q in row_peers
    ]
    input_out[r] = own_input[r]

    total = op_ref[r].astype(F32)
    for copy in op_copies:
        copy.wait_recv()
    for k in range(3):
        total += op_in[k].astype(F32)
    co_send[...] = total.astype(BF)
    final = go(co_send, co_in, sem_co.at[0], sem_co.at[1], col=1 - c)

    def swap(stage, source, target, k, **device):
        return go(source, target, sem_s.at[0, stage, k - 1], sem_s.at[1, stage, k - 1], **device)

    copy = swap(0, small, small_in.at[0], 1, dp=sibling)
    out.step()
    tail.step()
    copy.wait_recv()
    small_x[0] = small[...] + small_in[0]
    copies = [swap(1, small_x.at[0], small_in.at[k], k, dp=p) for k, p in x_peers]
    out.step()
    tail.step()
    for copy in copies:
        copy.wait_recv()
    small_x[1] = small_x[0] + small_in[1] + small_in[2] + small_in[3]
    copy = swap(2, small_x.at[1], small_in.at[4], 1, dp=other_y)
    tail.step()
    copy.wait_recv()
    small_x[2] = small_x[1] + small_in[4]
    copies = [swap(3, small_x.at[2, q], small_z.at[r], k, row=q) for k, q in row_peers]
    small_z[r] = small_x[2, r]
    for copy in copies:
        copy.wait_recv()
    small_out[...] = small_z[0] + small_z[1] + small_z[2] + small_z[3]
    tail.step()
    out.step()
    for flow in ff:
        flow.step()
    for copy in in_copies:
        copy.wait_recv()
    final.wait_recv()
    block_out[...] = (co_send[...].astype(F32) + co_in[...].astype(F32)).astype(BF)
    for copy in pending:
        copy.wait_send()


def back(*operands):
    dma = pltpu.SemaphoreType.DMA
    shape = jax.ShapeDtypeStruct
    width = MAXLEN + SHARE
    blocked = pltpu.VMEM((4, SHARE, FEAT), BF)
    count = 2
    return vmem_call(
        back_kernel,
        17,
        (
            shape((SHARD, FEAT), BF),
            shape((4, SHARE, FEAT), BF),
            shape((3, PADF, HALF_FF), BF),
            shape((PADF, WIN), BF),
            shape((PADF, WIN), BF),
            shape((8, WIN), F32),
        ),
        [
            pltpu.VMEM((SHARE, width), F32),
            pltpu.VMEM((4, SHARE, FEAT), F32),
            blocked,
            pltpu.VMEM((SHARE, 512), BF),
            pltpu.VMEM((SHARE, 512), F32),
            pltpu.VMEM((width, 128), F32),
            pltpu.VMEM((width, 128), F32),
            pltpu.VMEM((width, 128), BF),
            pltpu.VMEM((4, SHARE, 128), BF),
            pltpu.VMEM((SHARE, 512), BF),
            pltpu.VMEM((SHARE, 64), BF),
            blocked,
            blocked,
            pltpu.VMEM((3, SHARD, FEAT), BF),
            pltpu.VMEM((SHARD, FEAT), BF),
            pltpu.VMEM((SHARD, FEAT), BF),
            blocked,
            pltpu.VMEM((4, PADF, WIN), BF),
            pltpu.VMEM((4, PADF, WIN), BF),
            pltpu.VMEM((4, 8, WIN), F32),
            pltpu.VMEM((5, 4, 8, WIN), F32),
            pltpu.VMEM((3, 4, 8, WIN), F32),
            pltpu.VMEM((4, 8, WIN), F32),
            pltpu.VMEM((count, 4, 128, WIN), BF),
            pltpu.VMEM((count, 4, 128, WIN), F32),
            pltpu.VMEM((count, 4, 128, WIN), BF),
            pltpu.VMEM((count, 4, 96, WIN), BF),
            pltpu.VMEM((count, 4, 64, WIN), BF),
            pltpu.VMEM((count, 4, 48, WIN), BF),
            pltpu.VMEM((count, 4, 16, WIN), BF),
            pltpu.VMEM((count, 4, 16, WIN), BF),
            pltpu.VMEM((3, 4, 16, WIN), BF),
            dma((2, count, 7, 3)),
            dma((2, 3, 7, 3)),
            dma((2, 4)),
            dma((2,)),
            dma((2, 3)),
            dma((2, 4, 3)),
            dma((2, 3)),
            dma((2,)),
        ],
        1,
    )(*operands)


def body(
    activations,
    starts,
    first_gain,
    project_weight,
    project_bias,
    output_weight,
    second_gain,
    gate_weight,
    up_weight,
    down_weight,
    cotangent,
):
    r = lax.axis_index("row")
    shard = lax.axis_index("dp")
    query_width = HEADS // GROUPS * HEAD_DIM

    base = shard * SHARD + r * SHARE
    start_window = (
        lax.dynamic_slice_in_dim(starts, r * SHARE, SHARE, 0) - base + MAXLEN
    )[:, None]
    positions = (MAXLEN + jnp.arange(SHARE, dtype=jnp.int32))[:, None] - start_window
    half = HEAD_DIM // 2
    freqs = 1000000.0 ** (-jnp.arange(half, dtype=F32) * 2.0 / HEAD_DIM)
    angle = positions.astype(F32) * jnp.tile(freqs, 4)[None, :]
    cosine = jnp.cos(angle)
    sine = jnp.sin(angle) * jnp.tile(jnp.repeat(jnp.array([-1.0, 1.0], F32), half), 2)[None, :]
    gains = jnp.pad(jnp.stack([first_gain, second_gain]), ((0, 6), (0, 0)))
    (
        x_low,
        normed_first,
        queries,
        kv,
        lse,
        attended,
        middle,
        project_full,
        output_full,
        gains_full,
        cot_own,
        grad_second,
        out_partial,
        ff_part,
    ) = forward(
        activations,
        cotangent,
        project_weight,
        output_weight,
        gate_weight,
        up_weight,
        down_weight,
        gains,
        project_bias[None, :],
        cosine,
        sine,
        start_window,
    )
    block_output, input_grad, ff_sum, outw_sum, project_sum, small = back(
        grad_second,
        middle,
        cot_own,
        x_low,
        normed_first,
        queries,
        kv,
        lse,
        attended,
        project_full,
        output_full,
        gains_full,
        cosine,
        sine,
        start_window,
        ff_part,
        out_partial,
    )
    width = project_weight.shape[1]
    ff_sum = ff_sum[:, :FEAT].astype(F32)
    return (
        block_output,
        input_grad.reshape(SHARD, FEAT).astype(F32),
        small[0, :FEAT],
        project_sum[:FEAT, :width].astype(F32),
        small[2, :width],
        outw_sum[:FEAT, :query_width].astype(F32).T,
        small[1, :FEAT],
        ff_sum[0],
        ff_sum[1],
        ff_sum[2].T,
    )


def solution(mesh):
    return jax.shard_map(
        body,
        mesh=mesh,
        in_specs=(
            P("dp", "row"),
            P("dp"),
            P("row"),
            P("row", "col"),
            P("col"),
            P("col", "row"),
            P("row"),
            P("row", "col"),
            P("row", "col"),
            P("col", "row"),
            P("dp", "row"),
        ),
        out_specs=(
            P("dp", "row"),
            P("dp", "row"),
            P("row"),
            P("row", "col"),
            P("col"),
            P("col", "row"),
            P("row"),
            P("row", "col"),
            P("row", "col"),
            P("col", "row"),
        ),
        check_vma=False,
    )
```

```python
import functools

import jax
import jax.numpy as jnp
from jax import lax
from jax.experimental import pallas as pl
from jax.experimental.pallas import tpu as pltpu
from jax.sharding import PartitionSpec as P

D = 896
HEADS = 14
GROUPS = 2
HEAD_DIM = 64
MAXLEN = 1024
EPS = 1e-06
BF = jnp.bfloat16
F32 = jnp.float32
ROWS = 4
FEAT = 224
SHARE = 256
SHARD = 1024
HALF_FF = 2432
WIN = 640
LAST = HALF_FF - WIN
PADF = 256
VMEM_LIMIT = 60 * 1024 * 1024


def dot(a, b):
    return jnp.dot(a, b, preferred_element_type=F32)


def dot_nt(a, b):
    return lax.dot_general(a, b, (((1,), (1,)), ((), ())), preferred_element_type=F32)


def dot_tn(a, b):
    return lax.dot_general(a, b, (((0,), (0,)), ((), ())), preferred_element_type=F32)


def rcopy(src, dst, send, recv, **device):
    return pltpu.make_async_remote_copy(
        src_ref=src,
        dst_ref=dst,
        send_sem=send,
        recv_sem=recv,
        device_id=device,
        device_id_type=pl.DeviceIdType.MESH,
    )


def greet(peers):
    barrier = pltpu.get_barrier_semaphore()
    for peer in peers:
        pl.semaphore_signal(
            barrier, inc=1, device_id=peer, device_id_type=pl.DeviceIdType.MESH
        )
    pl.semaphore_wait(barrier, len(peers))


def vmem_call(kernel, inputs, outs, scratch, collective, cost=None):
    return pl.pallas_call(
        kernel,
        out_shape=outs,
        in_specs=[pl.BlockSpec(memory_space=pltpu.VMEM)] * inputs,
        out_specs=jax.tree.map(lambda _: pl.BlockSpec(memory_space=pltpu.VMEM), outs),
        scratch_shapes=scratch,
        compiler_params=pltpu.CompilerParams(
            collective_id=collective,
            has_side_effects=True,
            vmem_limit_bytes=VMEM_LIMIT,
        ),
        cost_estimate=cost,
    )


class GradSum:
    def __init__(self, t, source, out, joined, wide_first, place, buffers, sems, go):
        self.t, self.source, self.out, self.joined, self.go = t, source, out, joined, go
        self.r, d = place
        self.core = lax.rem(d, 2)
        y = lax.rem(d // 2, 2)
        x = d // 4
        self.sibling = d + 1 - 2 * self.core
        along_x = [
            (k, lax.rem(x + k, 4), lax.rem(x + k, 4) * 4 + lax.rem(d, 4)) for k in (1, 2, 3)
        ]
        along_y = [(1, 1 - y, d + 2 - 4 * y)]
        if wide_first:
            self.first, self.second = (along_x, x, 32), (along_y, y, 16)
        else:
            self.first, self.second = (along_y, y, 64), (along_x, x, 16)
        self.at_first = self.core * 128 + self.first[1] * self.first[2]
        self.at = self.at_first + self.second[1] * 16
        self.core_in, self.part, self.low, self.in1, self.low2, self.in2, self.mine, self.z_in = [
            buffer.at[t] if buffer is not None else None for buffer in buffers
        ]
        self.sem = lambda stage, k: (sems.at[0, t, stage, k - 1], sems.at[1, t, stage, k - 1])
        self.waiting = []
        self.done = 0

    def rows(self, start, size):
        return pl.ds(pl.multiple_of(start, 16), size)

    def settle(self):
        for copy in self.waiting:
            copy.wait_recv()
        self.waiting = []

    def send(self, source, target, stage, k, **device):
        self.waiting.append(self.go(source, target, *self.sem(stage, k), **device))

    def step(self):
        self.settle()
        getattr(self, "step%d" % self.done)()
        self.done += 1

    def step0(self):
        self.send(
            self.source.at[:, self.rows((1 - self.core) * 128, 128), :],
            self.core_in,
            0,
            1,
            dp=self.sibling,
        )

    def step1(self):
        peers, own, unit = self.first
        total = self.source[:, self.rows(self.core * 128, 128), :].astype(F32)
        total = total + self.core_in[...].astype(F32)
        self.part[...] = total
        self.low[...] = total.astype(BF)
        for k, index, device in peers:
            self.send(
                self.low.at[:, self.rows(index * unit, unit), :],
                self.in1.at[:, (k - 1) * unit : k * unit, :],
                1,
                k,
                dp=device,
            )

    def step2(self):
        peers, own, unit = self.first
        total = self.part[:, self.rows(own * unit, unit), :]
        for k, _, _ in peers:
            total = total + self.in1[:, (k - 1) * unit : k * unit, :].astype(F32)
        self.part[:, 0:unit, :] = total
        self.low2[:, 0:unit, :] = total.astype(BF)
        peers, own, unit = self.second
        for k, index, device in peers:
            self.send(
                self.low2.at[:, self.rows(index * unit, unit), :],
                self.in2.at[:, (k - 1) * unit : k * unit, :],
                2,
                k,
                dp=device,
            )

    def step3(self):
        self.reduce()
        self.cross_rows()

    def reduce(self):
        self.settle()
        peers, own, unit = self.second
        total = self.part[:, self.rows(own * unit, unit), :]
        for k, _, _ in peers:
            total = total + self.in2[:, (k - 1) * unit : k * unit, :].astype(F32)
        self.mine[...] = total.astype(BF)

    def cross_rows(self):
        for k in (1, 2, 3):
            q = lax.rem(self.r + k, 4)
            self.send(self.mine.at[q], self.z_in.at[self.r], 3, k, row=q)
        self.z_in[self.r] = self.mine[self.r]

    def step4(self):
        here = self.rows(self.at, 16)
        if self.joined:
            for q in range(3):
                self.out[here, q * WIN : (q + 1) * WIN] = self.z_in[q]
            self.out[here, 3 * WIN : HALF_FF] = self.z_in[3][:, 4 * WIN - HALF_FF :]
        else:
            total = self.z_in[0].astype(F32)
            for q in range(1, 4):
                total = total + self.z_in[q].astype(F32)
            self.out[here, :] = total.astype(BF)
        self.spread(self.second[0], self.at, 16, 4)

    def spread(self, peers, start, size, stage):
        block = self.out.at[self.rows(start, size), :]
        for k, _, device in peers:
            self.send(block, block, stage, k, dp=device)

    def step5(self):
        self.spread(self.first[0], self.at_first, self.first[2], 5)

    def step6(self):
        self.spread([(1, 0, self.sibling)], self.core * 128, 128, 6)

    def step7(self):
        pass


def swapped(values):
    width = values.shape[1]
    lane = lax.broadcasted_iota(jnp.int32, values.shape, 1)
    return jnp.where(
        lax.rem(lane, 64) < 32,
        pltpu.roll(values, width - 32, 1),
        pltpu.roll(values, 32, 1),
    )


def forward_kernel(
    act_ref,
    cot_ref,
    proj_ref,
    outw_ref,
    gate_ref,
    up_ref,
    down_ref,
    gains_ref,
    bias_ref,
    cos_ref,
    sin_ref,
    start_ref,
    x_out,
    nf_out,
    q_out,
    kv_out,
    lse_out,
    att_out,
    mid_out,
    proj_full,
    outw_full,
    gains_full,
    cot_out,
    second_out,
    op_out,
    mine_out,
    gate_full,
    up_full,
    down_full,
    cot_all,
    mask,
    own_kv,
    c_send,
    c_in,
    second_in,
    ns_all,
    hid,
    gg,
    gu,
    sp_send,
    sp_in,
    grads,
    core_in,
    part,
    low_buf,
    in1,
    low2,
    in2,
    sem_x,
    sem_g,
    sem_w,
    sem_wx,
    sem_wc,
    sem_cot,
    sem_kv,
    sem_c,
    sem_ag,
    sem_sp,
    sem_cs,
    sem_flow,
    sem_l,
):
    d = lax.axis_index("dp")
    r = lax.axis_index("row")
    c = lax.axis_index("col")
    core = lax.rem(d, 2)
    x_at = d // 4
    sibling = d + 1 - 2 * core
    other_y = d + 2 - 4 * lax.rem(d // 2, 2)
    x_peers = [(k, lax.rem(x_at + k, 4) * 4 + lax.rem(d, 4)) for k in (1, 2, 3)]
    block = 4 * d + r
    near = lambda i: {
        "dp": lax.rem((block + 64 + i) // 4, 16),
        "row": lax.rem(r + 4 + i, 4),
    }
    greet(
        [{"row": lax.rem(r + k, 4)} for k in (1, 2, 3)]
        + [{"dp": p} for _, p in x_peers]
        + [{"col": 1 - c}, {"dp": sibling}, {"dp": other_y}]
        + [near(i) for i in (1, 2, 3, 4, -1, -2, -3, -4)]
    )
    pending = []

    def go(*args, **device):
        copy = rcopy(*args, **device)
        copy.start()
        pending.append(copy)
        return copy

    peers = [(k, lax.rem(r + k, 4)) for k in (1, 2, 3)]
    span = lambda q: pl.ds(pl.multiple_of(q * SHARE, SHARE), SHARE)
    offset = lambda q: pl.multiple_of(jnp.minimum(q * WIN, LAST), 128)
    half = lambda n: pl.ds(pl.multiple_of(core * n, 16), n)

    def down_rows(q):
        return pl.ds(pl.multiple_of(offset(q) + core * (WIN // 2), 16), WIN // 2)

    pieces = (
        (lambda q: proj_ref.at[half(112), :], proj_full, 112),
        (lambda q: outw_ref.at[half(224), :], outw_full, 224),
        (lambda q: gate_ref.at[half(112), pl.ds(offset(q), WIN)], gate_full, 112),
        (lambda q: up_ref.at[half(112), pl.ds(offset(q), WIN)], up_full, 112),
        (lambda q: down_ref.at[down_rows(q), :], down_full, WIN // 2),
    )

    def crossing(w):
        source, full, n = pieces[w]
        return [
            rcopy(
                source(q),
                full.at[r, half(n), :],
                sem_w.at[0, w, k - 1],
                sem_w.at[1, w, k - 1],
                row=q,
            )
            for k, q in peers
        ]

    def passing(w):
        _, full, n = pieces[w]
        copies = []
        for k, q in peers:
            part = full.at[q, half(n), :]
            for e, device in x_peers:
                copies.append(
                    rcopy(
                        part,
                        part,
                        sem_wx.at[0, w - 2, k - 1, e - 1],
                        sem_wx.at[1, w - 2, k - 1, 0],
                        dp=device,
                    )
                )
        return copies

    def fetch(w):
        source, full, n = pieces[w]
        local = pltpu.make_async_copy(source(r), full.at[r, half(n), :], sem_l.at[w])
        local.start()
        copies = crossing(w)
        if w < 2:
            for copy in copies:
                copy.start()
                pending.append(copy)
        else:

            @pl.when(x_at == w - 2)
            def _():
                for copy in copies:
                    copy.start()

        return copies, local

    def pass_on(w, fetched):
        @pl.when(x_at == w - 2)
        def _():
            for copy in fetched[0]:
                copy.wait_recv()
            for copy in passing(w):
                copy.start()

    def share(w, fetched):
        _, full, n = pieces[w]
        copies, local = fetched
        local.wait()
        if w < 2:
            for copy in copies:
                copy.wait_recv()
        else:

            @pl.when(x_at != w - 2)
            def _():
                for copy in passing(w)[::3]:
                    copy.wait_recv()

        part = full.at[:, half(n), :]
        copy = rcopy(part, part, sem_wc.at[0, w], sem_wc.at[1, w], dp=sibling)
        copy.start()
        if w < 2:
            pending.append(copy)
        return copy

    def finish(w, fetched):
        @pl.when(x_at == w - 2)
        def _():
            for copy in fetched[0] + passing(w):
                copy.wait_send()

    x_copies = [
        go(
            act_ref.at[span(q), :],
            x_out.at[r],
            sem_x.at[0, k - 1],
            sem_x.at[1, k - 1],
            row=q,
        )
        for k, q in peers
    ]
    g_copies = [
        go(gains_ref, gains_full.at[r], sem_g.at[0, k - 1], sem_g.at[1, k - 1], row=q)
        for k, q in peers
    ]
    fetched = {0: fetch(0)}
    x_out[r] = act_ref[span(r), :]
    gains_full[r] = gains_ref[...]
    query_at = lax.broadcasted_iota(jnp.int32, (SHARE, 1), 0) + MAXLEN
    key_at = lax.broadcasted_iota(jnp.int32, (SHARE, MAXLEN + SHARE), 1)
    mask[...] = jnp.where(
        (key_at >= start_ref[...]) & (key_at <= query_at), 0.0, -1e30
    )
    shared = {0: share(0, fetched[0])}
    for copy in x_copies + g_copies:
        copy.wait_recv()
    for w in (1, 2, 3, 4):
        fetched[w] = fetch(w)
    cot_all[r] = cot_ref[...]
    square = jnp.zeros((SHARE, 1), F32)
    for j in range(4):
        value = x_out[j].astype(F32)
        square += jnp.sum(value * value, axis=1, keepdims=True)
    rate = lax.rsqrt(square / D + EPS)
    for j in range(4):
        nf_out[j] = (x_out[j].astype(F32) * rate * gains_full[j, 0:1, :]).astype(BF)
    shared[0].wait_recv()
    projected = dot(nf_out[0], proj_full[0, :, 0:512])
    values = dot(nf_out[0], proj_full[0, :, 512:576])
    for j in range(1, 4):
        projected += dot(nf_out[j], proj_full[j, :, 0:512])
        values += dot(nf_out[j], proj_full[j, :, 512:576])
    projected += bias_ref[:, 0:512]
    values = (values + bias_ref[:, 512:576]).astype(BF)
    cosine = jnp.concatenate([cos_ref[...]] * 4, axis=1)
    sine = jnp.concatenate([sin_ref[...]] * 4, axis=1)
    turned = projected * cosine + swapped(projected) * sine
    q_out[...] = (turned * HEAD_DIM ** (-0.5)).astype(BF)
    tile = turned[:, 384:512]
    lane = lax.broadcasted_iota(jnp.int32, (SHARE, 128), 1)
    low = lane < 64
    own_kv[0] = jnp.where(low, pltpu.roll(tile, 64, 1), tile).astype(BF)
    double = (
        lax.rem(lax.broadcasted_iota(jnp.int32, (64, 128), 1), 64)
        == lax.broadcasted_iota(jnp.int32, (64, 128), 0)
    ).astype(F32).astype(BF)
    own_kv[1] = dot(values, double).astype(BF)
    kv_copies = [
        go(
            own_kv,
            kv_out.at[:, (4 - i) * SHARE : (5 - i) * SHARE, :],
            sem_kv.at[0, i - 1],
            sem_kv.at[1, i - 1],
            **near(i),
        )
        for i in (1, 2, 3, 4)
    ]
    kv_out[:, MAXLEN : MAXLEN + SHARE, :] = own_kv[...]
    for w in (2, 3, 4):
        pass_on(w, fetched[w])
    for copy in kv_copies:
        copy.wait_recv()
    cot_copies = [
        go(cot_ref, cot_all.at[r], sem_cot.at[0, k - 1], sem_cot.at[1, k - 1], row=q)
        for k, q in (peers[0], peers[2], peers[1])
    ]
    for m in range(HEADS // GROUPS):
        at = 128 * (m // 2)
        mine = low if m % 2 == 0 else jnp.logical_not(low)
        query = jnp.where(mine, q_out[:, at : at + 128].astype(F32), 0.0).astype(BF)
        scores = dot_nt(query, kv_out[0]) + mask[...]
        peak = jnp.max(scores, axis=1, keepdims=True)
        powered = jnp.exp(scores - peak)
        total = jnp.sum(powered, axis=1, keepdims=True)
        probs = (powered * (1.0 / total)).astype(BF)
        lse_out[m] = peak + jnp.log(total)
        mixed = dot(probs, kv_out[1])
        if m == 6:
            att_out[:, 384:448] = mixed[:, 0:64].astype(BF)
        elif m % 2 == 0:
            even = mixed
        else:
            att_out[:, at : at + 128] = jnp.where(low, even, mixed).astype(BF)
    shared[1] = share(1, fetched[1])
    shared[1].wait_recv()
    for j in range(4):
        c_send[j] = dot(att_out[...], outw_full[j]).astype(BF)
    cross = rcopy(c_send, c_in, sem_c.at[0], sem_c.at[1], col=1 - c)
    cross.start()
    for w in (2, 3, 4):
        shared[w] = share(w, fetched[w])
    cross.wait_recv()
    square = jnp.zeros((SHARE, 1), F32)
    for j in range(4):
        value = x_out[j].astype(F32) + (
            c_send[j].astype(F32) + c_in[j].astype(F32)
        )
        mid_out[j] = value
        square += jnp.sum(value * value, axis=1, keepdims=True)
    rate = lax.rsqrt(square / D + EPS)
    for j in range(4):
        ns_all[j, span(r), :] = (mid_out[j] * rate * gains_full[j, 1:2, :]).astype(BF)

    right, across, left = [q for _, q in peers]

    def spread(blocks, source, index, q):
        part = ns_all.at[blocks, span(source), :]
        return go(part, part, sem_ag.at[0, index], sem_ag.at[1, index], row=q)

    every, front_half, back_half = pl.ds(0, 4), pl.ds(0, 2), pl.ds(2, 2)
    from_left = spread(every, r, 0, right)
    from_right = spread(every, r, 1, left)
    for copy in cot_copies:
        copy.wait_recv()
    for w in (2, 3, 4):
        shared[w].wait_recv()
        shared[w].wait_send()
        finish(w, fetched[w])
    live = jnp.where(r < 3, 1.0, 0.0)
    extra = 4 * WIN - HALF_FF
    for j in range(4):
        gate_full[j, :, 0:extra] = (gate_full[j, :, 0:extra].astype(F32) * live).astype(BF)
        up_full[j, :, 0:extra] = (up_full[j, :, 0:extra].astype(F32) * live).astype(BF)
        cot_out[j] = cot_all[j, span(r), :]

    def feed(k, q, arrived):
        grad_hidden = dot_nt(cot_all[0, span(q), :], down_full[0])
        for j in range(1, 4):
            grad_hidden += dot_nt(cot_all[j, span(q), :], down_full[j])
        arrived()
        gate = dot(ns_all[0, span(q), :], gate_full[0])
        up = dot(ns_all[0, span(q), :], up_full[0])
        for j in range(1, 4):
            gate += dot(ns_all[j, span(q), :], gate_full[j])
            up += dot(ns_all[j, span(q), :], up_full[j])
        sigma = 1.0 / (1.0 + jnp.exp(-gate))
        silu = gate * sigma
        hid[span(q), :] = (silu * up).astype(BF)
        g_gate = (grad_hidden * up * (sigma + silu * (1.0 - sigma))).astype(BF)
        g_up = (grad_hidden * silu).astype(BF)
        gg[span(q), :] = g_gate
        gu[span(q), :] = g_up
        copies = []
        for j in range(4):
            sp_send[k, j] = (
                dot_nt(g_gate, gate_full[j]) + dot_nt(g_up, up_full[j])
            ).astype(BF)
            if k and j % 2:
                copies.append(
                    go(
                        sp_send.at[k, j - 1 : j + 1],
                        sp_in.at[k - 1, j - 1 : j + 1],
                        sem_sp.at[0, k - 1, j // 2],
                        sem_sp.at[1, k - 1, j // 2],
                        row=q,
                    )
                )
        return copies

    forwarded = []

    def neighbours_here():
        from_left.wait_recv()
        forwarded.append(spread(front_half, left, 2, right))
        from_right.wait_recv()
        forwarded.append(spread(back_half, right, 3, left))

    def opposite_here():
        for copy in forwarded:
            copy.wait_recv()

    feed(0, r, lambda: None)
    back = {}
    back[1] = feed(1, right, neighbours_here)
    back[3] = feed(3, left, lambda: None)
    back[2] = feed(2, across, opposite_here)

    buffers = (core_in, part, low_buf, in1, low2, in2, mine_out, None)
    flows = [
        GradSum(t, grads.at[t], None, True, True, (r, d), buffers, sem_flow, go)
        for t in range(3)
    ]
    grads[:, :, FEAT:PADF, :] = jnp.zeros((3, 4, PADF - FEAT, WIN), BF)
    for t, left_side, right_side in ((0, ns_all, gg), (1, ns_all, gu), (2, cot_all, hid)):
        for j in range(4):
            grads[t, j, 0:FEAT, :] = dot_tn(left_side[j], right_side[...]).astype(BF)
        flows[t].step()
        if t:
            flows[t - 1].step()
    flows[2].step()
    cross.wait_send()
    crosses = []
    for h in (0, 2):
        total = sp_send[0, h : h + 2].astype(F32)
        for k in (1, 3, 2):
            back[k][h // 2].wait_recv()
            total += sp_in[k - 1, h : h + 2].astype(F32)
        c_send[h : h + 2] = total.astype(BF)
        crosses.append(
            go(
                c_send.at[h : h + 2],
                second_in.at[h : h + 2],
                sem_cs.at[0, h // 2],
                sem_cs.at[1, h // 2],
                col=1 - c,
            )
        )
    for j in range(4):
        for q in range(4):
            op_out[j, q * SHARE : (q + 1) * SHARE, :] = dot(
                hid[q * SHARE : (q + 1) * SHARE, :], down_full[j]
            ).astype(BF)
        op_out[j, span(r), :] = (
            op_out[j, span(r), :].astype(F32) + 0.5 * mid_out[j]
        ).astype(BF)
    for flow in flows:
        flow.step()
    for copy in crosses:
        copy.wait_recv()
    second_out[...] = c_send[...].astype(F32) + second_in[...].astype(F32)
    for flow in flows:
        flow.reduce()
    for copy in pending:
        copy.wait_send()


def forward(*operands):
    dma = pltpu.SemaphoreType.DMA
    shape = jax.ShapeDtypeStruct
    width = MAXLEN + SHARE
    blocked = pltpu.VMEM((4, SHARE, FEAT), BF)
    return vmem_call(
        forward_kernel,
        12,
        (
            shape((4, SHARE, FEAT), BF),
            shape((4, SHARE, FEAT), BF),
            shape((SHARE, 512), BF),
            shape((2, width, 128), BF),
            shape((HEADS // GROUPS, SHARE, 1), F32),
            shape((SHARE, 448), BF),
            shape((4, SHARE, FEAT), F32),
            shape((4, FEAT, 576), BF),
            shape((4, 448, FEAT), BF),
            shape((4, 8, FEAT), F32),
            shape((4, SHARE, FEAT), BF),
            shape((4, SHARE, FEAT), F32),
            shape((4, SHARD, FEAT), BF),
            shape((3, 4, 16, WIN), BF),
        ),
        [
            pltpu.VMEM((4, FEAT, WIN), BF),
            pltpu.VMEM((4, FEAT, WIN), BF),
            pltpu.VMEM((4, WIN, FEAT), BF),
            pltpu.VMEM((4, SHARD, FEAT), BF),
            pltpu.VMEM((SHARE, width), F32),
            pltpu.VMEM((2, SHARE, 128), BF),
            blocked,
            blocked,
            blocked,
            pltpu.VMEM((4, SHARD, FEAT), BF),
            pltpu.VMEM((SHARD, WIN), BF),
            pltpu.VMEM((SHARD, WIN), BF),
            pltpu.VMEM((SHARD, WIN), BF),
            pltpu.VMEM((4, 4, SHARE, FEAT), BF),
            pltpu.VMEM((3, 4, SHARE, FEAT), BF),
            pltpu.VMEM((3, 4, PADF, WIN), BF),
            pltpu.VMEM((3, 4, 128, WIN), BF),
            pltpu.VMEM((3, 4, 128, WIN), F32),
            pltpu.VMEM((3, 4, 128, WIN), BF),
            pltpu.VMEM((3, 4, 96, WIN), BF),
            pltpu.VMEM((3, 4, 64, WIN), BF),
            pltpu.VMEM((3, 4, 48, WIN), BF),
            dma((2, 3)),
            dma((2, 3)),
            dma((2, 5, 3)),
            dma((2, 3, 3, 3)),
            dma((2, 5)),
            dma((2, 3)),
            dma((2, 4)),
            dma((2,)),
            dma((2, 4)),
            dma((2, 3, 2)),
            dma((2, 2)),
            dma((2, 3, 3, 3)),
            dma((5,)),
        ],
        0,
    )(*operands)


def back_kernel(
    second_ref,
    mid_ref,
    cot_ref,
    x_ref,
    nf_ref,
    q_ref,
    kv_ref,
    lse_ref,
    att_ref,
    proj_full,
    outw_full,
    gains_full,
    cos_ref,
    sin_ref,
    start_ref,
    ff_ref,
    op_ref,
    block_out,
    input_out,
    ff_out,
    outw_out,
    proj_out,
    small_out,
    mask,
    g_mid,
    g_branch,
    g_att,
    dq,
    dk,
    dv,
    dkv,
    dkv_in,
    gp,
    gv,
    c_send,
    c_in,
    op_in,
    co_send,
    co_in,
    own_input,
    outw_grad,
    proj_grad,
    small,
    small_in,
    small_x,
    small_z,
    core_in,
    part,
    low_buf,
    in1,
    low2,
    in2,
    mine,
    z_in,
    ff_z,
    sem_flow,
    sem_ff,
    sem_kv,
    sem_c,
    sem_in,
    sem_s,
    sem_op,
    sem_co,
):
    d = lax.axis_index("dp")
    r = lax.axis_index("row")
    c = lax.axis_index("col")
    core = lax.rem(d, 2)
    y = lax.rem(d // 2, 2)
    x = d // 4
    sibling = d + 1 - 2 * core
    other_y = d + 2 - 4 * y
    x_peers = [(k, lax.rem(x + k, 4) * 4 + lax.rem(d, 4)) for k in (1, 2, 3)]
    row_peers = [(k, lax.rem(r + k, 4)) for k in (1, 2, 3)]
    block = 4 * d + r
    near = lambda i: {
        "dp": lax.rem((block + 64 + i) // 4, 16),
        "row": lax.rem(r + 4 + i, 4),
    }
    greet(
        [{"row": q} for _, q in row_peers]
        + [{"dp": p} for _, p in x_peers]
        + [{"col": 1 - c}, {"dp": sibling}, {"dp": other_y}]
        + [near(i) for i in (1, 2, 3, 4, -1, -2, -3, -4)]
    )
    pending = []

    def go(*args, **device):
        copy = rcopy(*args, **device)
        copy.start()
        pending.append(copy)
        return copy

    span = lambda q: pl.ds(pl.multiple_of(q * SHARE, SHARE), SHARE)
    buffers = (core_in, part, low_buf, in1, low2, in2, mine, z_in)
    flows = [
        GradSum(t, source, out, joined, wide_first, (r, d), buffers, sem_flow, go)
        for t, source, out, joined, wide_first in (
            (0, outw_grad, outw_out, False, True),
            (1, proj_grad, proj_out, False, True),
        )
    ]
    out, tail = flows
    spare = (None,) * 6 + (ff_ref, ff_z)
    ff = [
        GradSum(t, None, ff_out.at[t], True, True, (r, d), spare, sem_ff, go)
        for t in range(3)
    ]
    for flow in ff:
        flow.cross_rows()
        flow.done = 4

    def scatter(k, q):
        return go(
            op_ref.at[q], op_in.at[k - 1], sem_op.at[0, k - 1], sem_op.at[1, k - 1], row=q
        )

    op_copies = [scatter(*row_peers[0]), scatter(*row_peers[2])]

    small[...] = jnp.zeros_like(small)
    square = jnp.zeros((SHARE, 1), F32)
    inner = jnp.zeros((SHARE, 1), F32)
    for j in range(4):
        value = mid_ref[j]
        square += jnp.sum(value * value, axis=1, keepdims=True)
        inner += jnp.sum(second_ref[j] * gains_full[j, 1:2, :] * value, axis=1, keepdims=True)
    rate = lax.rsqrt(square / D + EPS)
    scale = rate * rate * rate * inner / D
    for j in range(4):
        value = mid_ref[j]
        grad = second_ref[j]
        small[j, 1:2, 0:FEAT] = jnp.sum(grad * value * rate, axis=0, keepdims=True)
        total = (
            cot_ref[j].astype(F32)
            + rate * (grad * gains_full[j, 1:2, :])
            - value * scale
        )
        g_mid[j] = total
        g_branch[j] = total.astype(BF)
    grad_att = dot_nt(g_branch[0], outw_full[0])
    for j in range(1, 4):
        grad_att += dot_nt(g_branch[j], outw_full[j])
    g_att[:, 448:512] = jnp.zeros((SHARE, 64), BF)
    g_att[:, 0:448] = grad_att.astype(BF)
    for flow in ff:
        flow.step()
    outw_grad[...] = jnp.zeros_like(outw_grad)
    for j in range(4):
        outw_grad[j, 0:FEAT, 0:448] = dot_tn(g_branch[j], att_ref[...]).astype(BF)
    out.step()
    query_at = lax.broadcasted_iota(jnp.int32, (SHARE, 1), 0) + MAXLEN
    key_at = lax.broadcasted_iota(jnp.int32, (SHARE, MAXLEN + SHARE), 1)
    mask[...] = jnp.where(
        (key_at >= start_ref[...]) & (key_at <= query_at), 0.0, -1e30
    )

    lane = lax.broadcasted_iota(jnp.int32, (SHARE, 128), 1)
    low = lane < 64
    for m in range(HEADS // GROUPS):
        at = 128 * (m // 2)
        mine_lanes = low if m % 2 == 0 else jnp.logical_not(low)
        pick = lambda ref: jnp.where(
            mine_lanes, ref[:, at : at + 128].astype(F32), 0.0
        ).astype(BF)
        query, grad = pick(q_ref), pick(g_att)
        probs = jnp.exp(dot_nt(query, kv_ref[0]) + mask[...] - lse_ref[m])
        grad_probs = dot_nt(grad, kv_ref[1])
        inner = jnp.sum(probs * grad_probs, axis=1, keepdims=True)
        grad_scores = (probs * (grad_probs - inner)).astype(BF)
        grad_v = dot_tn(probs.astype(BF), grad)
        grad_k = dot_tn(grad_scores, query)
        if m == 0:
            dv[...] = grad_v
            dk[...] = grad_k
        else:
            dv[...] += grad_v
            dk[...] += grad_k
        grad_q = dot(grad_scores, kv_ref[0]) * HEAD_DIM ** (-0.5)
        if m % 2 == 0:
            dq[:, at : at + 128] = grad_q
        else:
            dq[:, at : at + 128] = jnp.where(low, dq[:, at : at + 128], grad_q)
        if m == 1:
            out.step()
            ff[0].step()
    wide_low = lax.broadcasted_iota(jnp.int32, (MAXLEN + SHARE, 128), 1) < 64
    dkv[...] = jnp.where(
        wide_low,
        dk[...] + pltpu.roll(dk[...], 64, 1),
        dv[...] + pltpu.roll(dv[...], 64, 1),
    ).astype(BF)
    kv_copies = [
        go(
            dkv.at[(4 - i) * SHARE : (5 - i) * SHARE, :],
            dkv_in.at[i - 1],
            sem_kv.at[0, i - 1],
            sem_kv.at[1, i - 1],
            **near(-i),
        )
        for i in (1, 2, 3, 4)
    ]
    out.step()
    total = dkv[MAXLEN : MAXLEN + SHARE, :].astype(F32)
    for i in (1, 2, 3, 4):
        kv_copies[i - 1].wait_recv()
        total += dkv_in[i - 1].astype(F32)
    op_copies.append(scatter(*row_peers[1]))
    turned = pltpu.roll(total, 64, 1)
    dq[:, 384:512] = jnp.where(low, dq[:, 384:512], turned)
    gv[...] = turned[:, 0:64].astype(BF)
    cosine = jnp.concatenate([cos_ref[...]] * 4, axis=1)
    sine = jnp.concatenate([sin_ref[...]] * 4, axis=1)
    gp[...] = (dq[...] * cosine - swapped(dq[...]) * sine).astype(BF)
    for j in range(4):
        c_send[j] = (
            dot_nt(gp[...], proj_full[j, :, 0:512])
            + dot_nt(gv[...], proj_full[j, :, 512:576])
        ).astype(BF)
    cross = go(c_send, c_in, sem_c.at[0], sem_c.at[1], col=1 - c)
    proj_grad[...] = jnp.zeros_like(proj_grad)
    for j in range(4):
        proj_grad[j, 0:FEAT, 0:512] = dot_tn(nf_ref[j], gp[...]).astype(BF)
        proj_grad[j, 0:FEAT, 512:576] = dot_tn(nf_ref[j], gv[...]).astype(BF)
    tail.step()
    bias_a = jnp.sum(gp[...].astype(F32), axis=0, keepdims=True)
    bias_b = jnp.sum(gv[...].astype(F32), axis=0, keepdims=True)
    for j in range(4):
        small[j, 2:3, 0:512] = bias_a
        small[j, 2:3, 512:576] = bias_b
    out.step()
    tail.step()
    ff[1].step()
    ff[2].step()
    tail.step()
    out.step()
    tail.step()

    square = jnp.zeros((SHARE, 1), F32)
    for j in range(4):
        value = x_ref[j].astype(F32)
        square += jnp.sum(value * value, axis=1, keepdims=True)
    rate = lax.rsqrt(square / D + EPS)
    cross.wait_recv()
    inner = jnp.zeros((SHARE, 1), F32)
    for j in range(4):
        grad = c_send[j].astype(F32) + c_in[j].astype(F32)
        inner += jnp.sum(
            grad * gains_full[j, 0:1, :] * x_ref[j].astype(F32), axis=1, keepdims=True
        )
    scale = rate * rate * rate * inner / D
    for j in range(4):
        value = x_ref[j].astype(F32)
        grad = c_send[j].astype(F32) + c_in[j].astype(F32)
        small[j, 0:1, 0:FEAT] = jnp.sum(grad * value * rate, axis=0, keepdims=True)
        own_input[j] = (
            g_mid[j] + rate * (grad * gains_full[j, 0:1, :]) - value * scale
        ).astype(BF)
    in_copies = [
        go(
            own_input.at[q],
            input_out.at[r],
            sem_in.at[0, k - 1],
            sem_in.at[1, k - 1],
            row=q,
        )
        for k, q in row_peers
    ]
    input_out[r] = own_input[r]

    total = op_ref[r].astype(F32)
    for copy in op_copies:
        copy.wait_recv()
    for k in range(3):
        total += op_in[k].astype(F32)
    co_send[...] = total.astype(BF)
    final = go(co_send, co_in, sem_co.at[0], sem_co.at[1], col=1 - c)

    def swap(stage, source, target, k, **device):
        return go(source, target, sem_s.at[0, stage, k - 1], sem_s.at[1, stage, k - 1], **device)

    copy = swap(0, small, small_in.at[0], 1, dp=sibling)
    out.step()
    tail.step()
    ff[0].step()
    copy.wait_recv()
    small_x[0] = small[...] + small_in[0]
    copies = [swap(1, small_x.at[0], small_in.at[k], k, dp=p) for k, p in x_peers]
    out.step()
    tail.step()
    for copy in copies:
        copy.wait_recv()
    small_x[1] = small_x[0] + small_in[1] + small_in[2] + small_in[3]
    copy = swap(2, small_x.at[1], small_in.at[4], 1, dp=other_y)
    tail.step()
    copy.wait_recv()
    small_x[2] = small_x[1] + small_in[4]
    copies = [swap(3, small_x.at[2, q], small_z.at[r], k, row=q) for k, q in row_peers]
    small_z[r] = small_x[2, r]
    ff[1].step()
    ff[2].step()
    for copy in copies:
        copy.wait_recv()
    small_out[...] = small_z[0] + small_z[1] + small_z[2] + small_z[3]
    tail.step()
    out.step()
    for flow in ff:
        flow.step()
    for copy in in_copies:
        copy.wait_recv()
    final.wait_recv()
    block_out[...] = (co_send[...].astype(F32) + co_in[...].astype(F32)).astype(BF)
    for copy in pending:
        copy.wait_send()


def back(*operands):
    dma = pltpu.SemaphoreType.DMA
    shape = jax.ShapeDtypeStruct
    width = MAXLEN + SHARE
    blocked = pltpu.VMEM((4, SHARE, FEAT), BF)
    count = 2
    return vmem_call(
        back_kernel,
        17,
        (
            shape((SHARD, FEAT), BF),
            shape((4, SHARE, FEAT), BF),
            shape((3, PADF, HALF_FF), BF),
            shape((PADF, WIN), BF),
            shape((PADF, WIN), BF),
            shape((8, WIN), F32),
        ),
        [
            pltpu.VMEM((SHARE, width), F32),
            pltpu.VMEM((4, SHARE, FEAT), F32),
            blocked,
            pltpu.VMEM((SHARE, 512), BF),
            pltpu.VMEM((SHARE, 512), F32),
            pltpu.VMEM((width, 128), F32),
            pltpu.VMEM((width, 128), F32),
            pltpu.VMEM((width, 128), BF),
            pltpu.VMEM((4, SHARE, 128), BF),
            pltpu.VMEM((SHARE, 512), BF),
            pltpu.VMEM((SHARE, 64), BF),
            blocked,
            blocked,
            pltpu.VMEM((3, SHARD, FEAT), BF),
            pltpu.VMEM((SHARD, FEAT), BF),
            pltpu.VMEM((SHARD, FEAT), BF),
            blocked,
            pltpu.VMEM((4, PADF, WIN), BF),
            pltpu.VMEM((4, PADF, WIN), BF),
            pltpu.VMEM((4, 8, WIN), F32),
            pltpu.VMEM((5, 4, 8, WIN), F32),
            pltpu.VMEM((3, 4, 8, WIN), F32),
            pltpu.VMEM((4, 8, WIN), F32),
            pltpu.VMEM((count, 4, 128, WIN), BF),
            pltpu.VMEM((count, 4, 128, WIN), F32),
            pltpu.VMEM((count, 4, 128, WIN), BF),
            pltpu.VMEM((count, 4, 96, WIN), BF),
            pltpu.VMEM((count, 4, 64, WIN), BF),
            pltpu.VMEM((count, 4, 48, WIN), BF),
            pltpu.VMEM((count, 4, 16, WIN), BF),
            pltpu.VMEM((count, 4, 16, WIN), BF),
            pltpu.VMEM((3, 4, 16, WIN), BF),
            dma((2, count, 7, 3)),
            dma((2, 3, 7, 3)),
            dma((2, 4)),
            dma((2,)),
            dma((2, 3)),
            dma((2, 4, 3)),
            dma((2, 3)),
            dma((2,)),
        ],
        1,
    )(*operands)


def body(
    activations,
    starts,
    first_gain,
    project_weight,
    project_bias,
    output_weight,
    second_gain,
    gate_weight,
    up_weight,
    down_weight,
    cotangent,
):
    r = lax.axis_index("row")
    shard = lax.axis_index("dp")
    query_width = HEADS // GROUPS * HEAD_DIM

    base = shard * SHARD + r * SHARE
    start_window = (
        lax.dynamic_slice_in_dim(starts, r * SHARE, SHARE, 0) - base + MAXLEN
    )[:, None]
    positions = (MAXLEN + jnp.arange(SHARE, dtype=jnp.int32))[:, None] - start_window
    half = HEAD_DIM // 2
    freqs = 1000000.0 ** (-jnp.arange(half, dtype=F32) * 2.0 / HEAD_DIM)
    angle = positions.astype(F32) * jnp.tile(freqs, 4)[None, :]
    cosine = jnp.cos(angle)
    sine = jnp.sin(angle) * jnp.tile(jnp.repeat(jnp.array([-1.0, 1.0], F32), half), 2)[None, :]
    gains = jnp.pad(jnp.stack([first_gain, second_gain]), ((0, 6), (0, 0)))
    (
        x_low,
        normed_first,
        queries,
        kv,
        lse,
        attended,
        middle,
        project_full,
        output_full,
        gains_full,
        cot_own,
        grad_second,
        out_partial,
        ff_part,
    ) = forward(
        activations,
        cotangent,
        project_weight,
        output_weight,
        gate_weight,
        up_weight,
        down_weight,
        gains,
        project_bias[None, :],
        cosine,
        sine,
        start_window,
    )
    block_output, input_grad, ff_sum, outw_sum, project_sum, small = back(
        grad_second,
        middle,
        cot_own,
        x_low,
        normed_first,
        queries,
        kv,
        lse,
        attended,
        project_full,
        output_full,
        gains_full,
        cosine,
        sine,
        start_window,
        ff_part,
        out_partial,
    )
    width = project_weight.shape[1]
    ff_sum = ff_sum[:, :FEAT].astype(F32)
    return (
        block_output,
        input_grad.reshape(SHARD, FEAT).astype(F32),
        small[0, :FEAT],
        project_sum[:FEAT, :width].astype(F32),
        small[2, :width],
        outw_sum[:FEAT, :query_width].astype(F32).T,
        small[1, :FEAT],
        ff_sum[0],
        ff_sum[1],
        ff_sum[2].T,
    )


def solution(mesh):
    return jax.shard_map(
        body,
        mesh=mesh,
        in_specs=(
            P("dp", "row"),
            P("dp"),
            P("row"),
            P("row", "col"),
            P("col"),
            P("col", "row"),
            P("row"),
            P("row", "col"),
            P("row", "col"),
            P("col", "row"),
            P("dp", "row"),
        ),
        out_specs=(
            P("dp", "row"),
            P("dp", "row"),
            P("row"),
            P("row", "col"),
            P("col"),
            P("col", "row"),
            P("row"),
            P("row", "col"),
            P("row", "col"),
            P("col", "row"),
        ),
        check_vma=False,
    )
```

```python
import functools

import jax
import jax.numpy as jnp
from jax import lax
from jax.experimental import pallas as pl
from jax.experimental.pallas import tpu as pltpu
from jax.sharding import PartitionSpec as P

D = 896
HEADS = 14
GROUPS = 2
HEAD_DIM = 64
MAXLEN = 1024
EPS = 1e-06
BF = jnp.bfloat16
F32 = jnp.float32
ROWS = 4
FEAT = 224
SHARE = 256
SHARD = 1024
HALF_FF = 2432
WIN = 640
LAST = HALF_FF - WIN
PADF = 256
VMEM_LIMIT = 60 * 1024 * 1024


def dot(a, b):
    return jnp.dot(a, b, preferred_element_type=F32)


def dot_nt(a, b):
    return lax.dot_general(a, b, (((1,), (1,)), ((), ())), preferred_element_type=F32)


def dot_tn(a, b):
    return lax.dot_general(a, b, (((0,), (0,)), ((), ())), preferred_element_type=F32)


def rcopy(src, dst, send, recv, **device):
    return pltpu.make_async_remote_copy(
        src_ref=src,
        dst_ref=dst,
        send_sem=send,
        recv_sem=recv,
        device_id=device,
        device_id_type=pl.DeviceIdType.MESH,
    )


def greet(peers):
    barrier = pltpu.get_barrier_semaphore()
    for peer in peers:
        pl.semaphore_signal(
            barrier, inc=1, device_id=peer, device_id_type=pl.DeviceIdType.MESH
        )
    pl.semaphore_wait(barrier, len(peers))


def vmem_call(kernel, inputs, outs, scratch, collective, cost=None):
    return pl.pallas_call(
        kernel,
        out_shape=outs,
        in_specs=[pl.BlockSpec(memory_space=pltpu.VMEM)] * inputs,
        out_specs=jax.tree.map(lambda _: pl.BlockSpec(memory_space=pltpu.VMEM), outs),
        scratch_shapes=scratch,
        compiler_params=pltpu.CompilerParams(
            collective_id=collective,
            has_side_effects=True,
            vmem_limit_bytes=VMEM_LIMIT,
        ),
        cost_estimate=cost,
    )


class GradSum:
    def __init__(self, t, source, out, joined, wide_first, place, buffers, sems, go):
        self.t, self.source, self.out, self.joined, self.go = t, source, out, joined, go
        self.r, d = place
        self.core = lax.rem(d, 2)
        y = lax.rem(d // 2, 2)
        x = d // 4
        self.sibling = d + 1 - 2 * self.core
        along_x = [
            (k, lax.rem(x + k, 4), lax.rem(x + k, 4) * 4 + lax.rem(d, 4)) for k in (1, 2, 3)
        ]
        along_y = [(1, 1 - y, d + 2 - 4 * y)]
        if wide_first:
            self.first, self.second = (along_x, x, 32), (along_y, y, 16)
        else:
            self.first, self.second = (along_y, y, 64), (along_x, x, 16)
        self.at_first = self.core * 128 + self.first[1] * self.first[2]
        self.at = self.at_first + self.second[1] * 16
        self.core_in, self.part, self.low, self.in1, self.low2, self.in2, self.mine, self.z_in = [
            buffer.at[t] if buffer is not None else None for buffer in buffers
        ]
        self.sem = lambda stage, k: (sems.at[0, t, stage, k - 1], sems.at[1, t, stage, k - 1])
        self.waiting = []
        self.done = 0

    def rows(self, start, size):
        return pl.ds(pl.multiple_of(start, 16), size)

    def settle(self):
        for copy in self.waiting:
            copy.wait_recv()
        self.waiting = []

    def send(self, source, target, stage, k, **device):
        self.waiting.append(self.go(source, target, *self.sem(stage, k), **device))

    def step(self):
        self.settle()
        getattr(self, "step%d" % self.done)()
        self.done += 1

    def step0(self):
        self.send(
            self.source.at[:, self.rows((1 - self.core) * 128, 128), :],
            self.core_in,
            0,
            1,
            dp=self.sibling,
        )

    def step1(self):
        peers, own, unit = self.first
        total = self.source[:, self.rows(self.core * 128, 128), :].astype(F32)
        total = total + self.core_in[...].astype(F32)
        self.part[...] = total
        self.low[...] = total.astype(BF)
        for k, index, device in peers:
            self.send(
                self.low.at[:, self.rows(index * unit, unit), :],
                self.in1.at[:, (k - 1) * unit : k * unit, :],
                1,
                k,
                dp=device,
            )

    def step2(self):
        peers, own, unit = self.first
        total = self.part[:, self.rows(own * unit, unit), :]
        for k, _, _ in peers:
            total = total + self.in1[:, (k - 1) * unit : k * unit, :].astype(F32)
        self.part[:, 0:unit, :] = total
        self.low2[:, 0:unit, :] = total.astype(BF)
        peers, own, unit = self.second
        for k, index, device in peers:
            self.send(
                self.low2.at[:, self.rows(index * unit, unit), :],
                self.in2.at[:, (k - 1) * unit : k * unit, :],
                2,
                k,
                dp=device,
            )

    def step3(self):
        self.reduce()
        self.cross_rows()

    def reduce(self):
        self.settle()
        peers, own, unit = self.second
        total = self.part[:, self.rows(own * unit, unit), :]
        for k, _, _ in peers:
            total = total + self.in2[:, (k - 1) * unit : k * unit, :].astype(F32)
        self.mine[...] = total.astype(BF)

    def cross_rows(self):
        for k in (1, 2, 3):
            q = lax.rem(self.r + k, 4)
            self.send(self.mine.at[q], self.z_in.at[self.r], 3, k, row=q)
        self.z_in[self.r] = self.mine[self.r]

    def step4(self):
        here = self.rows(self.at, 16)
        if self.joined:
            for q in range(3):
                self.out[here, q * WIN : (q + 1) * WIN] = self.z_in[q]
            self.out[here, 3 * WIN : HALF_FF] = self.z_in[3][:, 4 * WIN - HALF_FF :]
        else:
            total = self.z_in[0].astype(F32)
            for q in range(1, 4):
                total = total + self.z_in[q].astype(F32)
            self.out[here, :] = total.astype(BF)
        self.spread(self.second[0], self.at, 16, 4)

    def spread(self, peers, start, size, stage):
        block = self.out.at[self.rows(start, size), :]
        for k, _, device in peers:
            self.send(block, block, stage, k, dp=device)

    def step5(self):
        self.spread(self.first[0], self.at_first, self.first[2], 5)

    def step6(self):
        self.spread([(1, 0, self.sibling)], self.core * 128, 128, 6)

    def step7(self):
        pass


def swapped(values):
    width = values.shape[1]
    lane = lax.broadcasted_iota(jnp.int32, values.shape, 1)
    return jnp.where(
        lax.rem(lane, 64) < 32,
        pltpu.roll(values, width - 32, 1),
        pltpu.roll(values, 32, 1),
    )


def forward_kernel(
    act_ref,
    cot_ref,
    proj_ref,
    outw_ref,
    gate_ref,
    up_ref,
    down_ref,
    gains_ref,
    bias_ref,
    cos_ref,
    sin_ref,
    start_ref,
    x_out,
    nf_out,
    q_out,
    kv_out,
    lse_out,
    att_out,
    mid_out,
    proj_full,
    outw_full,
    gains_full,
    cot_out,
    second_out,
    op_out,
    mine_out,
    gate_full,
    up_full,
    down_full,
    cot_all,
    mask,
    own_kv,
    kv_pack,
    c_send,
    c_in,
    second_in,
    ns_all,
    hid,
    gg,
    gu,
    sp_send,
    sp_in,
    grads,
    core_in,
    part,
    low_buf,
    in1,
    low2,
    in2,
    sem_x,
    sem_g,
    sem_w,
    sem_wx,
    sem_wc,
    sem_cot,
    sem_kv,
    sem_c,
    sem_ag,
    sem_sp,
    sem_cs,
    sem_flow,
    sem_l,
):
    d = lax.axis_index("dp")
    r = lax.axis_index("row")
    c = lax.axis_index("col")
    core = lax.rem(d, 2)
    x_at = d // 4
    sibling = d + 1 - 2 * core
    other_y = d + 2 - 4 * lax.rem(d // 2, 2)
    x_peers = [(k, lax.rem(x_at + k, 4) * 4 + lax.rem(d, 4)) for k in (1, 2, 3)]
    block = 4 * d + r
    near = lambda i: {
        "dp": lax.rem((block + 64 + i) // 4, 16),
        "row": lax.rem(r + 4 + i, 4),
    }
    greet(
        [{"row": lax.rem(r + k, 4)} for k in (1, 2, 3)]
        + [{"dp": p} for _, p in x_peers]
        + [{"col": 1 - c}, {"dp": sibling}, {"dp": other_y}]
        + [near(i) for i in (1, 2, 3, 4, -1, -2, -3, -4)]
    )
    pending = []

    def go(*args, **device):
        copy = rcopy(*args, **device)
        copy.start()
        pending.append(copy)
        return copy

    peers = [(k, lax.rem(r + k, 4)) for k in (1, 2, 3)]
    span = lambda q: pl.ds(pl.multiple_of(q * SHARE, SHARE), SHARE)
    offset = lambda q: pl.multiple_of(jnp.minimum(q * WIN, LAST), 128)
    half = lambda n: pl.ds(pl.multiple_of(core * n, 16), n)

    def down_rows(q):
        return pl.ds(pl.multiple_of(offset(q) + core * (WIN // 2), 16), WIN // 2)

    pieces = (
        (lambda q: proj_ref.at[half(112), :], proj_full, 112),
        (lambda q: outw_ref.at[half(224), :], outw_full, 224),
        (lambda q: gate_ref.at[half(112), pl.ds(offset(q), WIN)], gate_full, 112),
        (lambda q: up_ref.at[half(112), pl.ds(offset(q), WIN)], up_full, 112),
        (lambda q: down_ref.at[down_rows(q), :], down_full, WIN // 2),
    )

    def crossing(w):
        source, full, n = pieces[w]
        return [
            rcopy(
                source(q),
                full.at[r, half(n), :],
                sem_w.at[0, w, k - 1],
                sem_w.at[1, w, k - 1],
                row=q,
            )
            for k, q in peers
        ]

    def passing(w):
        _, full, n = pieces[w]
        copies = []
        for k, q in peers:
            part = full.at[q, half(n), :]
            for e, device in x_peers:
                copies.append(
                    rcopy(
                        part,
                        part,
                        sem_wx.at[0, w - 2, k - 1, e - 1],
                        sem_wx.at[1, w - 2, k - 1, 0],
                        dp=device,
                    )
                )
        return copies

    def fetch(w):
        source, full, n = pieces[w]
        local = pltpu.make_async_copy(source(r), full.at[r, half(n), :], sem_l.at[w])
        local.start()
        copies = crossing(w)
        if w < 2:
            for copy in copies:
                copy.start()
                pending.append(copy)
        else:

            @pl.when(x_at == w - 2)
            def _():
                for copy in copies:
                    copy.start()

        return copies, local

    def pass_on(w, fetched):
        @pl.when(x_at == w - 2)
        def _():
            for copy in fetched[0]:
                copy.wait_recv()
            for copy in passing(w):
                copy.start()

    def share(w, fetched):
        _, full, n = pieces[w]
        copies, local = fetched
        local.wait()
        if w < 2:
            for copy in copies:
                copy.wait_recv()
        else:

            @pl.when(x_at != w - 2)
            def _():
                for copy in passing(w)[::3]:
                    copy.wait_recv()

        part = full.at[:, half(n), :]
        copy = rcopy(part, part, sem_wc.at[0, w], sem_wc.at[1, w], dp=sibling)
        copy.start()
        if w < 2:
            pending.append(copy)
        return copy

    def finish(w, fetched):
        @pl.when(x_at == w - 2)
        def _():
            for copy in fetched[0] + passing(w):
                copy.wait_send()

    x_copies = [
        go(
            act_ref.at[span(q), :],
            x_out.at[r],
            sem_x.at[0, k - 1],
            sem_x.at[1, k - 1],
            row=q,
        )
        for k, q in peers
    ]
    g_copies = [
        go(gains_ref, gains_full.at[r], sem_g.at[0, k - 1], sem_g.at[1, k - 1], row=q)
        for k, q in peers
    ]
    fetched = {0: fetch(0)}
    x_out[r] = act_ref[span(r), :]
    gains_full[r] = gains_ref[...]
    query_at = lax.broadcasted_iota(jnp.int32, (SHARE, 1), 0) + MAXLEN
    key_at = lax.broadcasted_iota(jnp.int32, (SHARE, MAXLEN + SHARE), 1)
    mask[...] = jnp.where(
        (key_at >= start_ref[...]) & (key_at <= query_at), 0.0, -1e30
    )
    shared = {0: share(0, fetched[0])}
    for copy in x_copies + g_copies:
        copy.wait_recv()
    for w in (1, 2, 3, 4):
        fetched[w] = fetch(w)
    cot_all[r] = cot_ref[...]
    square = jnp.zeros((SHARE, 1), F32)
    for j in range(4):
        value = x_out[j].astype(F32)
        square += jnp.sum(value * value, axis=1, keepdims=True)
    rate = lax.rsqrt(square / D + EPS)
    for j in range(4):
        nf_out[j] = (x_out[j].astype(F32) * rate * gains_full[j, 0:1, :]).astype(BF)
    shared[0].wait_recv()
    projected = dot(nf_out[0], proj_full[0, :, 0:512])
    values = dot(nf_out[0], proj_full[0, :, 512:576])
    for j in range(1, 4):
        projected += dot(nf_out[j], proj_full[j, :, 0:512])
        values += dot(nf_out[j], proj_full[j, :, 512:576])
    projected += bias_ref[:, 0:512]
    values = (values + bias_ref[:, 512:576]).astype(BF)
    cosine = jnp.concatenate([cos_ref[...]] * 4, axis=1)
    sine = jnp.concatenate([sin_ref[...]] * 4, axis=1)
    turned = projected * cosine + swapped(projected) * sine
    q_out[...] = (turned * HEAD_DIM ** (-0.5)).astype(BF)
    tile = turned[:, 384:512]
    lane = lax.broadcasted_iota(jnp.int32, (SHARE, 128), 1)
    low = lane < 64
    double = (
        lax.rem(lax.broadcasted_iota(jnp.int32, (64, 128), 1), 64)
        == lax.broadcasted_iota(jnp.int32, (64, 128), 0)
    ).astype(F32).astype(BF)
    own_kv[...] = jnp.where(low, pltpu.roll(tile, 64, 1), dot(values, double)).astype(BF)
    kv_copies = [
        go(
            own_kv,
            kv_pack.at[(4 - i) * SHARE : (5 - i) * SHARE, :],
            sem_kv.at[0, i - 1],
            sem_kv.at[1, i - 1],
            **near(i),
        )
        for i in (1, 2, 3, 4)
    ]
    kv_pack[MAXLEN : MAXLEN + SHARE, :] = own_kv[...]
    for w in (2, 3, 4):
        pass_on(w, fetched[w])
    for copy in kv_copies:
        copy.wait_recv()
    right, across, left = [q for _, q in peers]

    def cot_go(source, target, index, q):
        return go(source, target, sem_cot.at[0, index], sem_cot.at[1, index], row=q)

    cot_left = cot_go(cot_ref, cot_all.at[r], 0, right)
    cot_right = cot_go(cot_ref, cot_all.at[r], 1, left)
    packed = kv_pack[...].astype(F32)
    turned_pack = pltpu.roll(packed, 64, 1)
    first_half = lax.broadcasted_iota(jnp.int32, packed.shape, 1) < 64
    kv_out[0] = jnp.where(first_half, packed, turned_pack).astype(BF)
    kv_out[1] = jnp.where(first_half, turned_pack, packed).astype(BF)
    for m in range(HEADS // GROUPS):
        at = 128 * (m // 2)
        mine = low if m % 2 == 0 else jnp.logical_not(low)
        query = jnp.where(mine, q_out[:, at : at + 128].astype(F32), 0.0).astype(BF)
        scores = dot_nt(query, kv_out[0]) + mask[...]
        peak = jnp.max(scores, axis=1, keepdims=True)
        powered = jnp.exp(scores - peak)
        total = jnp.sum(powered, axis=1, keepdims=True)
        probs = (powered * (1.0 / total)).astype(BF)
        lse_out[m] = peak + jnp.log(total)
        mixed = dot(probs, kv_out[1])
        if m == 6:
            att_out[:, 384:448] = mixed[:, 0:64].astype(BF)
        elif m % 2 == 0:
            even = mixed
        else:
            att_out[:, at : at + 128] = jnp.where(low, even, mixed).astype(BF)
    shared[1] = share(1, fetched[1])
    shared[1].wait_recv()
    for j in range(4):
        c_send[j] = dot(att_out[...], outw_full[j]).astype(BF)
    cross = rcopy(c_send, c_in, sem_c.at[0], sem_c.at[1], col=1 - c)
    cross.start()
    cot_left.wait_recv()
    upper = cot_all.at[left, 0 : SHARD // 2, :]
    cot_copies = [cot_go(upper, upper, 2, right)]
    cot_right.wait_recv()
    lower = cot_all.at[right, SHARD // 2 : SHARD, :]
    cot_copies.append(cot_go(lower, lower, 3, left))
    for w in (2, 3, 4):
        shared[w] = share(w, fetched[w])
    cross.wait_recv()
    square = jnp.zeros((SHARE, 1), F32)
    for j in range(4):
        value = x_out[j].astype(F32) + (
            c_send[j].astype(F32) + c_in[j].astype(F32)
        )
        mid_out[j] = value
        square += jnp.sum(value * value, axis=1, keepdims=True)
    rate = lax.rsqrt(square / D + EPS)
    for j in range(4):
        ns_all[j, span(r), :] = (mid_out[j] * rate * gains_full[j, 1:2, :]).astype(BF)

    def spread(blocks, source, index, q):
        part = ns_all.at[blocks, span(source), :]
        return go(part, part, sem_ag.at[0, index], sem_ag.at[1, index], row=q)

    every, front_half, back_half = pl.ds(0, 4), pl.ds(0, 2), pl.ds(2, 2)
    from_left = spread(every, r, 0, right)
    from_right = spread(every, r, 1, left)
    for copy in cot_copies:
        copy.wait_recv()
    for w in (2, 3, 4):
        shared[w].wait_recv()
        shared[w].wait_send()
        finish(w, fetched[w])
    live = jnp.where(r < 3, 1.0, 0.0)
    extra = 4 * WIN - HALF_FF
    for j in range(4):
        gate_full[j, :, 0:extra] = (gate_full[j, :, 0:extra].astype(F32) * live).astype(BF)
        up_full[j, :, 0:extra] = (up_full[j, :, 0:extra].astype(F32) * live).astype(BF)
        cot_out[j] = cot_all[j, span(r), :]

    def feed(k, q, arrived):
        grad_hidden = dot_nt(cot_all[0, span(q), :], down_full[0])
        for j in range(1, 4):
            grad_hidden += dot_nt(cot_all[j, span(q), :], down_full[j])
        arrived()
        gate = dot(ns_all[0, span(q), :], gate_full[0])
        up = dot(ns_all[0, span(q), :], up_full[0])
        for j in range(1, 4):
            gate += dot(ns_all[j, span(q), :], gate_full[j])
            up += dot(ns_all[j, span(q), :], up_full[j])
        sigma = 1.0 / (1.0 + jnp.exp(-gate))
        silu = gate * sigma
        hid[span(q), :] = (silu * up).astype(BF)
        g_gate = (grad_hidden * up * (sigma + silu * (1.0 - sigma))).astype(BF)
        g_up = (grad_hidden * silu).astype(BF)
        gg[span(q), :] = g_gate
        gu[span(q), :] = g_up
        copies = []
        for j in range(4):
            sp_send[k, j] = (
                dot_nt(g_gate, gate_full[j]) + dot_nt(g_up, up_full[j])
            ).astype(BF)
            if k and j % 2:
                copies.append(
                    go(
                        sp_send.at[k, j - 1 : j + 1],
                        sp_in.at[k - 1, j - 1 : j + 1],
                        sem_sp.at[0, k - 1, j // 2],
                        sem_sp.at[1, k - 1, j // 2],
                        row=q,
                    )
                )
        return copies

    forwarded = []

    def neighbours_here():
        from_left.wait_recv()
        forwarded.append(spread(front_half, left, 2, right))
        from_right.wait_recv()
        forwarded.append(spread(back_half, right, 3, left))

    def opposite_here():
        for copy in forwarded:
            copy.wait_recv()

    feed(0, r, lambda: None)
    back = {}
    back[1] = feed(1, right, neighbours_here)
    back[3] = feed(3, left, lambda: None)
    back[2] = feed(2, across, opposite_here)

    buffers = (core_in, part, low_buf, in1, low2, in2, mine_out, None)
    flows = [
        GradSum(t, grads.at[t], None, True, True, (r, d), buffers, sem_flow, go)
        for t in range(3)
    ]
    grads[:, :, FEAT:PADF, :] = jnp.zeros((3, 4, PADF - FEAT, WIN), BF)
    for t, left_side, right_side in ((0, ns_all, gg), (1, ns_all, gu), (2, cot_all, hid)):
        for j in range(4):
            grads[t, j, 0:FEAT, :] = dot_tn(left_side[j], right_side[...]).astype(BF)
        flows[t].step()
        if t:
            flows[t - 1].step()
    flows[2].step()
    cross.wait_send()
    crosses = []
    for h in (0, 2):
        total = sp_send[0, h : h + 2].astype(F32)
        for k in (1, 3, 2):
            back[k][h // 2].wait_recv()
            total += sp_in[k - 1, h : h + 2].astype(F32)
        c_send[h : h + 2] = total.astype(BF)
        crosses.append(
            go(
                c_send.at[h : h + 2],
                second_in.at[h : h + 2],
                sem_cs.at[0, h // 2],
                sem_cs.at[1, h // 2],
                col=1 - c,
            )
        )
    for j in range(4):
        for q in range(4):
            op_out[j, q * SHARE : (q + 1) * SHARE, :] = dot(
                hid[q * SHARE : (q + 1) * SHARE, :], down_full[j]
            ).astype(BF)
        op_out[j, span(r), :] = (
            op_out[j, span(r), :].astype(F32) + 0.5 * mid_out[j]
        ).astype(BF)
    for flow in flows:
        flow.step()
    for copy in crosses:
        copy.wait_recv()
    second_out[...] = c_send[...].astype(F32) + second_in[...].astype(F32)
    for flow in flows:
        flow.reduce()
    for copy in pending:
        copy.wait_send()


def forward(*operands):
    dma = pltpu.SemaphoreType.DMA
    shape = jax.ShapeDtypeStruct
    width = MAXLEN + SHARE
    blocked = pltpu.VMEM((4, SHARE, FEAT), BF)
    return vmem_call(
        forward_kernel,
        12,
        (
            shape((4, SHARE, FEAT), BF),
            shape((4, SHARE, FEAT), BF),
            shape((SHARE, 512), BF),
            shape((2, width, 128), BF),
            shape((HEADS // GROUPS, SHARE, 1), F32),
            shape((SHARE, 448), BF),
            shape((4, SHARE, FEAT), F32),
            shape((4, FEAT, 576), BF),
            shape((4, 448, FEAT), BF),
            shape((4, 8, FEAT), F32),
            shape((4, SHARE, FEAT), BF),
            shape((4, SHARE, FEAT), F32),
            shape((4, SHARD, FEAT), BF),
            shape((3, 4, 16, WIN), BF),
        ),
        [
            pltpu.VMEM((4, FEAT, WIN), BF),
            pltpu.VMEM((4, FEAT, WIN), BF),
            pltpu.VMEM((4, WIN, FEAT), BF),
            pltpu.VMEM((4, SHARD, FEAT), BF),
            pltpu.VMEM((SHARE, width), F32),
            pltpu.VMEM((SHARE, 128), BF),
            pltpu.VMEM((width, 128), BF),
            blocked,
            blocked,
            blocked,
            pltpu.VMEM((4, SHARD, FEAT), BF),
            pltpu.VMEM((SHARD, WIN), BF),
            pltpu.VMEM((SHARD, WIN), BF),
            pltpu.VMEM((SHARD, WIN), BF),
            pltpu.VMEM((4, 4, SHARE, FEAT), BF),
            pltpu.VMEM((3, 4, SHARE, FEAT), BF),
            pltpu.VMEM((3, 4, PADF, WIN), BF),
            pltpu.VMEM((3, 4, 128, WIN), BF),
            pltpu.VMEM((3, 4, 128, WIN), F32),
            pltpu.VMEM((3, 4, 128, WIN), BF),
            pltpu.VMEM((3, 4, 96, WIN), BF),
            pltpu.VMEM((3, 4, 64, WIN), BF),
            pltpu.VMEM((3, 4, 48, WIN), BF),
            dma((2, 3)),
            dma((2, 3)),
            dma((2, 5, 3)),
            dma((2, 3, 3, 3)),
            dma((2, 5)),
            dma((2, 4)),
            dma((2, 4)),
            dma((2,)),
            dma((2, 4)),
            dma((2, 3, 2)),
            dma((2, 2)),
            dma((2, 3, 3, 3)),
            dma((5,)),
        ],
        0,
    )(*operands)


def back_kernel(
    second_ref,
    mid_ref,
    cot_ref,
    x_ref,
    nf_ref,
    q_ref,
    kv_ref,
    lse_ref,
    att_ref,
    proj_full,
    outw_full,
    gains_full,
    cos_ref,
    sin_ref,
    start_ref,
    ff_ref,
    op_ref,
    block_out,
    input_out,
    ff_out,
    outw_out,
    proj_out,
    small_out,
    mask,
    g_mid,
    g_branch,
    g_att,
    dq,
    dk,
    dv,
    dkv,
    dkv_in,
    gp,
    gv,
    c_send,
    c_in,
    op_in,
    co_send,
    co_in,
    own_input,
    outw_grad,
    proj_grad,
    small,
    small_in,
    small_x,
    small_z,
    core_in,
    part,
    low_buf,
    in1,
    low2,
    in2,
    mine,
    z_in,
    ff_z,
    sem_flow,
    sem_ff,
    sem_kv,
    sem_c,
    sem_in,
    sem_s,
    sem_op,
    sem_co,
):
    d = lax.axis_index("dp")
    r = lax.axis_index("row")
    c = lax.axis_index("col")
    core = lax.rem(d, 2)
    y = lax.rem(d // 2, 2)
    x = d // 4
    sibling = d + 1 - 2 * core
    other_y = d + 2 - 4 * y
    x_peers = [(k, lax.rem(x + k, 4) * 4 + lax.rem(d, 4)) for k in (1, 2, 3)]
    row_peers = [(k, lax.rem(r + k, 4)) for k in (1, 2, 3)]
    block = 4 * d + r
    near = lambda i: {
        "dp": lax.rem((block + 64 + i) // 4, 16),
        "row": lax.rem(r + 4 + i, 4),
    }
    greet(
        [{"row": q} for _, q in row_peers]
        + [{"dp": p} for _, p in x_peers]
        + [{"col": 1 - c}, {"dp": sibling}, {"dp": other_y}]
        + [near(i) for i in (1, 2, 3, 4, -1, -2, -3, -4)]
    )
    pending = []

    def go(*args, **device):
        copy = rcopy(*args, **device)
        copy.start()
        pending.append(copy)
        return copy

    span = lambda q: pl.ds(pl.multiple_of(q * SHARE, SHARE), SHARE)
    buffers = (core_in, part, low_buf, in1, low2, in2, mine, z_in)
    flows = [
        GradSum(t, source, out, joined, wide_first, (r, d), buffers, sem_flow, go)
        for t, source, out, joined, wide_first in (
            (0, outw_grad, outw_out, False, True),
            (1, proj_grad, proj_out, False, True),
        )
    ]
    out, tail = flows
    spare = (None,) * 6 + (ff_ref, ff_z)
    ff = [
        GradSum(t, None, ff_out.at[t], True, True, (r, d), spare, sem_ff, go)
        for t in range(3)
    ]
    for flow in ff:
        flow.cross_rows()
        flow.done = 4

    def scatter(k, q):
        return go(
            op_ref.at[q], op_in.at[k - 1], sem_op.at[0, k - 1], sem_op.at[1, k - 1], row=q
        )

    op_copies = [scatter(*row_peers[0]), scatter(*row_peers[2])]

    small[...] = jnp.zeros_like(small)
    square = jnp.zeros((SHARE, 1), F32)
    inner = jnp.zeros((SHARE, 1), F32)
    for j in range(4):
        value = mid_ref[j]
        square += jnp.sum(value * value, axis=1, keepdims=True)
        inner += jnp.sum(second_ref[j] * gains_full[j, 1:2, :] * value, axis=1, keepdims=True)
    rate = lax.rsqrt(square / D + EPS)
    scale = rate * rate * rate * inner / D
    for j in range(4):
        value = mid_ref[j]
        grad = second_ref[j]
        small[j, 1:2, 0:FEAT] = jnp.sum(grad * value * rate, axis=0, keepdims=True)
        total = (
            cot_ref[j].astype(F32)
            + rate * (grad * gains_full[j, 1:2, :])
            - value * scale
        )
        g_mid[j] = total
        g_branch[j] = total.astype(BF)
    grad_att = dot_nt(g_branch[0], outw_full[0])
    for j in range(1, 4):
        grad_att += dot_nt(g_branch[j], outw_full[j])
    g_att[:, 448:512] = jnp.zeros((SHARE, 64), BF)
    g_att[:, 0:448] = grad_att.astype(BF)
    for flow in ff:
        flow.step()
    outw_grad[...] = jnp.zeros_like(outw_grad)
    for j in range(4):
        outw_grad[j, 0:FEAT, 0:448] = dot_tn(g_branch[j], att_ref[...]).astype(BF)
    out.step()
    query_at = lax.broadcasted_iota(jnp.int32, (SHARE, 1), 0) + MAXLEN
    key_at = lax.broadcasted_iota(jnp.int32, (SHARE, MAXLEN + SHARE), 1)
    mask[...] = jnp.where(
        (key_at >= start_ref[...]) & (key_at <= query_at), 0.0, -1e30
    )

    lane = lax.broadcasted_iota(jnp.int32, (SHARE, 128), 1)
    low = lane < 64
    for m in range(HEADS // GROUPS):
        at = 128 * (m // 2)
        mine_lanes = low if m % 2 == 0 else jnp.logical_not(low)
        pick = lambda ref: jnp.where(
            mine_lanes, ref[:, at : at + 128].astype(F32), 0.0
        ).astype(BF)
        query, grad = pick(q_ref), pick(g_att)
        probs = jnp.exp(dot_nt(query, kv_ref[0]) + mask[...] - lse_ref[m])
        grad_probs = dot_nt(grad, kv_ref[1])
        inner = jnp.sum(probs * grad_probs, axis=1, keepdims=True)
        grad_scores = (probs * (grad_probs - inner)).astype(BF)
        grad_v = dot_tn(probs.astype(BF), grad)
        grad_k = dot_tn(grad_scores, query)
        if m == 0:
            dv[...] = grad_v
            dk[...] = grad_k
        else:
            dv[...] += grad_v
            dk[...] += grad_k
        grad_q = dot(grad_scores, kv_ref[0]) * HEAD_DIM ** (-0.5)
        if m % 2 == 0:
            dq[:, at : at + 128] = grad_q
        else:
            dq[:, at : at + 128] = jnp.where(low, dq[:, at : at + 128], grad_q)
        if m == 1:
            out.step()
            ff[0].step()
    wide_low = lax.broadcasted_iota(jnp.int32, (MAXLEN + SHARE, 128), 1) < 64
    dkv[...] = jnp.where(
        wide_low,
        dk[...] + pltpu.roll(dk[...], 64, 1),
        dv[...] + pltpu.roll(dv[...], 64, 1),
    ).astype(BF)
    kv_copies = [
        go(
            dkv.at[(4 - i) * SHARE : (5 - i) * SHARE, :],
            dkv_in.at[i - 1],
            sem_kv.at[0, i - 1],
            sem_kv.at[1, i - 1],
            **near(-i),
        )
        for i in (1, 2, 3, 4)
    ]
    out.step()
    total = dkv[MAXLEN : MAXLEN + SHARE, :].astype(F32)
    for i in (1, 2, 3, 4):
        kv_copies[i - 1].wait_recv()
        total += dkv_in[i - 1].astype(F32)
    op_copies.append(scatter(*row_peers[1]))
    turned = pltpu.roll(total, 64, 1)
    dq[:, 384:512] = jnp.where(low, dq[:, 384:512], turned)
    gv[...] = turned[:, 0:64].astype(BF)
    cosine = jnp.concatenate([cos_ref[...]] * 4, axis=1)
    sine = jnp.concatenate([sin_ref[...]] * 4, axis=1)
    gp[...] = (dq[...] * cosine - swapped(dq[...]) * sine).astype(BF)
    for j in range(4):
        c_send[j] = (
            dot_nt(gp[...], proj_full[j, :, 0:512])
            + dot_nt(gv[...], proj_full[j, :, 512:576])
        ).astype(BF)
    cross = go(c_send, c_in, sem_c.at[0], sem_c.at[1], col=1 - c)
    proj_grad[...] = jnp.zeros_like(proj_grad)
    for j in range(4):
        proj_grad[j, 0:FEAT, 0:512] = dot_tn(nf_ref[j], gp[...]).astype(BF)
        proj_grad[j, 0:FEAT, 512:576] = dot_tn(nf_ref[j], gv[...]).astype(BF)
    tail.step()
    bias_a = jnp.sum(gp[...].astype(F32), axis=0, keepdims=True)
    bias_b = jnp.sum(gv[...].astype(F32), axis=0, keepdims=True)
    for j in range(4):
        small[j, 2:3, 0:512] = bias_a
        small[j, 2:3, 512:576] = bias_b
    out.step()
    tail.step()
    ff[1].step()
    ff[2].step()
    tail.step()
    out.step()
    tail.step()

    square = jnp.zeros((SHARE, 1), F32)
    for j in range(4):
        value = x_ref[j].astype(F32)
        square += jnp.sum(value * value, axis=1, keepdims=True)
    rate = lax.rsqrt(square / D + EPS)
    cross.wait_recv()
    inner = jnp.zeros((SHARE, 1), F32)
    for j in range(4):
        grad = c_send[j].astype(F32) + c_in[j].astype(F32)
        inner += jnp.sum(
            grad * gains_full[j, 0:1, :] * x_ref[j].astype(F32), axis=1, keepdims=True
        )
    scale = rate * rate * rate * inner / D
    for j in range(4):
        value = x_ref[j].astype(F32)
        grad = c_send[j].astype(F32) + c_in[j].astype(F32)
        small[j, 0:1, 0:FEAT] = jnp.sum(grad * value * rate, axis=0, keepdims=True)
        own_input[j] = (
            g_mid[j] + rate * (grad * gains_full[j, 0:1, :]) - value * scale
        ).astype(BF)
    in_copies = [
        go(
            own_input.at[q],
            input_out.at[r],
            sem_in.at[0, k - 1],
            sem_in.at[1, k - 1],
            row=q,
        )
        for k, q in row_peers
    ]
    input_out[r] = own_input[r]

    total = op_ref[r].astype(F32)
    for copy in op_copies:
        copy.wait_recv()
    for k in range(3):
        total += op_in[k].astype(F32)
    co_send[...] = total.astype(BF)
    final = go(co_send, co_in, sem_co.at[0], sem_co.at[1], col=1 - c)

    def swap(stage, source, target, k, **device):
        return go(source, target, sem_s.at[0, stage, k - 1], sem_s.at[1, stage, k - 1], **device)

    copy = swap(0, small, small_in.at[0], 1, dp=sibling)
    out.step()
    tail.step()
    ff[0].step()
    copy.wait_recv()
    small_x[0] = small[...] + small_in[0]
    copies = [swap(1, small_x.at[0], small_in.at[k], k, dp=p) for k, p in x_peers]
    out.step()
    tail.step()
    for copy in copies:
        copy.wait_recv()
    small_x[1] = small_x[0] + small_in[1] + small_in[2] + small_in[3]
    copy = swap(2, small_x.at[1], small_in.at[4], 1, dp=other_y)
    tail.step()
    copy.wait_recv()
    small_x[2] = small_x[1] + small_in[4]
    copies = [swap(3, small_x.at[2, q], small_z.at[r], k, row=q) for k, q in row_peers]
    small_z[r] = small_x[2, r]
    ff[1].step()
    ff[2].step()
    for copy in copies:
        copy.wait_recv()
    small_out[...] = small_z[0] + small_z[1] + small_z[2] + small_z[3]
    tail.step()
    out.step()
    for flow in ff:
        flow.step()
    for copy in in_copies:
        copy.wait_recv()
    final.wait_recv()
    block_out[...] = (co_send[...].astype(F32) + co_in[...].astype(F32)).astype(BF)
    for copy in pending:
        copy.wait_send()


def back(*operands):
    dma = pltpu.SemaphoreType.DMA
    shape = jax.ShapeDtypeStruct
    width = MAXLEN + SHARE
    blocked = pltpu.VMEM((4, SHARE, FEAT), BF)
    count = 2
    return vmem_call(
        back_kernel,
        17,
        (
            shape((SHARD, FEAT), BF),
            shape((4, SHARE, FEAT), BF),
            shape((3, PADF, HALF_FF), BF),
            shape((PADF, WIN), BF),
            shape((PADF, WIN), BF),
            shape((8, WIN), F32),
        ),
        [
            pltpu.VMEM((SHARE, width), F32),
            pltpu.VMEM((4, SHARE, FEAT), F32),
            blocked,
            pltpu.VMEM((SHARE, 512), BF),
            pltpu.VMEM((SHARE, 512), F32),
            pltpu.VMEM((width, 128), F32),
            pltpu.VMEM((width, 128), F32),
            pltpu.VMEM((width, 128), BF),
            pltpu.VMEM((4, SHARE, 128), BF),
            pltpu.VMEM((SHARE, 512), BF),
            pltpu.VMEM((SHARE, 64), BF),
            blocked,
            blocked,
            pltpu.VMEM((3, SHARD, FEAT), BF),
            pltpu.VMEM((SHARD, FEAT), BF),
            pltpu.VMEM((SHARD, FEAT), BF),
            blocked,
            pltpu.VMEM((4, PADF, WIN), BF),
            pltpu.VMEM((4, PADF, WIN), BF),
            pltpu.VMEM((4, 8, WIN), F32),
            pltpu.VMEM((5, 4, 8, WIN), F32),
            pltpu.VMEM((3, 4, 8, WIN), F32),
            pltpu.VMEM((4, 8, WIN), F32),
            pltpu.VMEM((count, 4, 128, WIN), BF),
            pltpu.VMEM((count, 4, 128, WIN), F32),
            pltpu.VMEM((count, 4, 128, WIN), BF),
            pltpu.VMEM((count, 4, 96, WIN), BF),
            pltpu.VMEM((count, 4, 64, WIN), BF),
            pltpu.VMEM((count, 4, 48, WIN), BF),
            pltpu.VMEM((count, 4, 16, WIN), BF),
            pltpu.VMEM((count, 4, 16, WIN), BF),
            pltpu.VMEM((3, 4, 16, WIN), BF),
            dma((2, count, 7, 3)),
            dma((2, 3, 7, 3)),
            dma((2, 4)),
            dma((2,)),
            dma((2, 3)),
            dma((2, 4, 3)),
            dma((2, 3)),
            dma((2,)),
        ],
        1,
    )(*operands)


def body(
    activations,
    starts,
    first_gain,
    project_weight,
    project_bias,
    output_weight,
    second_gain,
    gate_weight,
    up_weight,
    down_weight,
    cotangent,
):
    r = lax.axis_index("row")
    shard = lax.axis_index("dp")
    query_width = HEADS // GROUPS * HEAD_DIM

    base = shard * SHARD + r * SHARE
    start_window = (
        lax.dynamic_slice_in_dim(starts, r * SHARE, SHARE, 0) - base + MAXLEN
    )[:, None]
    positions = (MAXLEN + jnp.arange(SHARE, dtype=jnp.int32))[:, None] - start_window
    half = HEAD_DIM // 2
    freqs = 1000000.0 ** (-jnp.arange(half, dtype=F32) * 2.0 / HEAD_DIM)
    angle = positions.astype(F32) * jnp.tile(freqs, 4)[None, :]
    cosine = jnp.cos(angle)
    sine = jnp.sin(angle) * jnp.tile(jnp.repeat(jnp.array([-1.0, 1.0], F32), half), 2)[None, :]
    gains = jnp.pad(jnp.stack([first_gain, second_gain]), ((0, 6), (0, 0)))
    (
        x_low,
        normed_first,
        queries,
        kv,
        lse,
        attended,
        middle,
        project_full,
        output_full,
        gains_full,
        cot_own,
        grad_second,
        out_partial,
        ff_part,
    ) = forward(
        activations,
        cotangent,
        project_weight,
        output_weight,
        gate_weight,
        up_weight,
        down_weight,
        gains,
        project_bias[None, :],
        cosine,
        sine,
        start_window,
    )
    block_output, input_grad, ff_sum, outw_sum, project_sum, small = back(
        grad_second,
        middle,
        cot_own,
        x_low,
        normed_first,
        queries,
        kv,
        lse,
        attended,
        project_full,
        output_full,
        gains_full,
        cosine,
        sine,
        start_window,
        ff_part,
        out_partial,
    )
    width = project_weight.shape[1]
    ff_sum = ff_sum[:, :FEAT].astype(F32)
    return (
        block_output,
        input_grad.reshape(SHARD, FEAT).astype(F32),
        small[0, :FEAT],
        project_sum[:FEAT, :width].astype(F32),
        small[2, :width],
        outw_sum[:FEAT, :query_width].astype(F32).T,
        small[1, :FEAT],
        ff_sum[0],
        ff_sum[1],
        ff_sum[2].T,
    )


def solution(mesh):
    return jax.shard_map(
        body,
        mesh=mesh,
        in_specs=(
            P("dp", "row"),
            P("dp"),
            P("row"),
            P("row", "col"),
            P("col"),
            P("col", "row"),
            P("row"),
            P("row", "col"),
            P("row", "col"),
            P("col", "row"),
            P("dp", "row"),
        ),
        out_specs=(
            P("dp", "row"),
            P("dp", "row"),
            P("row"),
            P("row", "col"),
            P("col"),
            P("col", "row"),
            P("row"),
            P("row", "col"),
            P("row", "col"),
            P("col", "row"),
        ),
        check_vma=False,
    )
```

```python
import functools

import jax
import jax.numpy as jnp
from jax import lax
from jax.experimental import pallas as pl
from jax.experimental.pallas import tpu as pltpu
from jax.sharding import PartitionSpec as P

D = 896
HEADS = 14
GROUPS = 2
HEAD_DIM = 64
MAXLEN = 1024
EPS = 1e-06
BF = jnp.bfloat16
F32 = jnp.float32
ROWS = 4
FEAT = 224
SHARE = 256
SHARD = 1024
HALF_FF = 2432
WIN = 640
LAST = HALF_FF - WIN
PADF = 256
VMEM_LIMIT = 60 * 1024 * 1024


def dot(a, b):
    return jnp.dot(a, b, preferred_element_type=F32)


def dot_nt(a, b):
    return lax.dot_general(a, b, (((1,), (1,)), ((), ())), preferred_element_type=F32)


def dot_tn(a, b):
    return lax.dot_general(a, b, (((0,), (0,)), ((), ())), preferred_element_type=F32)


def rcopy(src, dst, send, recv, **device):
    return pltpu.make_async_remote_copy(
        src_ref=src,
        dst_ref=dst,
        send_sem=send,
        recv_sem=recv,
        device_id=device,
        device_id_type=pl.DeviceIdType.MESH,
    )


def greet(peers):
    barrier = pltpu.get_barrier_semaphore()
    for peer in peers:
        pl.semaphore_signal(
            barrier, inc=1, device_id=peer, device_id_type=pl.DeviceIdType.MESH
        )
    pl.semaphore_wait(barrier, len(peers))


def vmem_call(kernel, inputs, outs, scratch, collective, cost=None):
    return pl.pallas_call(
        kernel,
        out_shape=outs,
        in_specs=[pl.BlockSpec(memory_space=pltpu.VMEM)] * inputs,
        out_specs=jax.tree.map(lambda _: pl.BlockSpec(memory_space=pltpu.VMEM), outs),
        scratch_shapes=scratch,
        compiler_params=pltpu.CompilerParams(
            collective_id=collective,
            has_side_effects=True,
            vmem_limit_bytes=VMEM_LIMIT,
        ),
        cost_estimate=cost,
    )


class GradSum:
    def __init__(self, t, source, out, joined, wide_first, place, buffers, sems, go):
        self.t, self.source, self.out, self.joined, self.go = t, source, out, joined, go
        self.r, d = place
        self.core = lax.rem(d, 2)
        y = lax.rem(d // 2, 2)
        x = d // 4
        self.sibling = d + 1 - 2 * self.core
        along_x = [
            (k, lax.rem(x + k, 4), lax.rem(x + k, 4) * 4 + lax.rem(d, 4)) for k in (1, 2, 3)
        ]
        along_y = [(1, 1 - y, d + 2 - 4 * y)]
        if wide_first:
            self.first, self.second = (along_x, x, 32), (along_y, y, 16)
        else:
            self.first, self.second = (along_y, y, 64), (along_x, x, 16)
        self.at_first = self.core * 128 + self.first[1] * self.first[2]
        self.at = self.at_first + self.second[1] * 16
        self.core_in, self.part, self.low, self.in1, self.low2, self.in2, self.mine, self.z_in = [
            buffer.at[t] if buffer is not None else None for buffer in buffers
        ]
        self.sem = lambda stage, k: (sems.at[0, t, stage, k - 1], sems.at[1, t, stage, k - 1])
        self.waiting = []
        self.done = 0

    def rows(self, start, size):
        return pl.ds(pl.multiple_of(start, 16), size)

    def settle(self):
        for copy in self.waiting:
            copy.wait_recv()
        self.waiting = []

    def send(self, source, target, stage, k, **device):
        self.waiting.append(self.go(source, target, *self.sem(stage, k), **device))

    def step(self):
        self.settle()
        getattr(self, "step%d" % self.done)()
        self.done += 1

    def step0(self):
        self.send(
            self.source.at[:, self.rows((1 - self.core) * 128, 128), :],
            self.core_in,
            0,
            1,
            dp=self.sibling,
        )

    def step1(self):
        peers, own, unit = self.first
        total = self.source[:, self.rows(self.core * 128, 128), :].astype(F32)
        total = total + self.core_in[...].astype(F32)
        self.part[...] = total
        self.low[...] = total.astype(BF)
        for k, index, device in peers:
            self.send(
                self.low.at[:, self.rows(index * unit, unit), :],
                self.in1.at[:, (k - 1) * unit : k * unit, :],
                1,
                k,
                dp=device,
            )

    def step2(self):
        peers, own, unit = self.first
        total = self.part[:, self.rows(own * unit, unit), :]
        for k, _, _ in peers:
            total = total + self.in1[:, (k - 1) * unit : k * unit, :].astype(F32)
        self.part[:, 0:unit, :] = total
        self.low2[:, 0:unit, :] = total.astype(BF)
        peers, own, unit = self.second
        for k, index, device in peers:
            self.send(
                self.low2.at[:, self.rows(index * unit, unit), :],
                self.in2.at[:, (k - 1) * unit : k * unit, :],
                2,
                k,
                dp=device,
            )

    def step3(self):
        self.reduce()
        self.cross_rows()

    def reduce(self):
        self.settle()
        peers, own, unit = self.second
        total = self.part[:, self.rows(own * unit, unit), :]
        for k, _, _ in peers:
            total = total + self.in2[:, (k - 1) * unit : k * unit, :].astype(F32)
        self.mine[...] = total.astype(BF)

    def cross_rows(self):
        for k in (1, 2, 3):
            q = lax.rem(self.r + k, 4)
            self.send(self.mine.at[q], self.z_in.at[self.r], 3, k, row=q)
        self.z_in[self.r] = self.mine[self.r]

    def step4(self):
        here = self.rows(self.at, 16)
        if self.joined:
            for q in range(3):
                self.out[here, q * WIN : (q + 1) * WIN] = self.z_in[q]
            self.out[here, 3 * WIN : HALF_FF] = self.z_in[3][:, 4 * WIN - HALF_FF :]
        else:
            total = self.z_in[0].astype(F32)
            for q in range(1, 4):
                total = total + self.z_in[q].astype(F32)
            self.out[here, :] = total.astype(BF)
        self.spread(self.second[0], self.at, 16, 4)

    def spread(self, peers, start, size, stage):
        block = self.out.at[self.rows(start, size), :]
        for k, _, device in peers:
            self.send(block, block, stage, k, dp=device)

    def step5(self):
        self.spread(self.first[0], self.at_first, self.first[2], 5)

    def step6(self):
        self.spread([(1, 0, self.sibling)], self.core * 128, 128, 6)

    def step7(self):
        pass


def swapped(values):
    width = values.shape[1]
    lane = lax.broadcasted_iota(jnp.int32, values.shape, 1)
    return jnp.where(
        lax.rem(lane, 64) < 32,
        pltpu.roll(values, width - 32, 1),
        pltpu.roll(values, 32, 1),
    )


def forward_kernel(
    act_ref,
    cot_ref,
    proj_ref,
    outw_ref,
    gate_ref,
    up_ref,
    down_ref,
    gains_ref,
    bias_ref,
    cos_ref,
    sin_ref,
    start_ref,
    x_out,
    nf_out,
    q_out,
    kv_out,
    lse_out,
    att_out,
    mid_out,
    proj_full,
    outw_full,
    gains_full,
    cot_out,
    second_out,
    op_out,
    down_out,
    mine_out,
    gate_full,
    up_full,
    down_full,
    cot_all,
    mask,
    own_kv,
    kv_pack,
    c_send,
    c_in,
    second_in,
    ns_all,
    hid,
    gg,
    gu,
    sp_send,
    sp_in,
    grads,
    core_in,
    part,
    low_buf,
    in1,
    low2,
    in2,
    sem_x,
    sem_g,
    sem_w,
    sem_wx,
    sem_wc,
    sem_cot,
    sem_kv,
    sem_c,
    sem_ag,
    sem_sp,
    sem_cs,
    sem_flow,
    sem_l,
):
    d = lax.axis_index("dp")
    r = lax.axis_index("row")
    c = lax.axis_index("col")
    core = lax.rem(d, 2)
    x_at = d // 4
    sibling = d + 1 - 2 * core
    other_y = d + 2 - 4 * lax.rem(d // 2, 2)
    x_peers = [(k, lax.rem(x_at + k, 4) * 4 + lax.rem(d, 4)) for k in (1, 2, 3)]
    block = 4 * d + r
    near = lambda i: {
        "dp": lax.rem((block + 64 + i) // 4, 16),
        "row": lax.rem(r + 4 + i, 4),
    }
    greet(
        [{"row": lax.rem(r + k, 4)} for k in (1, 2, 3)]
        + [{"dp": p} for _, p in x_peers]
        + [{"col": 1 - c}, {"dp": sibling}, {"dp": other_y}]
        + [near(i) for i in (1, 2, 3, 4, -1, -2, -3, -4)]
    )
    pending = []

    def go(*args, **device):
        copy = rcopy(*args, **device)
        copy.start()
        pending.append(copy)
        return copy

    peers = [(k, lax.rem(r + k, 4)) for k in (1, 2, 3)]
    span = lambda q: pl.ds(pl.multiple_of(q * SHARE, SHARE), SHARE)
    offset = lambda q: pl.multiple_of(jnp.minimum(q * WIN, LAST), 128)
    half = lambda n: pl.ds(pl.multiple_of(core * n, 16), n)

    def down_rows(q):
        return pl.ds(pl.multiple_of(offset(q) + core * (WIN // 2), 16), WIN // 2)

    pieces = (
        (lambda q: proj_ref.at[half(112), :], proj_full, 112),
        (lambda q: outw_ref.at[half(224), :], outw_full, 224),
        (lambda q: gate_ref.at[half(112), pl.ds(offset(q), WIN)], gate_full, 112),
        (lambda q: up_ref.at[half(112), pl.ds(offset(q), WIN)], up_full, 112),
        (lambda q: down_ref.at[down_rows(q), :], down_full, WIN // 2),
    )

    def crossing(w):
        source, full, n = pieces[w]
        return [
            rcopy(
                source(q),
                full.at[r, half(n), :],
                sem_w.at[0, w, k - 1],
                sem_w.at[1, w, k - 1],
                row=q,
            )
            for k, q in peers
        ]

    def passing(w):
        _, full, n = pieces[w]
        copies = []
        for k, q in peers:
            part = full.at[q, half(n), :]
            for e, device in x_peers:
                copies.append(
                    rcopy(
                        part,
                        part,
                        sem_wx.at[0, w - 2, k - 1, e - 1],
                        sem_wx.at[1, w - 2, k - 1, 0],
                        dp=device,
                    )
                )
        return copies

    def fetch(w):
        source, full, n = pieces[w]
        local = pltpu.make_async_copy(source(r), full.at[r, half(n), :], sem_l.at[w])
        local.start()
        copies = crossing(w)
        if w < 2:
            for copy in copies:
                copy.start()
                pending.append(copy)
        else:

            @pl.when(x_at == w - 2)
            def _():
                for copy in copies:
                    copy.start()

        return copies, local

    def pass_on(w, fetched):
        @pl.when(x_at == w - 2)
        def _():
            for copy in fetched[0]:
                copy.wait_recv()
            for copy in passing(w):
                copy.start()

    def share(w, fetched):
        _, full, n = pieces[w]
        copies, local = fetched
        local.wait()
        if w < 2:
            for copy in copies:
                copy.wait_recv()
        else:

            @pl.when(x_at != w - 2)
            def _():
                for copy in passing(w)[::3]:
                    copy.wait_recv()

        part = full.at[:, half(n), :]
        copy = rcopy(part, part, sem_wc.at[0, w], sem_wc.at[1, w], dp=sibling)
        copy.start()
        if w < 2:
            pending.append(copy)
        return copy

    def finish(w, fetched):
        @pl.when(x_at == w - 2)
        def _():
            for copy in fetched[0] + passing(w):
                copy.wait_send()

    x_copies = [
        go(
            act_ref.at[span(q), :],
            x_out.at[r],
            sem_x.at[0, k - 1],
            sem_x.at[1, k - 1],
            row=q,
        )
        for k, q in peers
    ]
    g_copies = [
        go(gains_ref, gains_full.at[r], sem_g.at[0, k - 1], sem_g.at[1, k - 1], row=q)
        for k, q in peers
    ]
    fetched = {0: fetch(0)}
    x_out[r] = act_ref[span(r), :]
    gains_full[r] = gains_ref[...]
    query_at = lax.broadcasted_iota(jnp.int32, (SHARE, 1), 0) + MAXLEN
    key_at = lax.broadcasted_iota(jnp.int32, (SHARE, MAXLEN + SHARE), 1)
    mask[...] = jnp.where(
        (key_at >= start_ref[...]) & (key_at <= query_at), 0.0, -1e30
    )
    shared = {0: share(0, fetched[0])}
    for copy in x_copies + g_copies:
        copy.wait_recv()
    for w in (1, 2, 3, 4):
        fetched[w] = fetch(w)
    cot_all[r] = cot_ref[...]
    square = jnp.zeros((SHARE, 1), F32)
    for j in range(4):
        value = x_out[j].astype(F32)
        square += jnp.sum(value * value, axis=1, keepdims=True)
    rate = lax.rsqrt(square / D + EPS)
    for j in range(4):
        nf_out[j] = (x_out[j].astype(F32) * rate * gains_full[j, 0:1, :]).astype(BF)
    shared[0].wait_recv()
    projected = dot(nf_out[0], proj_full[0, :, 0:512])
    values = dot(nf_out[0], proj_full[0, :, 512:576])
    for j in range(1, 4):
        projected += dot(nf_out[j], proj_full[j, :, 0:512])
        values += dot(nf_out[j], proj_full[j, :, 512:576])
    projected += bias_ref[:, 0:512]
    values = (values + bias_ref[:, 512:576]).astype(BF)
    cosine = jnp.concatenate([cos_ref[...]] * 4, axis=1)
    sine = jnp.concatenate([sin_ref[...]] * 4, axis=1)
    turned = projected * cosine + swapped(projected) * sine
    q_out[...] = (turned * HEAD_DIM ** (-0.5)).astype(BF)
    tile = turned[:, 384:512]
    lane = lax.broadcasted_iota(jnp.int32, (SHARE, 128), 1)
    low = lane < 64
    double = (
        lax.rem(lax.broadcasted_iota(jnp.int32, (64, 128), 1), 64)
        == lax.broadcasted_iota(jnp.int32, (64, 128), 0)
    ).astype(F32).astype(BF)
    own_kv[...] = jnp.where(low, pltpu.roll(tile, 64, 1), dot(values, double)).astype(BF)
    kv_copies = [
        go(
            own_kv,
            kv_pack.at[(4 - i) * SHARE : (5 - i) * SHARE, :],
            sem_kv.at[0, i - 1],
            sem_kv.at[1, i - 1],
            **near(i),
        )
        for i in (1, 2, 3, 4)
    ]
    kv_pack[MAXLEN : MAXLEN + SHARE, :] = own_kv[...]
    for w in (2, 3, 4):
        pass_on(w, fetched[w])
    for copy in kv_copies:
        copy.wait_recv()
    right, across, left = [q for _, q in peers]

    def cot_go(source, target, index, q):
        return go(source, target, sem_cot.at[0, index], sem_cot.at[1, index], row=q)

    cot_left = cot_go(cot_ref, cot_all.at[r], 0, right)
    cot_right = cot_go(cot_ref, cot_all.at[r], 1, left)
    packed = kv_pack[...].astype(F32)
    turned_pack = pltpu.roll(packed, 64, 1)
    first_half = lax.broadcasted_iota(jnp.int32, packed.shape, 1) < 64
    kv_out[0] = jnp.where(first_half, packed, turned_pack).astype(BF)
    kv_out[1] = jnp.where(first_half, turned_pack, packed).astype(BF)
    for m in range(HEADS // GROUPS):
        at = 128 * (m // 2)
        mine = low if m % 2 == 0 else jnp.logical_not(low)
        query = jnp.where(mine, q_out[:, at : at + 128].astype(F32), 0.0).astype(BF)
        scores = dot_nt(query, kv_out[0]) + mask[...]
        peak = jnp.max(scores, axis=1, keepdims=True)
        powered = jnp.exp(scores - peak)
        total = jnp.sum(powered, axis=1, keepdims=True)
        probs = (powered * (1.0 / total)).astype(BF)
        lse_out[m] = peak + jnp.log(total)
        mixed = dot(probs, kv_out[1])
        if m == 6:
            att_out[:, 384:448] = mixed[:, 0:64].astype(BF)
        elif m % 2 == 0:
            even = mixed
        else:
            att_out[:, at : at + 128] = jnp.where(low, even, mixed).astype(BF)
    shared[1] = share(1, fetched[1])
    shared[1].wait_recv()
    for j in range(4):
        c_send[j] = dot(att_out[...], outw_full[j]).astype(BF)
    cross = rcopy(c_send, c_in, sem_c.at[0], sem_c.at[1], col=1 - c)
    cross.start()
    cot_left.wait_recv()
    upper = cot_all.at[left, 0 : SHARD // 2, :]
    cot_copies = [cot_go(upper, upper, 2, right)]
    cot_right.wait_recv()
    lower = cot_all.at[right, SHARD // 2 : SHARD, :]
    cot_copies.append(cot_go(lower, lower, 3, left))
    for w in (2, 3, 4):
        shared[w] = share(w, fetched[w])
    cross.wait_recv()
    square = jnp.zeros((SHARE, 1), F32)
    for j in range(4):
        value = x_out[j].astype(F32) + (
            c_send[j].astype(F32) + c_in[j].astype(F32)
        )
        mid_out[j] = value
        square += jnp.sum(value * value, axis=1, keepdims=True)
    rate = lax.rsqrt(square / D + EPS)
    for j in range(4):
        ns_all[j, span(r), :] = (mid_out[j] * rate * gains_full[j, 1:2, :]).astype(BF)

    def spread(blocks, source, index, q):
        part = ns_all.at[blocks, span(source), :]
        return go(part, part, sem_ag.at[0, index], sem_ag.at[1, index], row=q)

    every, front_half, back_half = pl.ds(0, 4), pl.ds(0, 2), pl.ds(2, 2)
    from_left = spread(every, r, 0, right)
    from_right = spread(every, r, 1, left)
    for copy in cot_copies:
        copy.wait_recv()
    for w in (2, 3, 4):
        shared[w].wait_recv()
        shared[w].wait_send()
        finish(w, fetched[w])
    live = jnp.where(r < 3, 1.0, 0.0)
    extra = 4 * WIN - HALF_FF
    for j in range(4):
        gate_full[j, :, 0:extra] = (gate_full[j, :, 0:extra].astype(F32) * live).astype(BF)
        up_full[j, :, 0:extra] = (up_full[j, :, 0:extra].astype(F32) * live).astype(BF)
        cot_out[j] = cot_all[j, span(r), :]

    def feed(k, q, arrived):
        grad_hidden = dot_nt(cot_all[0, span(q), :], down_full[0])
        for j in range(1, 4):
            grad_hidden += dot_nt(cot_all[j, span(q), :], down_full[j])
        arrived()
        gate = dot(ns_all[0, span(q), :], gate_full[0])
        up = dot(ns_all[0, span(q), :], up_full[0])
        for j in range(1, 4):
            gate += dot(ns_all[j, span(q), :], gate_full[j])
            up += dot(ns_all[j, span(q), :], up_full[j])
        sigma = 1.0 / (1.0 + jnp.exp(-gate))
        silu = gate * sigma
        hid[span(q), :] = (silu * up).astype(BF)
        g_gate = (grad_hidden * up * (sigma + silu * (1.0 - sigma))).astype(BF)
        g_up = (grad_hidden * silu).astype(BF)
        gg[span(q), :] = g_gate
        gu[span(q), :] = g_up
        copies = []
        for j in range(4):
            sp_send[k, j] = (
                dot_nt(g_gate, gate_full[j]) + dot_nt(g_up, up_full[j])
            ).astype(BF)
            if k and j % 2:
                copies.append(
                    go(
                        sp_send.at[k, j - 1 : j + 1],
                        sp_in.at[k - 1, j - 1 : j + 1],
                        sem_sp.at[0, k - 1, j // 2],
                        sem_sp.at[1, k - 1, j // 2],
                        row=q,
                    )
                )
        return copies

    forwarded = []

    def neighbours_here():
        from_left.wait_recv()
        forwarded.append(spread(front_half, left, 2, right))
        from_right.wait_recv()
        forwarded.append(spread(back_half, right, 3, left))

    def opposite_here():
        for copy in forwarded:
            copy.wait_recv()

    feed(0, r, lambda: None)
    back = {}
    back[1] = feed(1, right, neighbours_here)
    back[3] = feed(3, left, lambda: None)
    back[2] = feed(2, across, opposite_here)

    buffers = (core_in, part, low_buf, in1, low2, in2, mine_out, None)
    flows = [
        GradSum(t, grads.at[t], None, True, True, (r, d), buffers, sem_flow, go)
        for t in range(2)
    ]
    grads[:, :, FEAT:PADF, :] = jnp.zeros((2, 4, PADF - FEAT, WIN), BF)
    down_out[:, FEAT:PADF, :] = jnp.zeros((4, PADF - FEAT, WIN), BF)
    for t, right_side in ((0, gg), (1, gu)):
        for j in range(4):
            grads[t, j, 0:FEAT, :] = dot_tn(ns_all[j], right_side[...]).astype(BF)
        flows[t].step()
        if t:
            flows[t - 1].step()
    flows[1].step()
    cross.wait_send()
    crosses = []
    for h in (0, 2):
        total = sp_send[0, h : h + 2].astype(F32)
        for k in (1, 3, 2):
            back[k][h // 2].wait_recv()
            total += sp_in[k - 1, h : h + 2].astype(F32)
        c_send[h : h + 2] = total.astype(BF)
        crosses.append(
            go(
                c_send.at[h : h + 2],
                second_in.at[h : h + 2],
                sem_cs.at[0, h // 2],
                sem_cs.at[1, h // 2],
                col=1 - c,
            )
        )
        if h == 0:
            for j in range(4):
                down_out[j, 0:FEAT, :] = dot_tn(cot_all[j], hid[...]).astype(BF)
    for j in range(4):
        for q in range(4):
            op_out[j, q * SHARE : (q + 1) * SHARE, :] = dot(
                hid[q * SHARE : (q + 1) * SHARE, :], down_full[j]
            ).astype(BF)
        op_out[j, span(r), :] = (
            op_out[j, span(r), :].astype(F32) + 0.5 * mid_out[j]
        ).astype(BF)
    for flow in flows:
        flow.step()
    for copy in crosses:
        copy.wait_recv()
    second_out[...] = c_send[...].astype(F32) + second_in[...].astype(F32)
    for flow in flows:
        flow.reduce()
    for copy in pending:
        copy.wait_send()


def forward(*operands):
    dma = pltpu.SemaphoreType.DMA
    shape = jax.ShapeDtypeStruct
    width = MAXLEN + SHARE
    blocked = pltpu.VMEM((4, SHARE, FEAT), BF)
    return vmem_call(
        forward_kernel,
        12,
        (
            shape((4, SHARE, FEAT), BF),
            shape((4, SHARE, FEAT), BF),
            shape((SHARE, 512), BF),
            shape((2, width, 128), BF),
            shape((HEADS // GROUPS, SHARE, 1), F32),
            shape((SHARE, 448), BF),
            shape((4, SHARE, FEAT), F32),
            shape((4, FEAT, 576), BF),
            shape((4, 448, FEAT), BF),
            shape((4, 8, FEAT), F32),
            shape((4, SHARE, FEAT), BF),
            shape((4, SHARE, FEAT), F32),
            shape((4, SHARD, FEAT), BF),
            shape((4, PADF, WIN), BF),
            shape((2, 4, 16, WIN), BF),
        ),
        [
            pltpu.VMEM((4, FEAT, WIN), BF),
            pltpu.VMEM((4, FEAT, WIN), BF),
            pltpu.VMEM((4, WIN, FEAT), BF),
            pltpu.VMEM((4, SHARD, FEAT), BF),
            pltpu.VMEM((SHARE, width), F32),
            pltpu.VMEM((SHARE, 128), BF),
            pltpu.VMEM((width, 128), BF),
            blocked,
            blocked,
            blocked,
            pltpu.VMEM((4, SHARD, FEAT), BF),
            pltpu.VMEM((SHARD, WIN), BF),
            pltpu.VMEM((SHARD, WIN), BF),
            pltpu.VMEM((SHARD, WIN), BF),
            pltpu.VMEM((4, 4, SHARE, FEAT), BF),
            pltpu.VMEM((3, 4, SHARE, FEAT), BF),
            pltpu.VMEM((2, 4, PADF, WIN), BF),
            pltpu.VMEM((3, 4, 128, WIN), BF),
            pltpu.VMEM((3, 4, 128, WIN), F32),
            pltpu.VMEM((3, 4, 128, WIN), BF),
            pltpu.VMEM((3, 4, 96, WIN), BF),
            pltpu.VMEM((3, 4, 64, WIN), BF),
            pltpu.VMEM((3, 4, 48, WIN), BF),
            dma((2, 3)),
            dma((2, 3)),
            dma((2, 5, 3)),
            dma((2, 3, 3, 3)),
            dma((2, 5)),
            dma((2, 4)),
            dma((2, 4)),
            dma((2,)),
            dma((2, 4)),
            dma((2, 3, 2)),
            dma((2, 2)),
            dma((2, 3, 3, 3)),
            dma((5,)),
        ],
        0,
    )(*operands)


def back_kernel(
    second_ref,
    mid_ref,
    cot_ref,
    x_ref,
    nf_ref,
    q_ref,
    kv_ref,
    lse_ref,
    att_ref,
    proj_full,
    outw_full,
    gains_full,
    cos_ref,
    sin_ref,
    start_ref,
    ff_ref,
    op_ref,
    down_ref,
    block_out,
    input_out,
    ff_out,
    outw_out,
    proj_out,
    small_out,
    mask,
    g_mid,
    g_branch,
    g_att,
    dq,
    dk,
    dv,
    dkv,
    dkv_in,
    gp,
    gv,
    c_send,
    c_in,
    op_in,
    co_send,
    co_in,
    own_input,
    outw_grad,
    proj_grad,
    small,
    small_in,
    small_x,
    small_z,
    core_in,
    part,
    low_buf,
    in1,
    low2,
    in2,
    mine,
    z_in,
    ff_z,
    sem_flow,
    sem_ff,
    sem_kv,
    sem_c,
    sem_in,
    sem_s,
    sem_op,
    sem_co,
):
    d = lax.axis_index("dp")
    r = lax.axis_index("row")
    c = lax.axis_index("col")
    core = lax.rem(d, 2)
    y = lax.rem(d // 2, 2)
    x = d // 4
    sibling = d + 1 - 2 * core
    other_y = d + 2 - 4 * y
    x_peers = [(k, lax.rem(x + k, 4) * 4 + lax.rem(d, 4)) for k in (1, 2, 3)]
    row_peers = [(k, lax.rem(r + k, 4)) for k in (1, 2, 3)]
    block = 4 * d + r
    near = lambda i: {
        "dp": lax.rem((block + 64 + i) // 4, 16),
        "row": lax.rem(r + 4 + i, 4),
    }
    greet(
        [{"row": q} for _, q in row_peers]
        + [{"dp": p} for _, p in x_peers]
        + [{"col": 1 - c}, {"dp": sibling}, {"dp": other_y}]
        + [near(i) for i in (1, 2, 3, 4, -1, -2, -3, -4)]
    )
    pending = []

    def go(*args, **device):
        copy = rcopy(*args, **device)
        copy.start()
        pending.append(copy)
        return copy

    span = lambda q: pl.ds(pl.multiple_of(q * SHARE, SHARE), SHARE)
    buffers = (core_in, part, low_buf, in1, low2, in2, mine, z_in)
    flows = [
        GradSum(t, source, out, joined, wide_first, (r, d), buffers, sem_flow, go)
        for t, source, out, joined, wide_first in (
            (0, outw_grad, outw_out, False, True),
            (1, proj_grad, proj_out, False, True),
            (2, down_ref, ff_out.at[2], True, True),
        )
    ]
    out, tail, down = flows
    down.step()
    spare = (None,) * 6 + (ff_ref, ff_z)
    ff = [
        GradSum(t, None, ff_out.at[t], True, True, (r, d), spare, sem_ff, go)
        for t in range(2)
    ]
    for flow in ff:
        flow.cross_rows()
        flow.done = 4
    ff.append(down)

    def scatter(k, q):
        return go(
            op_ref.at[q], op_in.at[k - 1], sem_op.at[0, k - 1], sem_op.at[1, k - 1], row=q
        )

    op_copies = [scatter(*row_peers[0]), scatter(*row_peers[2])]

    small[...] = jnp.zeros_like(small)
    square = jnp.zeros((SHARE, 1), F32)
    inner = jnp.zeros((SHARE, 1), F32)
    for j in range(4):
        value = mid_ref[j]
        square += jnp.sum(value * value, axis=1, keepdims=True)
        inner += jnp.sum(second_ref[j] * gains_full[j, 1:2, :] * value, axis=1, keepdims=True)
    rate = lax.rsqrt(square / D + EPS)
    scale = rate * rate * rate * inner / D
    for j in range(4):
        value = mid_ref[j]
        grad = second_ref[j]
        small[j, 1:2, 0:FEAT] = jnp.sum(grad * value * rate, axis=0, keepdims=True)
        total = (
            cot_ref[j].astype(F32)
            + rate * (grad * gains_full[j, 1:2, :])
            - value * scale
        )
        g_mid[j] = total
        g_branch[j] = total.astype(BF)
    grad_att = dot_nt(g_branch[0], outw_full[0])
    for j in range(1, 4):
        grad_att += dot_nt(g_branch[j], outw_full[j])
    g_att[:, 448:512] = jnp.zeros((SHARE, 64), BF)
    g_att[:, 0:448] = grad_att.astype(BF)
    for flow in ff:
        flow.step()
    outw_grad[...] = jnp.zeros_like(outw_grad)
    for j in range(4):
        outw_grad[j, 0:FEAT, 0:448] = dot_tn(g_branch[j], att_ref[...]).astype(BF)
    out.step()
    query_at = lax.broadcasted_iota(jnp.int32, (SHARE, 1), 0) + MAXLEN
    key_at = lax.broadcasted_iota(jnp.int32, (SHARE, MAXLEN + SHARE), 1)
    mask[...] = jnp.where(
        (key_at >= start_ref[...]) & (key_at <= query_at), 0.0, -1e30
    )

    lane = lax.broadcasted_iota(jnp.int32, (SHARE, 128), 1)
    low = lane < 64
    for m in range(HEADS // GROUPS):
        at = 128 * (m // 2)
        mine_lanes = low if m % 2 == 0 else jnp.logical_not(low)
        pick = lambda ref: jnp.where(
            mine_lanes, ref[:, at : at + 128].astype(F32), 0.0
        ).astype(BF)
        query, grad = pick(q_ref), pick(g_att)
        probs = jnp.exp(dot_nt(query, kv_ref[0]) + mask[...] - lse_ref[m])
        grad_probs = dot_nt(grad, kv_ref[1])
        inner = jnp.sum(probs * grad_probs, axis=1, keepdims=True)
        grad_scores = (probs * (grad_probs - inner)).astype(BF)
        grad_v = dot_tn(probs.astype(BF), grad)
        grad_k = dot_tn(grad_scores, query)
        if m == 0:
            dv[...] = grad_v
            dk[...] = grad_k
        else:
            dv[...] += grad_v
            dk[...] += grad_k
        grad_q = dot(grad_scores, kv_ref[0]) * HEAD_DIM ** (-0.5)
        if m % 2 == 0:
            dq[:, at : at + 128] = grad_q
        else:
            dq[:, at : at + 128] = jnp.where(low, dq[:, at : at + 128], grad_q)
        if m == 1:
            out.step()
            down.step()
            ff[0].step()
    wide_low = lax.broadcasted_iota(jnp.int32, (MAXLEN + SHARE, 128), 1) < 64
    dkv[...] = jnp.where(
        wide_low,
        dk[...] + pltpu.roll(dk[...], 64, 1),
        dv[...] + pltpu.roll(dv[...], 64, 1),
    ).astype(BF)
    kv_copies = [
        go(
            dkv.at[(4 - i) * SHARE : (5 - i) * SHARE, :],
            dkv_in.at[i - 1],
            sem_kv.at[0, i - 1],
            sem_kv.at[1, i - 1],
            **near(-i),
        )
        for i in (1, 2, 3, 4)
    ]
    out.step()
    down.step()
    total = dkv[MAXLEN : MAXLEN + SHARE, :].astype(F32)
    for i in (1, 2, 3, 4):
        kv_copies[i - 1].wait_recv()
        total += dkv_in[i - 1].astype(F32)
    op_copies.append(scatter(*row_peers[1]))
    down.step()
    turned = pltpu.roll(total, 64, 1)
    dq[:, 384:512] = jnp.where(low, dq[:, 384:512], turned)
    gv[...] = turned[:, 0:64].astype(BF)
    cosine = jnp.concatenate([cos_ref[...]] * 4, axis=1)
    sine = jnp.concatenate([sin_ref[...]] * 4, axis=1)
    gp[...] = (dq[...] * cosine - swapped(dq[...]) * sine).astype(BF)
    for j in range(4):
        c_send[j] = (
            dot_nt(gp[...], proj_full[j, :, 0:512])
            + dot_nt(gv[...], proj_full[j, :, 512:576])
        ).astype(BF)
    cross = go(c_send, c_in, sem_c.at[0], sem_c.at[1], col=1 - c)
    proj_grad[...] = jnp.zeros_like(proj_grad)
    for j in range(4):
        proj_grad[j, 0:FEAT, 0:512] = dot_tn(nf_ref[j], gp[...]).astype(BF)
        proj_grad[j, 0:FEAT, 512:576] = dot_tn(nf_ref[j], gv[...]).astype(BF)
    tail.step()
    bias_a = jnp.sum(gp[...].astype(F32), axis=0, keepdims=True)
    bias_b = jnp.sum(gv[...].astype(F32), axis=0, keepdims=True)
    for j in range(4):
        small[j, 2:3, 0:512] = bias_a
        small[j, 2:3, 512:576] = bias_b
    out.step()
    tail.step()
    ff[1].step()
    ff[2].step()
    tail.step()
    out.step()
    tail.step()

    square = jnp.zeros((SHARE, 1), F32)
    for j in range(4):
        value = x_ref[j].astype(F32)
        square += jnp.sum(value * value, axis=1, keepdims=True)
    rate = lax.rsqrt(square / D + EPS)
    cross.wait_recv()
    inner = jnp.zeros((SHARE, 1), F32)
    for j in range(4):
        grad = c_send[j].astype(F32) + c_in[j].astype(F32)
        inner += jnp.sum(
            grad * gains_full[j, 0:1, :] * x_ref[j].astype(F32), axis=1, keepdims=True
        )
    scale = rate * rate * rate * inner / D
    for j in range(4):
        value = x_ref[j].astype(F32)
        grad = c_send[j].astype(F32) + c_in[j].astype(F32)
        small[j, 0:1, 0:FEAT] = jnp.sum(grad * value * rate, axis=0, keepdims=True)
        own_input[j] = (
            g_mid[j] + rate * (grad * gains_full[j, 0:1, :]) - value * scale
        ).astype(BF)
    in_copies = [
        go(
            own_input.at[q],
            input_out.at[r],
            sem_in.at[0, k - 1],
            sem_in.at[1, k - 1],
            row=q,
        )
        for k, q in row_peers
    ]
    input_out[r] = own_input[r]

    total = op_ref[r].astype(F32)
    for copy in op_copies:
        copy.wait_recv()
    for k in range(3):
        total += op_in[k].astype(F32)
    co_send[...] = total.astype(BF)
    final = go(co_send, co_in, sem_co.at[0], sem_co.at[1], col=1 - c)

    def swap(stage, source, target, k, **device):
        return go(source, target, sem_s.at[0, stage, k - 1], sem_s.at[1, stage, k - 1], **device)

    copy = swap(0, small, small_in.at[0], 1, dp=sibling)
    out.step()
    tail.step()
    ff[0].step()
    copy.wait_recv()
    small_x[0] = small[...] + small_in[0]
    copies = [swap(1, small_x.at[0], small_in.at[k], k, dp=p) for k, p in x_peers]
    out.step()
    tail.step()
    for copy in copies:
        copy.wait_recv()
    small_x[1] = small_x[0] + small_in[1] + small_in[2] + small_in[3]
    copy = swap(2, small_x.at[1], small_in.at[4], 1, dp=other_y)
    tail.step()
    copy.wait_recv()
    small_x[2] = small_x[1] + small_in[4]
    copies = [swap(3, small_x.at[2, q], small_z.at[r], k, row=q) for k, q in row_peers]
    small_z[r] = small_x[2, r]
    ff[1].step()
    ff[2].step()
    for copy in copies:
        copy.wait_recv()
    small_out[...] = small_z[0] + small_z[1] + small_z[2] + small_z[3]
    tail.step()
    out.step()
    for flow in ff:
        flow.step()
    for copy in in_copies:
        copy.wait_recv()
    final.wait_recv()
    block_out[...] = (co_send[...].astype(F32) + co_in[...].astype(F32)).astype(BF)
    for copy in pending:
        copy.wait_send()


def back(*operands):
    dma = pltpu.SemaphoreType.DMA
    shape = jax.ShapeDtypeStruct
    width = MAXLEN + SHARE
    blocked = pltpu.VMEM((4, SHARE, FEAT), BF)
    count = 3
    return vmem_call(
        back_kernel,
        18,
        (
            shape((SHARD, FEAT), BF),
            shape((4, SHARE, FEAT), BF),
            shape((3, PADF, HALF_FF), BF),
            shape((PADF, WIN), BF),
            shape((PADF, WIN), BF),
            shape((8, WIN), F32),
        ),
        [
            pltpu.VMEM((SHARE, width), F32),
            pltpu.VMEM((4, SHARE, FEAT), F32),
            blocked,
            pltpu.VMEM((SHARE, 512), BF),
            pltpu.VMEM((SHARE, 512), F32),
            pltpu.VMEM((width, 128), F32),
            pltpu.VMEM((width, 128), F32),
            pltpu.VMEM((width, 128), BF),
            pltpu.VMEM((4, SHARE, 128), BF),
            pltpu.VMEM((SHARE, 512), BF),
            pltpu.VMEM((SHARE, 64), BF),
            blocked,
            blocked,
            pltpu.VMEM((3, SHARD, FEAT), BF),
            pltpu.VMEM((SHARD, FEAT), BF),
            pltpu.VMEM((SHARD, FEAT), BF),
            blocked,
            pltpu.VMEM((4, PADF, WIN), BF),
            pltpu.VMEM((4, PADF, WIN), BF),
            pltpu.VMEM((4, 8, WIN), F32),
            pltpu.VMEM((5, 4, 8, WIN), F32),
            pltpu.VMEM((3, 4, 8, WIN), F32),
            pltpu.VMEM((4, 8, WIN), F32),
            pltpu.VMEM((count, 4, 128, WIN), BF),
            pltpu.VMEM((count, 4, 128, WIN), F32),
            pltpu.VMEM((count, 4, 128, WIN), BF),
            pltpu.VMEM((count, 4, 96, WIN), BF),
            pltpu.VMEM((count, 4, 64, WIN), BF),
            pltpu.VMEM((count, 4, 48, WIN), BF),
            pltpu.VMEM((count, 4, 16, WIN), BF),
            pltpu.VMEM((count, 4, 16, WIN), BF),
            pltpu.VMEM((3, 4, 16, WIN), BF),
            dma((2, count, 7, 3)),
            dma((2, 3, 7, 3)),
            dma((2, 4)),
            dma((2,)),
            dma((2, 3)),
            dma((2, 4, 3)),
            dma((2, 3)),
            dma((2,)),
        ],
        1,
    )(*operands)


def body(
    activations,
    starts,
    first_gain,
    project_weight,
    project_bias,
    output_weight,
    second_gain,
    gate_weight,
    up_weight,
    down_weight,
    cotangent,
):
    r = lax.axis_index("row")
    shard = lax.axis_index("dp")
    query_width = HEADS // GROUPS * HEAD_DIM

    base = shard * SHARD + r * SHARE
    start_window = (
        lax.dynamic_slice_in_dim(starts, r * SHARE, SHARE, 0) - base + MAXLEN
    )[:, None]
    positions = (MAXLEN + jnp.arange(SHARE, dtype=jnp.int32))[:, None] - start_window
    half = HEAD_DIM // 2
    freqs = 1000000.0 ** (-jnp.arange(half, dtype=F32) * 2.0 / HEAD_DIM)
    angle = positions.astype(F32) * jnp.tile(freqs, 4)[None, :]
    cosine = jnp.cos(angle)
    sine = jnp.sin(angle) * jnp.tile(jnp.repeat(jnp.array([-1.0, 1.0], F32), half), 2)[None, :]
    gains = jnp.pad(jnp.stack([first_gain, second_gain]), ((0, 6), (0, 0)))
    (
        x_low,
        normed_first,
        queries,
        kv,
        lse,
        attended,
        middle,
        project_full,
        output_full,
        gains_full,
        cot_own,
        grad_second,
        out_partial,
        down_part,
        ff_part,
    ) = forward(
        activations,
        cotangent,
        project_weight,
        output_weight,
        gate_weight,
        up_weight,
        down_weight,
        gains,
        project_bias[None, :],
        cosine,
        sine,
        start_window,
    )
    block_output, input_grad, ff_sum, outw_sum, project_sum, small = back(
        grad_second,
        middle,
        cot_own,
        x_low,
        normed_first,
        queries,
        kv,
        lse,
        attended,
        project_full,
        output_full,
        gains_full,
        cosine,
        sine,
        start_window,
        ff_part,
        out_partial,
        down_part,
    )
    width = project_weight.shape[1]
    ff_sum = ff_sum[:, :FEAT].astype(F32)
    return (
        block_output,
        input_grad.reshape(SHARD, FEAT).astype(F32),
        small[0, :FEAT],
        project_sum[:FEAT, :width].astype(F32),
        small[2, :width],
        outw_sum[:FEAT, :query_width].astype(F32).T,
        small[1, :FEAT],
        ff_sum[0],
        ff_sum[1],
        ff_sum[2].T,
    )


def solution(mesh):
    return jax.shard_map(
        body,
        mesh=mesh,
        in_specs=(
            P("dp", "row"),
            P("dp"),
            P("row"),
            P("row", "col"),
            P("col"),
            P("col", "row"),
            P("row"),
            P("row", "col"),
            P("row", "col"),
            P("col", "row"),
            P("dp", "row"),
        ),
        out_specs=(
            P("dp", "row"),
            P("dp", "row"),
            P("row"),
            P("row", "col"),
            P("col"),
            P("col", "row"),
            P("row"),
            P("row", "col"),
            P("row", "col"),
            P("col", "row"),
        ),
        check_vma=False,
    )
```
